32 devices in a mesh: vel: 4 (over y, core), pos: 8 (over z, x).
Axes of the slice: x: 2, y: 2, z: 4, core: 2. Of those that a mesh axis runs over, the one named last changes fastest.
Arguments:
- value_next: float32 [16, 64, 64, 512], P('pos', 'vel'), may hold values from -6 to 6
- density: float32 [16, 64, 64, 512], P('pos', 'vel'), as said below
Outputs:
- value_now: float32 [16, 64, 64, 512], P('pos', 'vel')
- density_next: float32 [16, 64, 64, 512], P('pos', 'vel')
The draws below stay inside these ranges and needn't reach their ends.
Inputs may be any that keep to these rules, and one draw needn't show every extreme that they name: density is positive everywhere.
All inputs are finite; a program needn't handle non-finite values.
Results may differ from the reference program's by a relative error of at most 0.00002.
Values sent between devices are 32-bit elements; how exact they have to be, the bound alone decides.
No kernel may reach another device: no remote copies, remote signals or barrier semaphores. Data moves between devices by JAX's collectives and lax.ppermute only.
A program may use at most 192 MiB of HBM per device.

```python
import math
import jax
import jax.numpy as jnp
from jax import lax

NV = 64
NY = 512
NX = 16


def draw_density(key, part):
    first, second, third = jax.random.split(key, 3)
    rising = 10.0 ** (jnp.arange(NV, dtype=jnp.float32) / (NV - 1))
    column_scale = jnp.exp(jax.random.uniform(first, (NV,), jnp.float32, 0.0, math.log(10.0)))
    noise = jax.random.uniform(second, (NX, NV, NV, NY), jnp.float32, 0.5, 1.5)
    place = jnp.exp(jax.random.uniform(third, (NX, NY), jnp.float32, math.log(0.3), math.log(3.0)))
    result = place[:, None, None, :] * rising[None, :, None, None] * column_scale[None, None, :, None] * noise / 15.0
    return result.astype(jnp.float32)


def block_scale(key, extent, cuts, smallest, high):
    level = 1.0
    for axis_at, blocks in cuts:
        heights = jax.random.uniform(jax.random.fold_in(jax.random.fold_in(key, 6), axis_at), (blocks,), jnp.float32, smallest / len(cuts), high / len(cuts))
        level = level * jnp.repeat(jnp.exp(heights), extent[axis_at] // blocks).reshape((-1,) + (1,) * (len(extent) - 1 - axis_at))
    return level


def bell_draw(rng, dims, width, limit, cuts=(), kind=jnp.bfloat16):
    values = width * jax.random.normal(rng, dims, jnp.float32)
    if cuts:
        values = values * block_scale(rng, dims, cuts, -0.22, 0.18)
    return jnp.clip(values, -limit, limit).astype(kind)


def setup_inputs(seed: int = 0) -> dict:
    streams_of = jax.random.split(jax.random.key(seed), 3)
    value_next = bell_draw(streams_of[0], (NX, NV, NV, NY), 1.0, 6.0, ((0, 8), (1, 4)), jnp.float32)
    density = draw_density(jax.random.fold_in(streams_of[2], 71), 0)
    return {"value_next": value_next, "density": density}


COURANT = 0.4
CONTROL_COST = 0.25
VISCOSITY = 0.15
CROWDING = 0.3


def speeds(first, count, total):
    index = first + jnp.arange(count, dtype=jnp.int32)
    return COURANT * ((index.astype(jnp.float32) + 0.5 - total / 2) / (total / 2))


def along_second(array, step):
    rolled = jnp.roll(array, -step, 2)
    place = lax.broadcasted_iota(jnp.int32, array.shape, 2)
    edge = array.shape[2] - 1 if step > 0 else 0
    return jnp.where(place == edge, array, rolled)


def value_core(centre, x_up, x_dn, a_up, a_dn, speed_x, speed_y, crowding):
    along_x = speed_x[None, :, None, None]
    along_y = speed_y[None, None, :, None]
    carry_x = jnp.where(along_x > 0, along_x * (x_up - centre), along_x * (centre - x_dn))
    ahead_y = jnp.roll(centre, -1, 3) - centre
    behind_y = centre - jnp.roll(centre, 1, 3)
    carry_y = jnp.where(along_y > 0, along_y * ahead_y, along_y * behind_y)
    upper_v = a_up - centre
    lower_v = centre - a_dn
    upper_w = along_second(centre, 1) - centre
    lower_w = centre - along_second(centre, -1)
    hamilton = 0.5 * (jnp.square(jnp.maximum(lower_v, 0.0)) + jnp.square(jnp.minimum(upper_v, 0.0))
                      + jnp.square(jnp.maximum(lower_w, 0.0)) + jnp.square(jnp.minimum(upper_w, 0.0)))
    laplace = upper_v - lower_v + upper_w - lower_w
    return centre + carry_x + carry_y - CONTROL_COST * hamilton + VISCOSITY * laplace + crowding[:, None, None, :]


def density_core(centre, x_up, x_dn, a_up, a_dn, control, control_up, control_dn, speed_x, speed_y):
    along_x = speed_x[None, :, None, None]
    along_y = speed_y[None, None, :, None]
    carry_x = jnp.where(along_x > 0, along_x * (centre - x_dn), along_x * (x_up - centre))
    behind_y = centre - jnp.roll(centre, 1, 3)
    ahead_y = jnp.roll(centre, -1, 3) - centre
    carry_y = jnp.where(along_y > 0, along_y * behind_y, along_y * ahead_y)
    speed_up = -CONTROL_COST * (control_up - control)
    speed_dn = -CONTROL_COST * (control - control_dn)
    flux_up = jnp.maximum(speed_up, 0.0) * centre + jnp.minimum(speed_up, 0.0) * a_up
    flux_dn = jnp.maximum(speed_dn, 0.0) * a_dn + jnp.minimum(speed_dn, 0.0) * centre
    b_up = along_second(centre, 1)
    b_dn = along_second(centre, -1)
    side_up = -CONTROL_COST * (along_second(control, 1) - control)
    side_dn = -CONTROL_COST * (control - along_second(control, -1))
    flux_right = jnp.maximum(side_up, 0.0) * centre + jnp.minimum(side_up, 0.0) * b_up
    flux_left = jnp.maximum(side_dn, 0.0) * b_dn + jnp.minimum(side_dn, 0.0) * centre
    spread = VISCOSITY * (a_up + a_dn - 2.0 * centre + b_up + b_dn - 2.0 * centre)
    return centre - carry_x - carry_y - (flux_up - flux_dn) - (flux_right - flux_left) + spread


def reference(value_next, density):
    grid_v = value_next.shape[1]
    mass = jnp.sum(density, axis=(1, 2)) / (grid_v * grid_v)
    crowding = CROWDING * mass * mass
    speed_all = speeds(0, grid_v, grid_v)
    pieces = []
    for offset in range(0, grid_v, 8):
        rows = offset + jnp.arange(8, dtype=jnp.int32)
        upper = jnp.minimum(rows + 1, grid_v - 1).astype(jnp.int32)
        lower = jnp.maximum(rows - 1, 0).astype(jnp.int32)
        centre = value_next[:, offset:offset + 8]
        pieces.append(value_core(centre, jnp.roll(centre, -1, 0), jnp.roll(centre, 1, 0),
                                 jnp.take(value_next, upper, axis=1), jnp.take(value_next, lower, axis=1),
                                 speed_all[offset:offset + 8], speed_all, crowding))
    value_now = jnp.concatenate(pieces, 1)
    parts = []
    for offset in range(0, grid_v, 8):
        rows = offset + jnp.arange(8, dtype=jnp.int32)
        upper = jnp.minimum(rows + 1, grid_v - 1).astype(jnp.int32)
        lower = jnp.maximum(rows - 1, 0).astype(jnp.int32)
        centre = density[:, offset:offset + 8]
        parts.append(density_core(centre, jnp.roll(centre, -1, 0), jnp.roll(centre, 1, 0),
                                  jnp.take(density, upper, axis=1), jnp.take(density, lower, axis=1),
                                  value_now[:, offset:offset + 8], jnp.take(value_now, upper, axis=1),
                                  jnp.take(value_now, lower, axis=1), speed_all[offset:offset + 8], speed_all))
    density_next = jnp.concatenate(parts, 1)
    return value_now, density_next
```

```python
import functools

import jax
import jax.numpy as jnp
from jax import lax
from jax.experimental import pallas as pl
from jax.experimental.pallas import tpu as pltpu
from jax.sharding import PartitionSpec as P

COURANT = 0.4
CONTROL_COST = 0.25
VISCOSITY = 0.15
CROWDING = 0.3

SUB = 8
VMEM_LIMIT = 48 * 1024 * 1024
ANY = pl.BlockSpec(memory_space=pl.ANY)


def is_negative():
    return lax.axis_index("vel") < lax.axis_size("vel") // 2


def slant(first, total):
    return COURANT * (jnp.abs(first.astype(jnp.float32) + 0.5 - total / 2) / (total / 2))


def start_all(copies):
    for copy in copies:
        copy.start()


def wait_all(copies):
    for copy in copies:
        copy.wait()


def copier(sems):
    count = [0]

    def copy(source, target):
        count[0] += 1
        return pltpu.make_async_copy(source, target, sems.at[count[0] - 1])

    return copy


def value_rows_kernel(begin, end, value, sent, sems):
    row = jnp.where(is_negative(), value.shape[0] - 1, 0)
    copy = copier(sems)
    half = (end - begin) // 2
    parts = ((0, half), (half, end - begin)) if half else ((0, end - begin),)
    copies = [
        copy(value.at[row, pl.ds(begin + lo, hi - lo)], sent.at[pl.ds(lo, hi - lo)])
        for lo, hi in parts
    ]
    start_all(copies)
    wait_all(copies)


def value_rows(value, begin, end):
    shape = (end - begin,) + value.shape[2:]
    return pl.pallas_call(
        functools.partial(value_rows_kernel, begin, end),
        out_shape=jax.ShapeDtypeStruct(shape, value.dtype),
        in_specs=[ANY],
        out_specs=ANY,
        scratch_shapes=[pltpu.SemaphoreType.DMA((2,))],
        cost_estimate=pl.CostEstimate(
            flops=0, transcendentals=0, bytes_accessed=8 * shape[0] * shape[1] * shape[2]
        ),
        name="value_rows",
    )(value)


def edges_kernel(cuts, value, density, low, high, *rest):
    sent, sems = rest[:-1], rest[-1]
    count, rows = value.shape[:2]
    row = jnp.where(is_negative(), 0, count - 1)
    copy = copier(sems)
    copies = []
    for k, field in enumerate((value, density)):
        copies.append(copy(field.at[:, rows - 1], low.at[k]))
        copies.append(copy(field.at[:, 0], high.at[k]))
    for (begin, end), target in zip(cuts, sent):
        copies.append(copy(density.at[row, pl.ds(begin, end - begin)], target))
    start_all(copies)
    wait_all(copies)


def edges(value, density, cuts):
    count, rows, second, width = value.shape
    edge = jax.ShapeDtypeStruct((2, count, second, width), value.dtype)
    parts = [jax.ShapeDtypeStruct((e - b, second, width), value.dtype) for b, e in cuts]
    return pl.pallas_call(
        functools.partial(edges_kernel, cuts),
        out_shape=[edge, edge, *parts],
        in_specs=[ANY, ANY],
        out_specs=[ANY] * (2 + len(cuts)),
        scratch_shapes=[pltpu.SemaphoreType.DMA((4 + len(cuts),))],
        cost_estimate=pl.CostEstimate(
            flops=0, transcendentals=0, bytes_accessed=8 * (4 * count + rows) * second * width
        ),
        name="edges",
    )(value, density)


def padded_copies(copy, field, low, high, pad, i, first, last):
    rows = field.shape[1]
    centre = copy(field.at[i], pad.at[i, pl.ds(1, rows)])
    below = (copy(field.at[i, 0], pad.at[i, 0]), low, 0)
    above = (copy(field.at[i, rows - 1], pad.at[i, rows + 1]), high, rows + 1)
    return centre, [(first, below), (last, above)]


def second_tile(ref, index, at, total):
    here = ref[*index, pl.ds(at, SUB), :]
    place = lax.broadcasted_iota(jnp.int32, here.shape, 0)
    if at + SUB < total:
        above = ref[*index, pl.ds(at + 1, SUB), :]
    else:
        above = jnp.where(place == SUB - 1, here, pltpu.roll(here, SUB - 1, 0))
    if at > 0:
        below = ref[*index, pl.ds(at - 1, SUB), :]
    else:
        below = jnp.where(place == 0, here, pltpu.roll(here, 1, 0))
    return here, above, below


def value_kernel(value, low, high, crowding, *rest):
    parts = len(rest) - 9
    halos = rest[:parts]
    value_now, low_now, high_now, pad, halo, fresh, load, edge, store = rest[parts:]
    count, rows, second, width = value.shape
    negative = is_negative()
    first = lax.axis_index("vel") == 0
    last = lax.axis_index("vel") == lax.axis_size("vel") - 1
    base = lax.axis_index("vel") * rows
    total = rows * lax.axis_size("vel")
    order = [jnp.where(negative, t, count - 1 - t) for t in range(count)]

    begin = 0
    halo_copies = []
    for k, part in enumerate(halos):
        extent = part.shape[0]
        halo_copies.append(
            pltpu.make_async_copy(part, halo.at[pl.ds(begin, extent)], load.at[count + k])
        )
        begin += extent
    start_all(halo_copies)
    centre_copies = [
        pltpu.make_async_copy(value.at[i], pad.at[i, pl.ds(1, rows)], load.at[t])
        for t, i in enumerate(order)
    ]
    start_all(centre_copies)
    below_own = pltpu.make_async_copy(value.at[:, 0], pad.at[:, 0], edge.at[0])
    below_far = pltpu.make_async_copy(low.at[0], pad.at[:, 0], edge.at[0])
    above_own = pltpu.make_async_copy(value.at[:, rows - 1], pad.at[:, rows + 1], edge.at[1])
    above_far = pltpu.make_async_copy(high.at[0], pad.at[:, rows + 1], edge.at[1])
    pl.when(first)(below_own.start)
    pl.when(jnp.logical_not(first))(below_far.start)
    pl.when(last)(above_own.start)
    pl.when(jnp.logical_not(last))(above_far.start)
    below_far.wait()
    above_far.wait()
    wait_all(halo_copies)

    stores = []
    for t, i in enumerate(order):
        centre_copies[t].wait()

        def step(a, carry, t=t, i=i):
            steep = slant(base + a, total)
            for at in range(0, second, SUB):
                here, up_w, dn_w = second_tile(pad, (i, a + 1), at, second)
                if t == 0:
                    x_near = halo[a, pl.ds(at, SUB), :]
                else:
                    x_near = pad[order[t - 1], a + 1, pl.ds(at, SUB), :]
                y_near = pltpu.roll(here, 1 if at < second // 2 else width - 1, 1)
                index = at + lax.broadcasted_iota(jnp.int32, here.shape, 0)
                up_v = pad[i, a + 2, pl.ds(at, SUB), :] - here
                dn_v = here - pad[i, a, pl.ds(at, SUB), :]
                up_w = up_w - here
                dn_w = here - dn_w
                hamilton = (
                    jnp.square(jnp.maximum(dn_v, 0.0))
                    + jnp.square(jnp.minimum(up_v, 0.0))
                    + jnp.square(jnp.maximum(dn_w, 0.0))
                    + jnp.square(jnp.minimum(up_w, 0.0))
                )
                laplace = up_v - dn_v + up_w - dn_w
                fresh[i, a, pl.ds(at, SUB), :] = (
                    here
                    + steep * (x_near - here)
                    + slant(index, second) * (y_near - here)
                    - (0.5 * CONTROL_COST) * hamilton
                    + VISCOSITY * laplace
                    + crowding[pl.ds(i, 1), :]
                )
            return carry

        lax.fori_loop(0, rows, step, 0)
        stores.append(pltpu.make_async_copy(fresh.at[i], value_now.at[i], store.at[t]))
        stores[-1].start()
    stores.append(pltpu.make_async_copy(fresh.at[:, rows - 1], low_now, store.at[count]))
    stores.append(pltpu.make_async_copy(fresh.at[:, 0], high_now, store.at[count + 1]))
    start_all(stores[count:])
    wait_all(stores)


def value_step(value, low, high, crowding, halos):
    count, rows, second, width = value.shape
    cells = count * rows * second * width
    edge = jax.ShapeDtypeStruct((count, second, width), value.dtype)
    return pl.pallas_call(
        value_kernel,
        out_shape=[jax.ShapeDtypeStruct(value.shape, value.dtype), edge, edge],
        in_specs=[ANY, ANY, ANY, pl.BlockSpec(memory_space=pltpu.VMEM)] + [ANY] * len(halos),
        out_specs=[ANY] * 3,
        scratch_shapes=[
            pltpu.VMEM((count, rows + 2, second, width), value.dtype),
            pltpu.VMEM((rows, second, width), value.dtype),
            pltpu.VMEM(value.shape, value.dtype),
            pltpu.SemaphoreType.DMA((count + len(halos),)),
            pltpu.SemaphoreType.DMA((2,)),
            pltpu.SemaphoreType.DMA((count + 2,)),
        ],
        compiler_params=pltpu.CompilerParams(vmem_limit_bytes=VMEM_LIMIT),
        cost_estimate=pl.CostEstimate(
            flops=40 * cells, transcendentals=0, bytes_accessed=12 * cells
        ),
        name="value_step",
    )(value, low, high, crowding, *halos)


def density_kernel(
    density, control, low, high, low_now, high_now, out, pad, ctl, fresh, load, edge, store
):
    count, rows, second, width = density.shape
    negative = is_negative()
    first = lax.axis_index("vel") == 0
    last = lax.axis_index("vel") == lax.axis_size("vel") - 1
    base = lax.axis_index("vel") * rows
    total = rows * lax.axis_size("vel")
    order = [jnp.where(negative, count - 1 - t, t) for t in range(count)]

    centre_copies = []
    for t, i in enumerate(order):
        pair = [
            pltpu.make_async_copy(density.at[i], pad.at[i, pl.ds(1, rows)], load.at[2 * t]),
            pltpu.make_async_copy(control.at[i], ctl.at[i, pl.ds(1, rows)], load.at[2 * t + 1]),
        ]
        start_all(pair)
        centre_copies.append(pair)
    waits = []
    fields = ((density, low.at[1], high.at[1], pad), (control, low_now, high_now, ctl))
    for k, (field, below, above, padded) in enumerate(fields):
        for outer, own, far, place, sem in (
            (first, field.at[:, 0], below, 0, edge.at[2 * k]),
            (last, field.at[:, rows - 1], above, rows + 1, edge.at[2 * k + 1]),
        ):
            own_copy = pltpu.make_async_copy(own, padded.at[:, place], sem)
            far_copy = pltpu.make_async_copy(far, padded.at[:, place], sem)
            pl.when(outer)(own_copy.start)
            pl.when(jnp.logical_not(outer))(far_copy.start)
            waits.append(far_copy)
    wait_all(waits)

    stores = []
    for t, i in enumerate(order):
        wait_all(centre_copies[t])

        def step(a, carry, t=t, i=i):
            steep = slant(base + a, total)
            for at in range(0, second, SUB):
                here, up_w, dn_w = second_tile(pad, (i, a + 1), at, second)
                ctl_here, ctl_up_w, ctl_dn_w = second_tile(ctl, (i, a + 1), at, second)
                up_v = pad[i, a + 2, pl.ds(at, SUB), :]
                dn_v = pad[i, a, pl.ds(at, SUB), :]
                y_near = pltpu.roll(here, width - 1 if at < second // 2 else 1, 1)
                index = at + lax.broadcasted_iota(jnp.int32, here.shape, 0)
                if t == 0:
                    along_x = -steep * here
                else:
                    along_x = steep * (pad[order[t - 1], a + 1, pl.ds(at, SUB), :] - here)
                speed_up = -CONTROL_COST * (ctl[i, a + 2, pl.ds(at, SUB), :] - ctl_here)
                speed_dn = -CONTROL_COST * (ctl_here - ctl[i, a, pl.ds(at, SUB), :])
                flux_up = jnp.maximum(speed_up, 0.0) * here + jnp.minimum(speed_up, 0.0) * up_v
                flux_dn = jnp.maximum(speed_dn, 0.0) * dn_v + jnp.minimum(speed_dn, 0.0) * here
                side_up = -CONTROL_COST * (ctl_up_w - ctl_here)
                side_dn = -CONTROL_COST * (ctl_here - ctl_dn_w)
                flux_right = jnp.maximum(side_up, 0.0) * here + jnp.minimum(side_up, 0.0) * up_w
                flux_left = jnp.maximum(side_dn, 0.0) * dn_w + jnp.minimum(side_dn, 0.0) * here
                spread = up_v + dn_v - 2.0 * here + up_w + dn_w - 2.0 * here
                fresh[i, a, pl.ds(at, SUB), :] = (
                    here
                    + along_x
                    + slant(index, second) * (y_near - here)
                    - (flux_up - flux_dn)
                    - (flux_right - flux_left)
                    + VISCOSITY * spread
                )
            return carry

        lax.fori_loop(0, rows, step, 0)
        stores.append(pltpu.make_async_copy(fresh.at[i], out.at[i], store.at[t]))
        stores[-1].start()
    wait_all(stores)


def density_step(density, control, low, high, low_now, high_now):
    count, rows, second, width = density.shape
    cells = count * rows * second * width
    padded = pltpu.VMEM((count, rows + 2, second, width), density.dtype)
    return pl.pallas_call(
        density_kernel,
        out_shape=jax.ShapeDtypeStruct(density.shape, density.dtype),
        in_specs=[ANY] * 6,
        out_specs=ANY,
        scratch_shapes=[
            padded,
            padded,
            pltpu.VMEM(density.shape, density.dtype),
            pltpu.SemaphoreType.DMA((2 * count,)),
            pltpu.SemaphoreType.DMA((4,)),
            pltpu.SemaphoreType.DMA((count,)),
        ],
        compiler_params=pltpu.CompilerParams(vmem_limit_bytes=VMEM_LIMIT),
        cost_estimate=pl.CostEstimate(
            flops=60 * cells, transcendentals=0, bytes_accessed=12 * cells
        ),
        name="density_step",
    )(density, control, low, high, low_now, high_now)


def arrive_kernel(begin, partial, halo, out, held, near, sems):
    count, rows = partial.shape[:2]
    extent, second = halo.shape[:2]
    row = jnp.where(is_negative(), count - 1, 0)
    base = lax.axis_index("vel") * rows + begin
    total = rows * lax.axis_size("vel")
    loads = [
        pltpu.make_async_copy(partial.at[row, pl.ds(begin, extent)], held, sems.at[0]),
        pltpu.make_async_copy(halo, near, sems.at[1]),
    ]
    start_all(loads)
    wait_all(loads)

    def step(a, carry):
        held[a] = held[a] + slant(base + a, total) * near[a]
        return carry

    lax.fori_loop(0, extent, step, 0)
    back = pltpu.make_async_copy(held, out.at[row, pl.ds(begin, extent)], sems.at[2])
    back.start()
    back.wait()


def arrive(partial, halo, begin):
    block = pltpu.VMEM(halo.shape, halo.dtype)
    return pl.pallas_call(
        functools.partial(arrive_kernel, begin),
        out_shape=jax.ShapeDtypeStruct(partial.shape, partial.dtype),
        in_specs=[ANY, ANY],
        out_specs=ANY,
        scratch_shapes=[block, block, pltpu.SemaphoreType.DMA((3,))],
        input_output_aliases={0: 0},
        compiler_params=pltpu.CompilerParams(vmem_limit_bytes=VMEM_LIMIT),
        cost_estimate=pl.CostEstimate(
            flops=2 * halo.size, transcendentals=0, bytes_accessed=12 * halo.size
        ),
        name="arrive",
    )(partial, halo)


def routes(mesh):
    names = tuple(mesh.axis_names)
    sizes = [mesh.shape[name] for name in names]
    slabs, groups = mesh.shape["pos"], mesh.shape["vel"]

    def place(pos, vel):
        at = {"pos": pos % slabs, "vel": vel}
        index = 0
        for name, size in zip(names, sizes):
            index = index * size + at[name]
        return index

    value_route, density_route = [], []
    for pos in range(slabs):
        for vel in range(groups):
            onward = 1 if vel < groups // 2 else -1
            value_route.append((place(pos, vel), place(pos + onward, vel)))
            density_route.append((place(pos, vel), place(pos - onward, vel)))
    return names, value_route, density_route


def body(mesh, value_next, density):
    names, value_route, density_route = routes(mesh)
    groups = mesh.shape["vel"]
    count, rows, second, width = value_next.shape
    tail = max(1, rows // 8)
    cuts = ((0, rows - tail), (rows - tail, rows))
    onward = [(v, v + 1) for v in range(groups - 1)]
    back = [(v + 1, v) for v in range(groups - 1)]

    value_halos = []
    for begin, end in cuts:
        sent = value_rows(value_next, begin, end)
        value_halos.append(lax.ppermute(sent, names, value_route))
    low, high, *leaving = edges(value_next, density, cuts)
    low = lax.ppermute(low, "vel", onward)
    high = lax.ppermute(high, "vel", back)
    mass = lax.psum(jnp.sum(density, axis=(1, 2)), "vel") / (second * second)
    crowding = CROWDING * mass * mass

    *leaving, ready = lax.optimization_barrier((*leaving, value_halos[0]))
    value_halos[0] = ready
    density_halos = [lax.ppermute(part, names, density_route) for part in leaving]

    value_now, low_now, high_now = value_step(value_next, low, high, crowding, value_halos)
    low_now = lax.ppermute(low_now, "vel", onward)
    high_now = lax.ppermute(high_now, "vel", back)
    density_next = density_step(density, value_now, low, high, low_now, high_now)
    for (begin, _), halo in zip(cuts, density_halos):
        density_next = arrive(density_next, halo, begin)
    return value_now, density_next


def solution(mesh):
    placed = (P("pos", "vel", None, None), P("pos", "vel", None, None))
    return jax.shard_map(
        functools.partial(body, mesh),
        mesh=mesh,
        in_specs=placed,
        out_specs=placed,
        check_vma=False,
    )
```

```python
import functools

import jax
import jax.numpy as jnp
from jax import lax
from jax.experimental import pallas as pl
from jax.experimental.pallas import tpu as pltpu
from jax.sharding import PartitionSpec as P

COURANT = 0.4
CONTROL_COST = 0.25
VISCOSITY = 0.15
CROWDING = 0.3

SUB = 8
VMEM_LIMIT = 60 * 1024 * 1024
ANY = pl.BlockSpec(memory_space=pl.ANY)
HBM = pl.BlockSpec(memory_space=pltpu.HBM)
VMEM = pl.BlockSpec(memory_space=pltpu.VMEM)


def is_negative():
    return lax.axis_index("vel") < lax.axis_size("vel") // 2


def slant(first, total):
    return COURANT * (jnp.abs(first.astype(jnp.float32) + 0.5 - total / 2) / (total / 2))


def start_all(copies):
    for copy in copies:
        copy.start()


def wait_all(copies):
    for copy in copies:
        copy.wait()


def value_rows_kernel(cuts, value, *rest):
    sent, sems = rest[:-1], rest[-1]
    row = jnp.where(is_negative(), value.shape[0] - 1, 0)
    copies = [
        pltpu.make_async_copy(value.at[row, pl.ds(begin, end - begin)], target, sems.at[k])
        for k, ((begin, end), target) in enumerate(zip(cuts, sent))
    ]
    start_all(copies)
    wait_all(copies)


def value_rows(value, cuts):
    _, rows, second, width = value.shape
    parts = [jax.ShapeDtypeStruct((e - b, second, width), value.dtype) for b, e in cuts]
    return pl.pallas_call(
        functools.partial(value_rows_kernel, cuts),
        out_shape=parts,
        in_specs=[HBM],
        out_specs=[VMEM] * len(cuts),
        scratch_shapes=[pltpu.SemaphoreType.DMA((len(cuts),))],
        compiler_params=pltpu.CompilerParams(vmem_limit_bytes=VMEM_LIMIT),
        cost_estimate=pl.CostEstimate(
            flops=0, transcendentals=0, bytes_accessed=8 * rows * second * width
        ),
        name="value_rows",
    )(value)


def edges_kernel(cuts, value, density, low, high, *rest):
    sent, sems = rest[:-1], rest[-1]
    count, rows = value.shape[:2]
    row = jnp.where(is_negative(), 0, count - 1)
    pairs = []
    for k, field in enumerate((value, density)):
        pairs.append((field.at[:, rows - 1], low.at[k]))
        pairs.append((field.at[:, 0], high.at[k]))
    for (begin, end), target in zip(cuts, sent):
        pairs.append((density.at[row, pl.ds(begin, end - begin)], target))
    copies = [pltpu.make_async_copy(s, t, sems.at[k]) for k, (s, t) in enumerate(pairs)]
    start_all(copies)
    wait_all(copies)


def edges(value, density, cuts):
    count, rows, second, width = value.shape
    edge = jax.ShapeDtypeStruct((2, count, second, width), value.dtype)
    parts = [jax.ShapeDtypeStruct((e - b, second, width), value.dtype) for b, e in cuts]
    return pl.pallas_call(
        functools.partial(edges_kernel, cuts),
        out_shape=[edge, edge, *parts],
        in_specs=[HBM, HBM],
        out_specs=[VMEM] * (2 + len(cuts)),
        scratch_shapes=[pltpu.SemaphoreType.DMA((4 + len(cuts),))],
        compiler_params=pltpu.CompilerParams(vmem_limit_bytes=VMEM_LIMIT),
        cost_estimate=pl.CostEstimate(
            flops=0, transcendentals=0, bytes_accessed=8 * (4 * count + rows) * second * width
        ),
        name="edges",
    )(value, density)


def second_tile(ref, index, at, total):
    here = ref[*index, pl.ds(at, SUB), :]
    place = lax.broadcasted_iota(jnp.int32, here.shape, 0)
    if at + SUB < total:
        above = ref[*index, pl.ds(at + 1, SUB), :]
    else:
        above = jnp.where(place == SUB - 1, here, pltpu.roll(here, SUB - 1, 0))
    if at > 0:
        below = ref[*index, pl.ds(at - 1, SUB), :]
    else:
        below = jnp.where(place == 0, here, pltpu.roll(here, 1, 0))
    return here, above, below


def value_kernel(value, low, high, crowding, *rest):
    parts = len(rest) - 9
    halos = rest[:parts]
    value_now, low_now, high_now, pad, halo, fresh, load, edge, store = rest[parts:]
    count, rows, second, width = value.shape
    negative = is_negative()
    first = lax.axis_index("vel") == 0
    last = lax.axis_index("vel") == lax.axis_size("vel") - 1
    base = lax.axis_index("vel") * rows
    total = rows * lax.axis_size("vel")
    order = [jnp.where(negative, t, count - 1 - t) for t in range(count)]

    begin = 0
    halo_copies = []
    for k, part in enumerate(halos):
        extent = part.shape[0]
        halo_copies.append(
            pltpu.make_async_copy(part, halo.at[pl.ds(begin, extent)], load.at[count + k])
        )
        begin += extent
    start_all(halo_copies)
    centre_copies = [
        pltpu.make_async_copy(value.at[i], pad.at[i, pl.ds(1, rows)], load.at[t])
        for t, i in enumerate(order)
    ]
    start_all(centre_copies)
    below_own = pltpu.make_async_copy(value.at[:, 0], pad.at[:, 0], edge.at[0])
    below_far = pltpu.make_async_copy(low.at[0], pad.at[:, 0], edge.at[0])
    above_own = pltpu.make_async_copy(value.at[:, rows - 1], pad.at[:, rows + 1], edge.at[1])
    above_far = pltpu.make_async_copy(high.at[0], pad.at[:, rows + 1], edge.at[1])
    pl.when(first)(below_own.start)
    pl.when(jnp.logical_not(first))(below_far.start)
    pl.when(last)(above_own.start)
    pl.when(jnp.logical_not(last))(above_far.start)
    below_far.wait()
    above_far.wait()
    wait_all(halo_copies)

    stores = []
    for t, i in enumerate(order):
        centre_copies[t].wait()

        def step(a, carry, t=t, i=i):
            steep = slant(base + a, total)
            for at in range(0, second, SUB):
                here, up_w, dn_w = second_tile(pad, (i, a + 1), at, second)
                if t == 0:
                    x_near = halo[a, pl.ds(at, SUB), :]
                else:
                    x_near = pad[order[t - 1], a + 1, pl.ds(at, SUB), :]
                y_near = pltpu.roll(here, 1 if at < second // 2 else width - 1, 1)
                index = at + lax.broadcasted_iota(jnp.int32, here.shape, 0)
                up_v = pad[i, a + 2, pl.ds(at, SUB), :] - here
                dn_v = here - pad[i, a, pl.ds(at, SUB), :]
                up_w = up_w - here
                dn_w = here - dn_w
                hamilton = (
                    jnp.square(jnp.maximum(dn_v, 0.0))
                    + jnp.square(jnp.minimum(up_v, 0.0))
                    + jnp.square(jnp.maximum(dn_w, 0.0))
                    + jnp.square(jnp.minimum(up_w, 0.0))
                )
                laplace = up_v - dn_v + up_w - dn_w
                fresh[i, a, pl.ds(at, SUB), :] = (
                    here
                    + steep * (x_near - here)
                    + slant(index, second) * (y_near - here)
                    - (0.5 * CONTROL_COST) * hamilton
                    + VISCOSITY * laplace
                    + crowding[pl.ds(i, 1), :]
                )
            return carry

        lax.fori_loop(0, rows, step, 0)
        stores.append(pltpu.make_async_copy(fresh.at[i], value_now.at[i], store.at[t]))
        stores[-1].start()
    stores.append(pltpu.make_async_copy(fresh.at[:, rows - 1], low_now, store.at[count]))
    stores.append(pltpu.make_async_copy(fresh.at[:, 0], high_now, store.at[count + 1]))
    start_all(stores[count:])
    wait_all(stores)


def value_step(value, low, high, crowding, halos):
    count, rows, second, width = value.shape
    cells = count * rows * second * width
    edge = jax.ShapeDtypeStruct((count, second, width), value.dtype)
    return pl.pallas_call(
        value_kernel,
        out_shape=[jax.ShapeDtypeStruct(value.shape, value.dtype), edge, edge],
        in_specs=[ANY, ANY, ANY, VMEM] + [ANY] * len(halos),
        out_specs=[ANY] * 3,
        scratch_shapes=[
            pltpu.VMEM((count, rows + 2, second, width), value.dtype),
            pltpu.VMEM((rows, second, width), value.dtype),
            pltpu.VMEM(value.shape, value.dtype),
            pltpu.SemaphoreType.DMA((count + len(halos),)),
            pltpu.SemaphoreType.DMA((2,)),
            pltpu.SemaphoreType.DMA((count + 2,)),
        ],
        compiler_params=pltpu.CompilerParams(vmem_limit_bytes=VMEM_LIMIT),
        cost_estimate=pl.CostEstimate(
            flops=40 * cells, transcendentals=0, bytes_accessed=12 * cells
        ),
        name="value_step",
    )(value, low, high, crowding, *halos)


def density_kernel(
    density, control, low, high, low_now, high_now, out, pad, ctl, fresh, load, edge, store
):
    count, rows, second, width = density.shape
    negative = is_negative()
    first = lax.axis_index("vel") == 0
    last = lax.axis_index("vel") == lax.axis_size("vel") - 1
    base = lax.axis_index("vel") * rows
    total = rows * lax.axis_size("vel")
    order = [jnp.where(negative, count - 1 - t, t) for t in range(count)]

    centre_copies = []
    for t, i in enumerate(order):
        pair = [
            pltpu.make_async_copy(density.at[i], pad.at[i, pl.ds(1, rows)], load.at[2 * t]),
            pltpu.make_async_copy(control.at[i], ctl.at[i, pl.ds(1, rows)], load.at[2 * t + 1]),
        ]
        start_all(pair)
        centre_copies.append(pair)
    waits = []
    fields = ((density, low.at[1], high.at[1], pad), (control, low_now, high_now, ctl))
    for k, (field, below, above, padded) in enumerate(fields):
        for outer, own, far, place, sem in (
            (first, field.at[:, 0], below, 0, edge.at[2 * k]),
            (last, field.at[:, rows - 1], above, rows + 1, edge.at[2 * k + 1]),
        ):
            own_copy = pltpu.make_async_copy(own, padded.at[:, place], sem)
            far_copy = pltpu.make_async_copy(far, padded.at[:, place], sem)
            pl.when(outer)(own_copy.start)
            pl.when(jnp.logical_not(outer))(far_copy.start)
            waits.append(far_copy)
    wait_all(waits)

    stores = []
    for t, i in enumerate(order):
        wait_all(centre_copies[t])

        def step(a, carry, t=t, i=i):
            steep = slant(base + a, total)
            for at in range(0, second, SUB):
                here, up_w, dn_w = second_tile(pad, (i, a + 1), at, second)
                ctl_here, ctl_up_w, ctl_dn_w = second_tile(ctl, (i, a + 1), at, second)
                up_v = pad[i, a + 2, pl.ds(at, SUB), :]
                dn_v = pad[i, a, pl.ds(at, SUB), :]
                y_near = pltpu.roll(here, width - 1 if at < second // 2 else 1, 1)
                index = at + lax.broadcasted_iota(jnp.int32, here.shape, 0)
                if t == 0:
                    along_x = -steep * here
                else:
                    along_x = steep * (pad[order[t - 1], a + 1, pl.ds(at, SUB), :] - here)
                speed_up = -CONTROL_COST * (ctl[i, a + 2, pl.ds(at, SUB), :] - ctl_here)
                speed_dn = -CONTROL_COST * (ctl_here - ctl[i, a, pl.ds(at, SUB), :])
                flux_up = jnp.maximum(speed_up, 0.0) * here + jnp.minimum(speed_up, 0.0) * up_v
                flux_dn = jnp.maximum(speed_dn, 0.0) * dn_v + jnp.minimum(speed_dn, 0.0) * here
                side_up = -CONTROL_COST * (ctl_up_w - ctl_here)
                side_dn = -CONTROL_COST * (ctl_here - ctl_dn_w)
                flux_right = jnp.maximum(side_up, 0.0) * here + jnp.minimum(side_up, 0.0) * up_w
                flux_left = jnp.maximum(side_dn, 0.0) * dn_w + jnp.minimum(side_dn, 0.0) * here
                spread = up_v + dn_v - 2.0 * here + up_w + dn_w - 2.0 * here
                fresh[i, a, pl.ds(at, SUB), :] = (
                    here
                    + along_x
                    + slant(index, second) * (y_near - here)
                    - (flux_up - flux_dn)
                    - (flux_right - flux_left)
                    + VISCOSITY * spread
                )
            return carry

        lax.fori_loop(0, rows, step, 0)
        stores.append(pltpu.make_async_copy(fresh.at[i], out.at[i], store.at[t]))
        stores[-1].start()
    wait_all(stores)


def density_step(density, control, low, high, low_now, high_now):
    count, rows, second, width = density.shape
    cells = count * rows * second * width
    padded = pltpu.VMEM((count, rows + 2, second, width), density.dtype)
    return pl.pallas_call(
        density_kernel,
        out_shape=jax.ShapeDtypeStruct(density.shape, density.dtype),
        in_specs=[ANY] * 6,
        out_specs=ANY,
        scratch_shapes=[
            padded,
            padded,
            pltpu.VMEM(density.shape, density.dtype),
            pltpu.SemaphoreType.DMA((2 * count,)),
            pltpu.SemaphoreType.DMA((4,)),
            pltpu.SemaphoreType.DMA((count,)),
        ],
        compiler_params=pltpu.CompilerParams(vmem_limit_bytes=VMEM_LIMIT),
        cost_estimate=pl.CostEstimate(
            flops=60 * cells, transcendentals=0, bytes_accessed=12 * cells
        ),
        name="density_step",
    )(density, control, low, high, low_now, high_now)


def arrive_kernel(begin, partial, halo, out, held, near, sems):
    count, rows = partial.shape[:2]
    extent, second = halo.shape[:2]
    row = jnp.where(is_negative(), count - 1, 0)
    base = lax.axis_index("vel") * rows + begin
    total = rows * lax.axis_size("vel")
    loads = [
        pltpu.make_async_copy(partial.at[row, pl.ds(begin, extent)], held, sems.at[0]),
        pltpu.make_async_copy(halo, near, sems.at[1]),
    ]
    start_all(loads)
    wait_all(loads)

    def step(a, carry):
        held[a] = held[a] + slant(base + a, total) * near[a]
        return carry

    lax.fori_loop(0, extent, step, 0)
    back = pltpu.make_async_copy(held, out.at[row, pl.ds(begin, extent)], sems.at[2])
    back.start()
    back.wait()


def arrive(partial, halo, begin):
    block = pltpu.VMEM(halo.shape, halo.dtype)
    return pl.pallas_call(
        functools.partial(arrive_kernel, begin),
        out_shape=jax.ShapeDtypeStruct(partial.shape, partial.dtype),
        in_specs=[ANY, ANY],
        out_specs=ANY,
        scratch_shapes=[block, block, pltpu.SemaphoreType.DMA((3,))],
        input_output_aliases={0: 0},
        compiler_params=pltpu.CompilerParams(vmem_limit_bytes=VMEM_LIMIT),
        cost_estimate=pl.CostEstimate(
            flops=2 * halo.size, transcendentals=0, bytes_accessed=12 * halo.size
        ),
        name="arrive",
    )(partial, halo)


def routes(mesh):
    names = tuple(mesh.axis_names)
    sizes = [mesh.shape[name] for name in names]
    slabs, groups = mesh.shape["pos"], mesh.shape["vel"]

    def place(pos, vel):
        at = {"pos": pos % slabs, "vel": vel}
        index = 0
        for name, size in zip(names, sizes):
            index = index * size + at[name]
        return index

    value_route, density_route = [], []
    for pos in range(slabs):
        for vel in range(groups):
            onward = 1 if vel < groups // 2 else -1
            value_route.append((place(pos, vel), place(pos + onward, vel)))
            density_route.append((place(pos, vel), place(pos - onward, vel)))
    return names, value_route, density_route


def body(mesh, value_next, density):
    names, value_route, density_route = routes(mesh)
    groups = mesh.shape["vel"]
    count, rows, second, width = value_next.shape
    tail = max(1, rows // 8)
    cuts = ((0, rows - tail), (rows - tail, rows))
    onward = [(v, v + 1) for v in range(groups - 1)]
    back = [(v + 1, v) for v in range(groups - 1)]

    value_halos = [
        lax.ppermute(part, names, value_route) for part in value_rows(value_next, ((0, rows),))
    ]
    low, high, *leaving = edges(value_next, density, cuts)
    low = lax.ppermute(low, "vel", onward)
    high = lax.ppermute(high, "vel", back)
    mass = lax.psum(jnp.sum(density, axis=(1, 2)), "vel") / (second * second)
    crowding = CROWDING * mass * mass

    held = (*leaving, *value_halos, crowding, low, high)
    *leaving, value_halo, crowding, low, high = lax.optimization_barrier(held)
    value_halos = [value_halo]
    density_halos = [lax.ppermute(part, names, density_route) for part in leaving]

    value_now, low_now, high_now = value_step(value_next, low, high, crowding, value_halos)
    low_now = lax.ppermute(low_now, "vel", onward)
    high_now = lax.ppermute(high_now, "vel", back)
    density_next = density_step(density, value_now, low, high, low_now, high_now)
    for (begin, _), halo in zip(cuts, density_halos):
        density_next = arrive(density_next, halo, begin)
    return value_now, density_next


def solution(mesh):
    placed = (P("pos", "vel", None, None), P("pos", "vel", None, None))
    return jax.shard_map(
        functools.partial(body, mesh),
        mesh=mesh,
        in_specs=placed,
        out_specs=placed,
        check_vma=False,
    )
```

```python
import functools

import jax
import jax.numpy as jnp
from jax import lax
from jax.experimental import pallas as pl
from jax.experimental.pallas import tpu as pltpu
from jax.sharding import PartitionSpec as P

COURANT = 0.4
CONTROL_COST = 0.25
VISCOSITY = 0.15
CROWDING = 0.3

SUB = 8
VMEM_LIMIT = 18 * 1024 * 1024
ANY = pl.BlockSpec(memory_space=pl.ANY)
HBM = pl.BlockSpec(memory_space=pltpu.HBM)
VMEM = pl.BlockSpec(memory_space=pltpu.VMEM)


def is_negative():
    return lax.axis_index("vel") < lax.axis_size("vel") // 2


def slant(first, total):
    return COURANT * (jnp.abs(first.astype(jnp.float32) + 0.5 - total / 2) / (total / 2))


def start_all(copies):
    for copy in copies:
        copy.start()


def wait_all(copies):
    for copy in copies:
        copy.wait()


def in_hbm(array):
    return pltpu.with_memory_space_constraint(array, pltpu.HBM)


def in_vmem(array):
    return pltpu.with_memory_space_constraint(array, pltpu.VMEM)


def relay(pairs, held, load, store):
    inward = [
        pltpu.make_async_copy(source, held.at[k], load.at[k]) for k, (source, _) in enumerate(pairs)
    ]
    outward = [
        pltpu.make_async_copy(held.at[k], target, store.at[k]) for k, (_, target) in enumerate(pairs)
    ]
    start_all(inward)
    for come, go in zip(inward, outward):
        come.wait()
        go.start()
    wait_all(outward)


def relay_scratch(slots, second, width, dtype):
    sems = pltpu.SemaphoreType.DMA((slots,))
    return [pltpu.VMEM((slots, second, width), dtype), sems, sems]


def leaving_rows(field, row, cuts, sent):
    return [
        (field.at[row, a], target.at[a - begin])
        for (begin, end), target in zip(cuts, sent)
        for a in range(begin, end)
    ]


def value_rows_kernel(begin, end, value, sent, *scratch):
    row = jnp.where(is_negative(), value.shape[0] - 1, 0)
    relay(leaving_rows(value, row, ((begin, end),), (sent,)), *scratch)


def value_rows(value, begin, end):
    shape = (end - begin,) + value.shape[2:]
    sent = jax.ShapeDtypeStruct(shape, value.dtype)
    return pl.pallas_call(
        functools.partial(value_rows_kernel, begin, end),
        out_shape=sent,
        in_specs=[ANY],
        out_specs=ANY,
        scratch_shapes=relay_scratch(*shape, value.dtype),
        compiler_params=pltpu.CompilerParams(vmem_limit_bytes=VMEM_LIMIT),
        cost_estimate=pl.CostEstimate(flops=0, transcendentals=0, bytes_accessed=8 * sent.size),
        name="value_rows",
    )(in_hbm(value))


def edges_kernel(cuts, value, density, low, high, *rest):
    count, rows = value.shape[:2]
    row = jnp.where(is_negative(), 0, count - 1)
    pairs = []
    for k, field in enumerate((value, density)):
        for i in range(count):
            pairs.append((field.at[i, rows - 1], low.at[k, i]))
            pairs.append((field.at[i, 0], high.at[k, i]))
    pairs += leaving_rows(density, row, cuts, rest[: len(cuts)])
    relay(pairs, *rest[len(cuts) :])


def edges(value, density, cuts):
    count, rows, second, width = value.shape
    edge = jax.ShapeDtypeStruct((2, count, second, width), value.dtype)
    parts = [jax.ShapeDtypeStruct((e - b, second, width), value.dtype) for b, e in cuts]
    return pl.pallas_call(
        functools.partial(edges_kernel, cuts),
        out_shape=[edge, edge, *parts],
        in_specs=[ANY, ANY],
        out_specs=[ANY] * (2 + len(cuts)),
        scratch_shapes=relay_scratch(4 * count + rows, second, width, value.dtype),
        compiler_params=pltpu.CompilerParams(vmem_limit_bytes=VMEM_LIMIT),
        cost_estimate=pl.CostEstimate(
            flops=0, transcendentals=0, bytes_accessed=8 * (4 * count + rows) * second * width
        ),
        name="edges",
    )(in_hbm(value), in_hbm(density))


def second_tile(ref, index, at, total):
    here = ref[*index, pl.ds(at, SUB), :]
    place = lax.broadcasted_iota(jnp.int32, here.shape, 0)
    if at + SUB < total:
        above = ref[*index, pl.ds(at + 1, SUB), :]
    else:
        above = jnp.where(place == SUB - 1, here, pltpu.roll(here, SUB - 1, 0))
    if at > 0:
        below = ref[*index, pl.ds(at - 1, SUB), :]
    else:
        below = jnp.where(place == 0, here, pltpu.roll(here, 1, 0))
    return here, above, below


def value_kernel(value, low, high, crowding, *rest):
    parts = len(rest) - 9
    halos = rest[:parts]
    value_now, low_now, high_now, pad, halo, fresh, load, edge, store = rest[parts:]
    count, rows, second, width = value.shape
    negative = is_negative()
    first = lax.axis_index("vel") == 0
    last = lax.axis_index("vel") == lax.axis_size("vel") - 1
    base = lax.axis_index("vel") * rows
    total = rows * lax.axis_size("vel")
    order = [jnp.where(negative, t, count - 1 - t) for t in range(count)]

    begin = 0
    halo_copies = []
    for k, part in enumerate(halos):
        extent = part.shape[0]
        halo_copies.append(
            pltpu.make_async_copy(part, halo.at[pl.ds(begin, extent)], load.at[count + k])
        )
        begin += extent
    start_all(halo_copies)
    centre_copies = [
        pltpu.make_async_copy(value.at[i], pad.at[i, pl.ds(1, rows)], load.at[t])
        for t, i in enumerate(order)
    ]
    start_all(centre_copies)
    below_own = pltpu.make_async_copy(value.at[:, 0], pad.at[:, 0], edge.at[0])
    below_far = pltpu.make_async_copy(low.at[0], pad.at[:, 0], edge.at[0])
    above_own = pltpu.make_async_copy(value.at[:, rows - 1], pad.at[:, rows + 1], edge.at[1])
    above_far = pltpu.make_async_copy(high.at[0], pad.at[:, rows + 1], edge.at[1])
    pl.when(first)(below_own.start)
    pl.when(jnp.logical_not(first))(below_far.start)
    pl.when(last)(above_own.start)
    pl.when(jnp.logical_not(last))(above_far.start)
    below_far.wait()
    above_far.wait()
    wait_all(halo_copies)

    stores = []
    for t, i in enumerate(order):
        centre_copies[t].wait()

        def step(a, carry, t=t, i=i):
            steep = slant(base + a, total)
            for at in range(0, second, SUB):
                here, up_w, dn_w = second_tile(pad, (i, a + 1), at, second)
                if t == 0:
                    x_near = halo[a, pl.ds(at, SUB), :]
                else:
                    x_near = pad[order[t - 1], a + 1, pl.ds(at, SUB), :]
                y_near = pltpu.roll(here, 1 if at < second // 2 else width - 1, 1)
                index = at + lax.broadcasted_iota(jnp.int32, here.shape, 0)
                up_v = pad[i, a + 2, pl.ds(at, SUB), :] - here
                dn_v = here - pad[i, a, pl.ds(at, SUB), :]
                up_w = up_w - here
                dn_w = here - dn_w
                hamilton = (
                    jnp.square(jnp.maximum(dn_v, 0.0))
                    + jnp.square(jnp.minimum(up_v, 0.0))
                    + jnp.square(jnp.maximum(dn_w, 0.0))
                    + jnp.square(jnp.minimum(up_w, 0.0))
                )
                laplace = up_v - dn_v + up_w - dn_w
                fresh[i, a, pl.ds(at, SUB), :] = (
                    here
                    + steep * (x_near - here)
                    + slant(index, second) * (y_near - here)
                    - (0.5 * CONTROL_COST) * hamilton
                    + VISCOSITY * laplace
                    + crowding[pl.ds(i, 1), :]
                )
            return carry

        lax.fori_loop(0, rows, step, 0)
        stores.append(pltpu.make_async_copy(fresh.at[i], value_now.at[i], store.at[t]))
        stores[-1].start()
    stores.append(pltpu.make_async_copy(fresh.at[:, rows - 1], low_now, store.at[count]))
    stores.append(pltpu.make_async_copy(fresh.at[:, 0], high_now, store.at[count + 1]))
    start_all(stores[count:])
    wait_all(stores)


def value_step(value, low, high, crowding, halos):
    count, rows, second, width = value.shape
    cells = count * rows * second * width
    edge = jax.ShapeDtypeStruct((count, second, width), value.dtype)
    return pl.pallas_call(
        value_kernel,
        out_shape=[jax.ShapeDtypeStruct(value.shape, value.dtype), edge, edge],
        in_specs=[ANY, ANY, ANY, VMEM] + [ANY] * len(halos),
        out_specs=[ANY] * 3,
        scratch_shapes=[
            pltpu.VMEM((count, rows + 2, second, width), value.dtype),
            pltpu.VMEM((rows, second, width), value.dtype),
            pltpu.VMEM(value.shape, value.dtype),
            pltpu.SemaphoreType.DMA((count + len(halos),)),
            pltpu.SemaphoreType.DMA((2,)),
            pltpu.SemaphoreType.DMA((count + 2,)),
        ],
        compiler_params=pltpu.CompilerParams(vmem_limit_bytes=VMEM_LIMIT),
        cost_estimate=pl.CostEstimate(
            flops=40 * cells, transcendentals=0, bytes_accessed=12 * cells
        ),
        name="value_step",
    )(in_hbm(value), low, high, crowding, *halos)


def density_kernel(
    density, control, low, high, low_now, high_now, out, rest, pad, ctl, fresh, load, edge, store
):
    count, rows, second, width = density.shape
    negative = is_negative()
    first = lax.axis_index("vel") == 0
    last = lax.axis_index("vel") == lax.axis_size("vel") - 1
    base = lax.axis_index("vel") * rows
    total = rows * lax.axis_size("vel")
    order = [jnp.where(negative, count - 1 - t, t) for t in range(count)]

    centre_copies = []
    for t, i in enumerate(order):
        pair = [
            pltpu.make_async_copy(density.at[i], pad.at[i, pl.ds(1, rows)], load.at[2 * t]),
            pltpu.make_async_copy(control.at[i], ctl.at[i, pl.ds(1, rows)], load.at[2 * t + 1]),
        ]
        start_all(pair)
        centre_copies.append(pair)
    waits = []
    fields = ((density, low.at[1], high.at[1], pad), (control, low_now, high_now, ctl))
    for k, (field, below, above, padded) in enumerate(fields):
        for outer, own, far, place, sem in (
            (first, field.at[:, 0], below, 0, edge.at[2 * k]),
            (last, field.at[:, rows - 1], above, rows + 1, edge.at[2 * k + 1]),
        ):
            own_copy = pltpu.make_async_copy(own, padded.at[:, place], sem)
            far_copy = pltpu.make_async_copy(far, padded.at[:, place], sem)
            pl.when(outer)(own_copy.start)
            pl.when(jnp.logical_not(outer))(far_copy.start)
            waits.append(far_copy)
    wait_all(waits)

    stores = []
    for t, i in enumerate(order):
        wait_all(centre_copies[t])

        def step(a, carry, t=t, i=i):
            steep = slant(base + a, total)
            for at in range(0, second, SUB):
                here, up_w, dn_w = second_tile(pad, (i, a + 1), at, second)
                ctl_here, ctl_up_w, ctl_dn_w = second_tile(ctl, (i, a + 1), at, second)
                up_v = pad[i, a + 2, pl.ds(at, SUB), :]
                dn_v = pad[i, a, pl.ds(at, SUB), :]
                y_near = pltpu.roll(here, width - 1 if at < second // 2 else 1, 1)
                index = at + lax.broadcasted_iota(jnp.int32, here.shape, 0)
                if t == 0:
                    along_x = -steep * here
                else:
                    along_x = steep * (pad[order[t - 1], a + 1, pl.ds(at, SUB), :] - here)
                speed_up = -CONTROL_COST * (ctl[i, a + 2, pl.ds(at, SUB), :] - ctl_here)
                speed_dn = -CONTROL_COST * (ctl_here - ctl[i, a, pl.ds(at, SUB), :])
                flux_up = jnp.maximum(speed_up, 0.0) * here + jnp.minimum(speed_up, 0.0) * up_v
                flux_dn = jnp.maximum(speed_dn, 0.0) * dn_v + jnp.minimum(speed_dn, 0.0) * here
                side_up = -CONTROL_COST * (ctl_up_w - ctl_here)
                side_dn = -CONTROL_COST * (ctl_here - ctl_dn_w)
                flux_right = jnp.maximum(side_up, 0.0) * here + jnp.minimum(side_up, 0.0) * up_w
                flux_left = jnp.maximum(side_dn, 0.0) * dn_w + jnp.minimum(side_dn, 0.0) * here
                spread = up_v + dn_v - 2.0 * here + up_w + dn_w - 2.0 * here
                fresh[i, a, pl.ds(at, SUB), :] = (
                    here
                    + along_x
                    + slant(index, second) * (y_near - here)
                    - (flux_up - flux_dn)
                    - (flux_right - flux_left)
                    + VISCOSITY * spread
                )
            return carry

        lax.fori_loop(0, rows, step, 0)
        stores.append(pltpu.make_async_copy(fresh.at[i], out.at[i], store.at[t]))
        stores[-1].start()
        if t == 0:
            extent = rest.shape[0]
            rest[...] = fresh[i, pl.ds(rows - extent, extent)]
    wait_all(stores)


def density_step(density, control, low, high, low_now, high_now, extent):
    count, rows, second, width = density.shape
    cells = count * rows * second * width
    padded = pltpu.VMEM((count, rows + 2, second, width), density.dtype)
    return pl.pallas_call(
        density_kernel,
        out_shape=[
            jax.ShapeDtypeStruct(density.shape, density.dtype),
            pltpu.VMEM((extent, second, width), density.dtype),
        ],
        in_specs=[ANY] * 6,
        out_specs=[ANY, VMEM],
        scratch_shapes=[
            padded,
            padded,
            pltpu.VMEM(density.shape, density.dtype),
            pltpu.SemaphoreType.DMA((2 * count,)),
            pltpu.SemaphoreType.DMA((4,)),
            pltpu.SemaphoreType.DMA((count,)),
        ],
        compiler_params=pltpu.CompilerParams(vmem_limit_bytes=VMEM_LIMIT),
        cost_estimate=pl.CostEstimate(
            flops=60 * cells, transcendentals=0, bytes_accessed=12 * cells
        ),
        name="density_step",
    )(in_hbm(density), in_hbm(control), low, high, low_now, high_now)


def arrive_kernel(begin, partial, halo, out, held, near, sems):
    count, rows = partial.shape[:2]
    extent, second = halo.shape[:2]
    row = jnp.where(is_negative(), count - 1, 0)
    base = lax.axis_index("vel") * rows + begin
    total = rows * lax.axis_size("vel")
    loads = []
    for a in range(extent):
        loads.append(pltpu.make_async_copy(partial.at[row, begin + a], held.at[a], sems.at[a]))
        loads.append(pltpu.make_async_copy(halo.at[a], near.at[a], sems.at[extent + a]))
    start_all(loads)
    stores = []
    for a in range(extent):
        wait_all(loads[2 * a : 2 * a + 2])
        held[a] = held[a] + slant(base + a, total) * near[a]
        stores.append(pltpu.make_async_copy(held.at[a], out.at[row, begin + a], sems.at[2 * extent + a]))
        stores[-1].start()
    wait_all(stores)


def arrive(partial, halo, begin):
    block = pltpu.VMEM(halo.shape, halo.dtype)
    return pl.pallas_call(
        functools.partial(arrive_kernel, begin),
        out_shape=jax.ShapeDtypeStruct(partial.shape, partial.dtype),
        in_specs=[ANY, ANY],
        out_specs=ANY,
        scratch_shapes=[block, block, pltpu.SemaphoreType.DMA((3 * halo.shape[0],))],
        input_output_aliases={0: 0},
        compiler_params=pltpu.CompilerParams(vmem_limit_bytes=VMEM_LIMIT),
        cost_estimate=pl.CostEstimate(
            flops=2 * halo.size, transcendentals=0, bytes_accessed=12 * halo.size
        ),
        name="arrive",
    )(in_hbm(partial), halo)


def arrive_last_kernel(partial, rest, halo, out, held, sem):
    count, rows = partial.shape[:2]
    extent = halo.shape[0]
    row = jnp.where(is_negative(), count - 1, 0)
    base = lax.axis_index("vel") * rows + rows - extent
    total = rows * lax.axis_size("vel")
    copies = []
    for a in range(extent):
        held[a] = rest[a] + slant(base + a, total) * halo[a]
        copies.append(pltpu.make_async_copy(held.at[a], out.at[row, rows - extent + a], sem.at[a]))
        copies[-1].start()
    wait_all(copies)


def arrive_last(partial, rest, halo):
    return pl.pallas_call(
        arrive_last_kernel,
        out_shape=jax.ShapeDtypeStruct(partial.shape, partial.dtype),
        in_specs=[ANY, VMEM, VMEM],
        out_specs=ANY,
        scratch_shapes=[pltpu.VMEM(halo.shape, halo.dtype), pltpu.SemaphoreType.DMA((halo.shape[0],))],
        input_output_aliases={0: 0},
        compiler_params=pltpu.CompilerParams(vmem_limit_bytes=VMEM_LIMIT),
        cost_estimate=pl.CostEstimate(
            flops=2 * halo.size, transcendentals=0, bytes_accessed=8 * halo.size
        ),
        name="arrive_last",
    )(in_hbm(partial), in_vmem(rest), in_vmem(halo))


def routes(mesh):
    names = tuple(mesh.axis_names)
    sizes = [mesh.shape[name] for name in names]
    slabs, groups = mesh.shape["pos"], mesh.shape["vel"]

    def place(pos, vel):
        at = {"pos": pos % slabs, "vel": vel}
        index = 0
        for name, size in zip(names, sizes):
            index = index * size + at[name]
        return index

    value_route, density_route = [], []
    for pos in range(slabs):
        for vel in range(groups):
            onward = 1 if vel < groups // 2 else -1
            value_route.append((place(pos, vel), place(pos + onward, vel)))
            density_route.append((place(pos, vel), place(pos - onward, vel)))
    return names, value_route, density_route


def body(mesh, value_next, density):
    names, value_route, density_route = routes(mesh)
    groups = mesh.shape["vel"]
    count, rows, second, width = value_next.shape
    tail = max(1, rows // 8)
    cuts = ((0, rows - tail), (rows - tail, rows))
    onward = [(v, v + 1) for v in range(groups - 1)]
    back = [(v + 1, v) for v in range(groups - 1)]

    value_halos = [lax.ppermute(value_rows(value_next, 0, rows), names, value_route)]
    low, high, *leaving = edges(value_next, density, cuts)
    low = lax.ppermute(low, "vel", onward)
    high = lax.ppermute(high, "vel", back)
    mass = lax.psum(jnp.sum(density, axis=(1, 2)), "vel") / (second * second)
    crowding = CROWDING * mass * mass

    held = (*leaving, *value_halos, crowding, low, high)
    *leaving, value_halo, crowding, low, high = lax.optimization_barrier(held)
    value_halos = [value_halo]
    density_halos = [lax.ppermute(part, names, density_route) for part in leaving]

    value_now, low_now, high_now = value_step(value_next, low, high, crowding, value_halos)
    low_now = lax.ppermute(low_now, "vel", onward)
    high_now = lax.ppermute(high_now, "vel", back)
    density_next, rest = density_step(
        density, value_now, low, high, low_now, high_now, tail
    )
    density_next = arrive(density_next, density_halos[0], 0)
    density_next = arrive_last(density_next, rest, density_halos[1])
    return value_now, density_next


def solution(mesh):
    placed = (P("pos", "vel", None, None), P("pos", "vel", None, None))
    return jax.shard_map(
        functools.partial(body, mesh),
        mesh=mesh,
        in_specs=placed,
        out_specs=placed,
        check_vma=False,
    )
```

```python
import functools

import jax
import jax.numpy as jnp
from jax import lax
from jax.experimental import pallas as pl
from jax.experimental.pallas import tpu as pltpu
from jax.sharding import PartitionSpec as P

COURANT = 0.4
CONTROL_COST = 0.25
VISCOSITY = 0.15
CROWDING = 0.3

SUB = 8
VMEM_LIMIT = 18 * 1024 * 1024
ANY = pl.BlockSpec(memory_space=pl.ANY)
VMEM = pl.BlockSpec(memory_space=pltpu.VMEM)
LIGHT = pl.CostEstimate(flops=0, transcendentals=0, bytes_accessed=0)


def is_negative():
    return lax.axis_index("vel") < lax.axis_size("vel") // 2


def slant(first, total):
    return COURANT * (jnp.abs(first.astype(jnp.float32) + 0.5 - total / 2) / (total / 2))


def start_all(copies):
    for copy in copies:
        copy.start()


def wait_all(copies):
    for copy in copies:
        copy.wait()


def in_hbm(array):
    return pltpu.with_memory_space_constraint(array, pltpu.HBM)


def in_vmem(array):
    return pltpu.with_memory_space_constraint(array, pltpu.VMEM)


def relay(pairs, held, load, store):
    inward = [
        pltpu.make_async_copy(source, held.at[k], load.at[k]) for k, (source, _) in enumerate(pairs)
    ]
    outward = [
        pltpu.make_async_copy(held.at[k], target, store.at[k]) for k, (_, target) in enumerate(pairs)
    ]
    start_all(inward)
    for come, go in zip(inward, outward):
        come.wait()
        go.start()
    wait_all(outward)


def relay_scratch(slots, second, width, dtype):
    sems = pltpu.SemaphoreType.DMA((slots,))
    return [pltpu.VMEM((slots, second, width), dtype), sems, sems]


def leaving_rows(field, row, cuts, sent):
    return [
        (field.at[row, a], target.at[a - begin])
        for (begin, end), target in zip(cuts, sent)
        for a in range(begin, end)
    ]


def value_rows_kernel(begin, end, value, sent, *scratch):
    row = jnp.where(is_negative(), value.shape[0] - 1, 0)
    relay(leaving_rows(value, row, ((begin, end),), (sent,)), *scratch)


def value_rows(value, begin, end):
    shape = (end - begin,) + value.shape[2:]
    sent = pltpu.HBM(shape, value.dtype)
    return pl.pallas_call(
        functools.partial(value_rows_kernel, begin, end),
        out_shape=sent,
        in_specs=[ANY],
        out_specs=ANY,
        scratch_shapes=relay_scratch(*shape, value.dtype),
        compiler_params=pltpu.CompilerParams(vmem_limit_bytes=VMEM_LIMIT),
        cost_estimate=LIGHT,
        name="value_rows",
    )(in_hbm(value))


def edges_kernel(cuts, value, density, low, high, *rest):
    count, rows = value.shape[:2]
    row = jnp.where(is_negative(), 0, count - 1)
    pairs = []
    for k, field in enumerate((value, density)):
        for i in range(count):
            pairs.append((field.at[i, rows - 1], low.at[k, i]))
            pairs.append((field.at[i, 0], high.at[k, i]))
    pairs += leaving_rows(density, row, cuts, rest[: len(cuts)])
    relay(pairs, *rest[len(cuts) :])


def edges(value, density, cuts):
    count, rows, second, width = value.shape
    edge = pltpu.HBM((2, count, second, width), value.dtype)
    parts = [pltpu.HBM((e - b, second, width), value.dtype) for b, e in cuts]
    return pl.pallas_call(
        functools.partial(edges_kernel, cuts),
        out_shape=[edge, edge, *parts],
        in_specs=[ANY, ANY],
        out_specs=[ANY] * (2 + len(cuts)),
        scratch_shapes=relay_scratch(4 * count + rows, second, width, value.dtype),
        compiler_params=pltpu.CompilerParams(vmem_limit_bytes=VMEM_LIMIT),
        cost_estimate=LIGHT,
        name="edges",
    )(in_hbm(value), in_hbm(density))


def second_tile(ref, index, at, total):
    here = ref[*index, pl.ds(at, SUB), :]
    place = lax.broadcasted_iota(jnp.int32, here.shape, 0)
    if at + SUB < total:
        above = ref[*index, pl.ds(at + 1, SUB), :]
    else:
        above = jnp.where(place == SUB - 1, here, pltpu.roll(here, SUB - 1, 0))
    if at > 0:
        below = ref[*index, pl.ds(at - 1, SUB), :]
    else:
        below = jnp.where(place == 0, here, pltpu.roll(here, 1, 0))
    return here, above, below


def value_kernel(value, low, high, crowding, *rest):
    parts = len(rest) - 9
    halos = rest[:parts]
    value_now, low_now, high_now, pad, halo, fresh, load, edge, store = rest[parts:]
    count, rows, second, width = value.shape
    negative = is_negative()
    first = lax.axis_index("vel") == 0
    last = lax.axis_index("vel") == lax.axis_size("vel") - 1
    base = lax.axis_index("vel") * rows
    total = rows * lax.axis_size("vel")
    order = [jnp.where(negative, t, count - 1 - t) for t in range(count)]

    begin = 0
    halo_copies = []
    for k, part in enumerate(halos):
        extent = part.shape[0]
        halo_copies.append(
            pltpu.make_async_copy(part, halo.at[pl.ds(begin, extent)], load.at[count + k])
        )
        begin += extent
    start_all(halo_copies)
    centre_copies = [
        pltpu.make_async_copy(value.at[i], pad.at[i, pl.ds(1, rows)], load.at[t])
        for t, i in enumerate(order)
    ]
    start_all(centre_copies)
    below_own = pltpu.make_async_copy(value.at[:, 0], pad.at[:, 0], edge.at[0])
    below_far = pltpu.make_async_copy(low.at[0], pad.at[:, 0], edge.at[0])
    above_own = pltpu.make_async_copy(value.at[:, rows - 1], pad.at[:, rows + 1], edge.at[1])
    above_far = pltpu.make_async_copy(high.at[0], pad.at[:, rows + 1], edge.at[1])
    pl.when(first)(below_own.start)
    pl.when(jnp.logical_not(first))(below_far.start)
    pl.when(last)(above_own.start)
    pl.when(jnp.logical_not(last))(above_far.start)
    below_far.wait()
    above_far.wait()
    wait_all(halo_copies)

    stores = []
    for t, i in enumerate(order):
        centre_copies[t].wait()

        def step(a, carry, t=t, i=i):
            steep = slant(base + a, total)
            for at in range(0, second, SUB):
                here, up_w, dn_w = second_tile(pad, (i, a + 1), at, second)
                if t == 0:
                    x_near = halo[a, pl.ds(at, SUB), :]
                else:
                    x_near = pad[order[t - 1], a + 1, pl.ds(at, SUB), :]
                y_near = pltpu.roll(here, 1 if at < second // 2 else width - 1, 1)
                index = at + lax.broadcasted_iota(jnp.int32, here.shape, 0)
                up_v = pad[i, a + 2, pl.ds(at, SUB), :] - here
                dn_v = here - pad[i, a, pl.ds(at, SUB), :]
                up_w = up_w - here
                dn_w = here - dn_w
                hamilton = (
                    jnp.square(jnp.maximum(dn_v, 0.0))
                    + jnp.square(jnp.minimum(up_v, 0.0))
                    + jnp.square(jnp.maximum(dn_w, 0.0))
                    + jnp.square(jnp.minimum(up_w, 0.0))
                )
                laplace = up_v - dn_v + up_w - dn_w
                fresh[i, a, pl.ds(at, SUB), :] = (
                    here
                    + steep * (x_near - here)
                    + slant(index, second) * (y_near - here)
                    - (0.5 * CONTROL_COST) * hamilton
                    + VISCOSITY * laplace
                    + crowding[pl.ds(i, 1), :]
                )
            return carry

        lax.fori_loop(0, rows, step, 0)
        stores.append(pltpu.make_async_copy(fresh.at[i], value_now.at[i], store.at[t]))
        stores[-1].start()
    stores.append(pltpu.make_async_copy(fresh.at[:, rows - 1], low_now, store.at[count]))
    stores.append(pltpu.make_async_copy(fresh.at[:, 0], high_now, store.at[count + 1]))
    start_all(stores[count:])
    wait_all(stores)


def value_step(value, low, high, crowding, halos):
    count, rows, second, width = value.shape
    cells = count * rows * second * width
    edge = jax.ShapeDtypeStruct((count, second, width), value.dtype)
    return pl.pallas_call(
        value_kernel,
        out_shape=[jax.ShapeDtypeStruct(value.shape, value.dtype), edge, edge],
        in_specs=[ANY, ANY, ANY, VMEM] + [ANY] * len(halos),
        out_specs=[ANY] * 3,
        scratch_shapes=[
            pltpu.VMEM((count, rows + 2, second, width), value.dtype),
            pltpu.VMEM((rows, second, width), value.dtype),
            pltpu.VMEM(value.shape, value.dtype),
            pltpu.SemaphoreType.DMA((count + len(halos),)),
            pltpu.SemaphoreType.DMA((2,)),
            pltpu.SemaphoreType.DMA((count + 2,)),
        ],
        compiler_params=pltpu.CompilerParams(vmem_limit_bytes=VMEM_LIMIT),
        cost_estimate=LIGHT,
        name="value_step",
    )(in_hbm(value), low, high, crowding, *halos)


def density_kernel(
    density, control, low, high, low_now, high_now, out, rest, pad, ctl, fresh, load, edge, store
):
    count, rows, second, width = density.shape
    negative = is_negative()
    first = lax.axis_index("vel") == 0
    last = lax.axis_index("vel") == lax.axis_size("vel") - 1
    base = lax.axis_index("vel") * rows
    total = rows * lax.axis_size("vel")
    order = [jnp.where(negative, count - 1 - t, t) for t in range(count)]

    centre_copies = []
    for t, i in enumerate(order):
        pair = [
            pltpu.make_async_copy(density.at[i], pad.at[i, pl.ds(1, rows)], load.at[2 * t]),
            pltpu.make_async_copy(control.at[i], ctl.at[i, pl.ds(1, rows)], load.at[2 * t + 1]),
        ]
        start_all(pair)
        centre_copies.append(pair)
    waits = []
    fields = ((density, low.at[1], high.at[1], pad), (control, low_now, high_now, ctl))
    for k, (field, below, above, padded) in enumerate(fields):
        for outer, own, far, place, sem in (
            (first, field.at[:, 0], below, 0, edge.at[2 * k]),
            (last, field.at[:, rows - 1], above, rows + 1, edge.at[2 * k + 1]),
        ):
            own_copy = pltpu.make_async_copy(own, padded.at[:, place], sem)
            far_copy = pltpu.make_async_copy(far, padded.at[:, place], sem)
            pl.when(outer)(own_copy.start)
            pl.when(jnp.logical_not(outer))(far_copy.start)
            waits.append(far_copy)
    wait_all(waits)

    stores = []
    for t, i in enumerate(order):
        wait_all(centre_copies[t])

        def step(a, carry, t=t, i=i):
            steep = slant(base + a, total)
            for at in range(0, second, SUB):
                here, up_w, dn_w = second_tile(pad, (i, a + 1), at, second)
                ctl_here, ctl_up_w, ctl_dn_w = second_tile(ctl, (i, a + 1), at, second)
                up_v = pad[i, a + 2, pl.ds(at, SUB), :]
                dn_v = pad[i, a, pl.ds(at, SUB), :]
                y_near = pltpu.roll(here, width - 1 if at < second // 2 else 1, 1)
                index = at + lax.broadcasted_iota(jnp.int32, here.shape, 0)
                if t == 0:
                    along_x = -steep * here
                else:
                    along_x = steep * (pad[order[t - 1], a + 1, pl.ds(at, SUB), :] - here)
                speed_up = -CONTROL_COST * (ctl[i, a + 2, pl.ds(at, SUB), :] - ctl_here)
                speed_dn = -CONTROL_COST * (ctl_here - ctl[i, a, pl.ds(at, SUB), :])
                flux_up = jnp.maximum(speed_up, 0.0) * here + jnp.minimum(speed_up, 0.0) * up_v
                flux_dn = jnp.maximum(speed_dn, 0.0) * dn_v + jnp.minimum(speed_dn, 0.0) * here
                side_up = -CONTROL_COST * (ctl_up_w - ctl_here)
                side_dn = -CONTROL_COST * (ctl_here - ctl_dn_w)
                flux_right = jnp.maximum(side_up, 0.0) * here + jnp.minimum(side_up, 0.0) * up_w
                flux_left = jnp.maximum(side_dn, 0.0) * dn_w + jnp.minimum(side_dn, 0.0) * here
                spread = up_v + dn_v - 2.0 * here + up_w + dn_w - 2.0 * here
                fresh[i, a, pl.ds(at, SUB), :] = (
                    here
                    + along_x
                    + slant(index, second) * (y_near - here)
                    - (flux_up - flux_dn)
                    - (flux_right - flux_left)
                    + VISCOSITY * spread
                )
            return carry

        lax.fori_loop(0, rows, step, 0)
        stores.append(pltpu.make_async_copy(fresh.at[i], out.at[i], store.at[t]))
        stores[-1].start()
        if t == 0:
            extent = rest.shape[0]
            rest[...] = fresh[i, pl.ds(rows - extent, extent)]
    wait_all(stores)


def density_step(density, control, low, high, low_now, high_now, extent):
    count, rows, second, width = density.shape
    cells = count * rows * second * width
    padded = pltpu.VMEM((count, rows + 2, second, width), density.dtype)
    return pl.pallas_call(
        density_kernel,
        out_shape=[
            jax.ShapeDtypeStruct(density.shape, density.dtype),
            pltpu.VMEM((extent, second, width), density.dtype),
        ],
        in_specs=[ANY] * 6,
        out_specs=[ANY, VMEM],
        scratch_shapes=[
            padded,
            padded,
            pltpu.VMEM(density.shape, density.dtype),
            pltpu.SemaphoreType.DMA((2 * count,)),
            pltpu.SemaphoreType.DMA((4,)),
            pltpu.SemaphoreType.DMA((count,)),
        ],
        compiler_params=pltpu.CompilerParams(vmem_limit_bytes=VMEM_LIMIT),
        cost_estimate=LIGHT,
        name="density_step",
    )(in_hbm(density), in_hbm(control), low, high, low_now, high_now)


def arrive_kernel(partial, *refs):
    halos, (out, held, near, load, store) = refs[:-5], refs[-5:]
    count, rows = partial.shape[:2]
    row = jnp.where(is_negative(), count - 1, 0)
    base = lax.axis_index("vel") * rows
    total = rows * lax.axis_size("vel")
    loads = []
    for halo in halos:
        for k in range(halo.shape[0]):
            a = len(loads)
            pair = [
                pltpu.make_async_copy(partial.at[row, a], held.at[a], load.at[2 * a]),
                pltpu.make_async_copy(halo.at[k], near.at[a], load.at[2 * a + 1]),
            ]
            start_all(pair)
            loads.append(pair)
    stores = []
    for a, pair in enumerate(loads):
        wait_all(pair)
        held[a] = held[a] + slant(base + a, total) * near[a]
        stores.append(pltpu.make_async_copy(held.at[a], out.at[row, a], store.at[a]))
        stores[-1].start()
    wait_all(stores)


def arrive(partial, halos):
    extent = sum(halo.shape[0] for halo in halos)
    block = pltpu.VMEM((extent,) + partial.shape[2:], partial.dtype)
    return pl.pallas_call(
        arrive_kernel,
        out_shape=jax.ShapeDtypeStruct(partial.shape, partial.dtype),
        in_specs=[ANY] * (1 + len(halos)),
        out_specs=ANY,
        scratch_shapes=[
            block,
            block,
            pltpu.SemaphoreType.DMA((2 * extent,)),
            pltpu.SemaphoreType.DMA((extent,)),
        ],
        input_output_aliases={0: 0},
        compiler_params=pltpu.CompilerParams(vmem_limit_bytes=VMEM_LIMIT),
        cost_estimate=LIGHT,
        name="arrive",
    )(in_hbm(partial), *halos)


def arrive_last_kernel(partial, rest, *refs):
    halos, (out, held, sems) = refs[:-3], refs[-3:]
    count, rows = partial.shape[:2]
    extent = rest.shape[0]
    row = jnp.where(is_negative(), count - 1, 0)
    base = lax.axis_index("vel") * rows + rows - extent
    total = rows * lax.axis_size("vel")
    copies = []
    for halo in halos:
        for k in range(halo.shape[0]):
            a = len(copies)
            held[a] = rest[a] + slant(base + a, total) * halo[k]
            target = out.at[row, rows - extent + a]
            copies.append(pltpu.make_async_copy(held.at[a], target, sems.at[a]))
            copies[-1].start()
    wait_all(copies)


def arrive_last(partial, rest, halos):
    return pl.pallas_call(
        arrive_last_kernel,
        out_shape=jax.ShapeDtypeStruct(partial.shape, partial.dtype),
        in_specs=[ANY] + [VMEM] * (1 + len(halos)),
        out_specs=ANY,
        scratch_shapes=[
            pltpu.VMEM(rest.shape, rest.dtype),
            pltpu.SemaphoreType.DMA((rest.shape[0],)),
        ],
        input_output_aliases={0: 0},
        compiler_params=pltpu.CompilerParams(vmem_limit_bytes=VMEM_LIMIT),
        cost_estimate=LIGHT,
        name="arrive_last",
    )(in_hbm(partial), in_vmem(rest), *[in_vmem(halo) for halo in halos])


def routes(mesh):
    names = tuple(mesh.axis_names)
    sizes = [mesh.shape[name] for name in names]
    slabs, groups = mesh.shape["pos"], mesh.shape["vel"]

    def place(pos, vel):
        at = {"pos": pos % slabs, "vel": vel}
        index = 0
        for name, size in zip(names, sizes):
            index = index * size + at[name]
        return index

    value_route, density_route, over_route, swap_route = [], [], [], []
    for pos in range(slabs):
        for vel in range(groups):
            onward = 1 if vel < groups // 2 else -1
            value_route.append((place(pos, vel), place(pos + onward, vel)))
            density_route.append((place(pos, vel), place(pos - onward, vel)))
            leads = slabs % 2 == 0 and (pos % 2 == 0) == (onward > 0)
            over_route.append((place(pos, vel), place(pos - 2 * onward if leads else pos, vel)))
            swap_route.append((place(pos, vel), place(pos + onward if leads else pos - onward, vel)))
    return names, value_route, density_route, over_route, swap_route


def body(mesh, value_next, density):
    names, value_route, density_route, over_route, swap_route = routes(mesh)
    groups = mesh.shape["vel"]
    count, rows, second, width = value_next.shape
    tail = max(1, rows // 8)
    near = rows // 2 - tail - 1
    cuts = (
        (0, near),
        (near, rows - 2 * tail),
        (rows - 2 * tail, rows - tail),
        (rows - tail, rows),
    )
    onward = [(v, v + 1) for v in range(groups - 1)]
    back = [(v + 1, v) for v in range(groups - 1)]

    value_halo = lax.ppermute(value_rows(value_next, 0, rows), names, value_route)
    low, high, *parts = edges(value_next, density, cuts)
    fillers = [lax.ppermute(part, names, over_route) for part in parts[1::2]]
    low = lax.ppermute(low, "vel", onward)
    high = lax.ppermute(high, "vel", back)
    mass = lax.psum(jnp.sum(density, axis=(1, 2)), "vel") / (second * second)
    crowding = CROWDING * mass * mass

    held = (*parts[::2], value_halo, crowding, low, high, *fillers)
    *parts, value_halo, crowding, low, high = lax.optimization_barrier(held)[: -len(fillers)]
    fillers = [lax.ppermute(part, names, swap_route) for part in fillers]
    parts = [lax.ppermute(part, names, density_route) for part in parts]

    value_now, low_now, high_now = value_step(value_next, low, high, crowding, [value_halo])
    low_now = lax.ppermute(low_now, "vel", onward)
    high_now = lax.ppermute(high_now, "vel", back)
    density_next, rest = density_step(
        density, value_now, low, high, low_now, high_now, 2 * tail
    )
    density_next = arrive(density_next, (parts[0], fillers[0]))
    density_next = arrive_last(density_next, rest, (parts[1], fillers[1]))
    return value_now, density_next


def solution(mesh):
    placed = (P("pos", "vel", None, None), P("pos", "vel", None, None))
    return jax.shard_map(
        functools.partial(body, mesh),
        mesh=mesh,
        in_specs=placed,
        out_specs=placed,
        check_vma=False,
    )
```

```python
import functools

import jax
import jax.numpy as jnp
from jax import lax
from jax.experimental import pallas as pl
from jax.experimental.pallas import tpu as pltpu
from jax.sharding import PartitionSpec as P

COURANT = 0.4
CONTROL_COST = 0.25
VISCOSITY = 0.15
CROWDING = 0.3

SUB = 8
VMEM_LIMIT = 18 * 1024 * 1024
ANY = pl.BlockSpec(memory_space=pl.ANY)
VMEM = pl.BlockSpec(memory_space=pltpu.VMEM)
LIGHT = pl.CostEstimate(flops=0, transcendentals=0, bytes_accessed=0)


def is_negative():
    return lax.axis_index("vel") < lax.axis_size("vel") // 2


def slant(first, total):
    return COURANT * (jnp.abs(first.astype(jnp.float32) + 0.5 - total / 2) / (total / 2))


def start_all(copies):
    for copy in copies:
        copy.start()


def wait_all(copies):
    for copy in copies:
        copy.wait()


def in_hbm(array):
    return pltpu.with_memory_space_constraint(array, pltpu.HBM)


def in_vmem(array):
    return pltpu.with_memory_space_constraint(array, pltpu.VMEM)


def relay(pairs, held, load, store):
    inward = [
        pltpu.make_async_copy(source, held.at[k], load.at[k]) for k, (source, _) in enumerate(pairs)
    ]
    outward = [
        pltpu.make_async_copy(held.at[k], target, store.at[k]) for k, (_, target) in enumerate(pairs)
    ]
    start_all(inward)
    for come, go in zip(inward, outward):
        come.wait()
        go.start()
    wait_all(outward)


def relay_scratch(slots, second, width, dtype):
    sems = pltpu.SemaphoreType.DMA((slots,))
    return [pltpu.VMEM((slots, second, width), dtype), sems, sems]


def leaving_rows(field, row, cuts, sent):
    return [
        (field.at[row, a], target.at[a - begin])
        for (begin, end), target in zip(cuts, sent)
        for a in range(begin, end)
    ]


def value_rows_kernel(begin, end, value, sent, sems):
    row = jnp.where(is_negative(), value.shape[0] - 1, 0)
    pairs = leaving_rows(value, row, ((begin, end),), (sent,))
    copies = [pltpu.make_async_copy(s, t, sems.at[k]) for k, (s, t) in enumerate(pairs)]
    start_all(copies)
    wait_all(copies)


def value_rows(value, begin, end):
    shape = (end - begin,) + value.shape[2:]
    return pl.pallas_call(
        functools.partial(value_rows_kernel, begin, end),
        out_shape=[pltpu.VMEM(shape, value.dtype)],
        in_specs=[ANY],
        out_specs=[VMEM],
        scratch_shapes=[pltpu.SemaphoreType.DMA((end - begin,))],
        compiler_params=pltpu.CompilerParams(vmem_limit_bytes=VMEM_LIMIT),
        cost_estimate=LIGHT,
        name="value_rows",
    )(in_hbm(value))[0]


def edges_kernel(cuts, value, density, low, high, *rest):
    count, rows = value.shape[:2]
    row = jnp.where(is_negative(), 0, count - 1)
    pairs = []
    for k, field in enumerate((value, density)):
        for i in range(count):
            pairs.append((field.at[i, rows - 1], low.at[k, i]))
            pairs.append((field.at[i, 0], high.at[k, i]))
    pairs += leaving_rows(density, row, cuts, rest[: len(cuts)])
    relay(pairs, *rest[len(cuts) :])


def edges(value, density, cuts):
    count, rows, second, width = value.shape
    edge = pltpu.HBM((2, count, second, width), value.dtype)
    parts = [pltpu.HBM((e - b, second, width), value.dtype) for b, e in cuts]
    return pl.pallas_call(
        functools.partial(edges_kernel, cuts),
        out_shape=[edge, edge, *parts],
        in_specs=[ANY, ANY],
        out_specs=[ANY] * (2 + len(cuts)),
        scratch_shapes=relay_scratch(4 * count + rows, second, width, value.dtype),
        compiler_params=pltpu.CompilerParams(vmem_limit_bytes=VMEM_LIMIT),
        cost_estimate=LIGHT,
        name="edges",
    )(in_hbm(value), in_hbm(density))


def second_tile(ref, index, at, total):
    here = ref[*index, pl.ds(at, SUB), :]
    place = lax.broadcasted_iota(jnp.int32, here.shape, 0)
    if at + SUB < total:
        above = ref[*index, pl.ds(at + 1, SUB), :]
    else:
        above = jnp.where(place == SUB - 1, here, pltpu.roll(here, SUB - 1, 0))
    if at > 0:
        below = ref[*index, pl.ds(at - 1, SUB), :]
    else:
        below = jnp.where(place == 0, here, pltpu.roll(here, 1, 0))
    return here, above, below


def value_kernel(value, low, high, crowding, *rest):
    parts = len(rest) - 9
    halos = rest[:parts]
    value_now, low_now, high_now, pad, halo, fresh, load, edge, store = rest[parts:]
    count, rows, second, width = value.shape
    negative = is_negative()
    first = lax.axis_index("vel") == 0
    last = lax.axis_index("vel") == lax.axis_size("vel") - 1
    base = lax.axis_index("vel") * rows
    total = rows * lax.axis_size("vel")
    order = [jnp.where(negative, t, count - 1 - t) for t in range(count)]

    begin = 0
    halo_copies = []
    for k, part in enumerate(halos):
        extent = part.shape[0]
        halo_copies.append(
            pltpu.make_async_copy(part, halo.at[pl.ds(begin, extent)], load.at[count + k])
        )
        begin += extent
    start_all(halo_copies)
    centre_copies = [
        pltpu.make_async_copy(value.at[i], pad.at[i, pl.ds(1, rows)], load.at[t])
        for t, i in enumerate(order)
    ]
    start_all(centre_copies)
    below_own = pltpu.make_async_copy(value.at[:, 0], pad.at[:, 0], edge.at[0])
    below_far = pltpu.make_async_copy(low.at[0], pad.at[:, 0], edge.at[0])
    above_own = pltpu.make_async_copy(value.at[:, rows - 1], pad.at[:, rows + 1], edge.at[1])
    above_far = pltpu.make_async_copy(high.at[0], pad.at[:, rows + 1], edge.at[1])
    pl.when(first)(below_own.start)
    pl.when(jnp.logical_not(first))(below_far.start)
    pl.when(last)(above_own.start)
    pl.when(jnp.logical_not(last))(above_far.start)
    below_far.wait()
    above_far.wait()
    wait_all(halo_copies)

    stores = []
    for t, i in enumerate(order):
        centre_copies[t].wait()

        def step(a, carry, t=t, i=i):
            steep = slant(base + a, total)
            for at in range(0, second, SUB):
                here, up_w, dn_w = second_tile(pad, (i, a + 1), at, second)
                if t == 0:
                    x_near = halo[a, pl.ds(at, SUB), :]
                else:
                    x_near = pad[order[t - 1], a + 1, pl.ds(at, SUB), :]
                y_near = pltpu.roll(here, 1 if at < second // 2 else width - 1, 1)
                index = at + lax.broadcasted_iota(jnp.int32, here.shape, 0)
                up_v = pad[i, a + 2, pl.ds(at, SUB), :] - here
                dn_v = here - pad[i, a, pl.ds(at, SUB), :]
                up_w = up_w - here
                dn_w = here - dn_w
                hamilton = (
                    jnp.square(jnp.maximum(dn_v, 0.0))
                    + jnp.square(jnp.minimum(up_v, 0.0))
                    + jnp.square(jnp.maximum(dn_w, 0.0))
                    + jnp.square(jnp.minimum(up_w, 0.0))
                )
                laplace = up_v - dn_v + up_w - dn_w
                fresh[i, a, pl.ds(at, SUB), :] = (
                    here
                    + steep * (x_near - here)
                    + slant(index, second) * (y_near - here)
                    - (0.5 * CONTROL_COST) * hamilton
                    + VISCOSITY * laplace
                    + crowding[pl.ds(i, 1), :]
                )
            return carry

        lax.fori_loop(0, rows, step, 0)
        stores.append(pltpu.make_async_copy(fresh.at[i], value_now.at[i], store.at[t]))
        stores[-1].start()
    stores.append(pltpu.make_async_copy(fresh.at[:, rows - 1], low_now, store.at[count]))
    stores.append(pltpu.make_async_copy(fresh.at[:, 0], high_now, store.at[count + 1]))
    start_all(stores[count:])
    wait_all(stores)


def value_step(value, low, high, crowding, halos):
    count, rows, second, width = value.shape
    cells = count * rows * second * width
    edge = jax.ShapeDtypeStruct((count, second, width), value.dtype)
    return pl.pallas_call(
        value_kernel,
        out_shape=[jax.ShapeDtypeStruct(value.shape, value.dtype), edge, edge],
        in_specs=[ANY, ANY, ANY, VMEM] + [ANY] * len(halos),
        out_specs=[ANY] * 3,
        scratch_shapes=[
            pltpu.VMEM((count, rows + 2, second, width), value.dtype),
            pltpu.VMEM((rows, second, width), value.dtype),
            pltpu.VMEM(value.shape, value.dtype),
            pltpu.SemaphoreType.DMA((count + len(halos),)),
            pltpu.SemaphoreType.DMA((2,)),
            pltpu.SemaphoreType.DMA((count + 2,)),
        ],
        compiler_params=pltpu.CompilerParams(vmem_limit_bytes=VMEM_LIMIT),
        cost_estimate=LIGHT,
        name="value_step",
    )(in_hbm(value), low, high, crowding, *halos)


def density_kernel(
    density, control, low, high, low_now, high_now, out, rest, pad, ctl, fresh, load, edge, store
):
    count, rows, second, width = density.shape
    negative = is_negative()
    first = lax.axis_index("vel") == 0
    last = lax.axis_index("vel") == lax.axis_size("vel") - 1
    base = lax.axis_index("vel") * rows
    total = rows * lax.axis_size("vel")
    order = [jnp.where(negative, count - 1 - t, t) for t in range(count)]

    centre_copies = []
    for t, i in enumerate(order):
        pair = [
            pltpu.make_async_copy(density.at[i], pad.at[i, pl.ds(1, rows)], load.at[2 * t]),
            pltpu.make_async_copy(control.at[i], ctl.at[i, pl.ds(1, rows)], load.at[2 * t + 1]),
        ]
        start_all(pair)
        centre_copies.append(pair)
    waits = []
    fields = ((density, low.at[1], high.at[1], pad), (control, low_now, high_now, ctl))
    for k, (field, below, above, padded) in enumerate(fields):
        for outer, own, far, place, sem in (
            (first, field.at[:, 0], below, 0, edge.at[2 * k]),
            (last, field.at[:, rows - 1], above, rows + 1, edge.at[2 * k + 1]),
        ):
            own_copy = pltpu.make_async_copy(own, padded.at[:, place], sem)
            far_copy = pltpu.make_async_copy(far, padded.at[:, place], sem)
            pl.when(outer)(own_copy.start)
            pl.when(jnp.logical_not(outer))(far_copy.start)
            waits.append(far_copy)
    wait_all(waits)

    stores = []
    for t, i in enumerate(order):
        wait_all(centre_copies[t])

        def step(a, carry, t=t, i=i):
            steep = slant(base + a, total)
            for at in range(0, second, SUB):
                here, up_w, dn_w = second_tile(pad, (i, a + 1), at, second)
                ctl_here, ctl_up_w, ctl_dn_w = second_tile(ctl, (i, a + 1), at, second)
                up_v = pad[i, a + 2, pl.ds(at, SUB), :]
                dn_v = pad[i, a, pl.ds(at, SUB), :]
                y_near = pltpu.roll(here, width - 1 if at < second // 2 else 1, 1)
                index = at + lax.broadcasted_iota(jnp.int32, here.shape, 0)
                if t == 0:
                    along_x = -steep * here
                else:
                    along_x = steep * (pad[order[t - 1], a + 1, pl.ds(at, SUB), :] - here)
                speed_up = -CONTROL_COST * (ctl[i, a + 2, pl.ds(at, SUB), :] - ctl_here)
                speed_dn = -CONTROL_COST * (ctl_here - ctl[i, a, pl.ds(at, SUB), :])
                flux_up = jnp.maximum(speed_up, 0.0) * here + jnp.minimum(speed_up, 0.0) * up_v
                flux_dn = jnp.maximum(speed_dn, 0.0) * dn_v + jnp.minimum(speed_dn, 0.0) * here
                side_up = -CONTROL_COST * (ctl_up_w - ctl_here)
                side_dn = -CONTROL_COST * (ctl_here - ctl_dn_w)
                flux_right = jnp.maximum(side_up, 0.0) * here + jnp.minimum(side_up, 0.0) * up_w
                flux_left = jnp.maximum(side_dn, 0.0) * dn_w + jnp.minimum(side_dn, 0.0) * here
                spread = up_v + dn_v - 2.0 * here + up_w + dn_w - 2.0 * here
                fresh[i, a, pl.ds(at, SUB), :] = (
                    here
                    + along_x
                    + slant(index, second) * (y_near - here)
                    - (flux_up - flux_dn)
                    - (flux_right - flux_left)
                    + VISCOSITY * spread
                )
            return carry

        lax.fori_loop(0, rows, step, 0)
        stores.append(pltpu.make_async_copy(fresh.at[i], out.at[i], store.at[t]))
        stores[-1].start()
        if t == 0:
            extent = rest.shape[0]
            rest[...] = fresh[i, pl.ds(rows - extent, extent)]
    wait_all(stores)


def density_step(density, control, low, high, low_now, high_now, extent):
    count, rows, second, width = density.shape
    cells = count * rows * second * width
    padded = pltpu.VMEM((count, rows + 2, second, width), density.dtype)
    return pl.pallas_call(
        density_kernel,
        out_shape=[
            jax.ShapeDtypeStruct(density.shape, density.dtype),
            pltpu.VMEM((extent, second, width), density.dtype),
        ],
        in_specs=[ANY] * 6,
        out_specs=[ANY, VMEM],
        scratch_shapes=[
            padded,
            padded,
            pltpu.VMEM(density.shape, density.dtype),
            pltpu.SemaphoreType.DMA((2 * count,)),
            pltpu.SemaphoreType.DMA((4,)),
            pltpu.SemaphoreType.DMA((count,)),
        ],
        compiler_params=pltpu.CompilerParams(vmem_limit_bytes=VMEM_LIMIT),
        cost_estimate=LIGHT,
        name="density_step",
    )(in_hbm(density), in_hbm(control), low, high, low_now, high_now)


def arrive_kernel(partial, *refs):
    halos, (out, held, near, load, store) = refs[:-5], refs[-5:]
    count, rows = partial.shape[:2]
    row = jnp.where(is_negative(), count - 1, 0)
    base = lax.axis_index("vel") * rows
    total = rows * lax.axis_size("vel")
    loads = []
    for halo in halos:
        for k in range(halo.shape[0]):
            a = len(loads)
            pair = [
                pltpu.make_async_copy(partial.at[row, a], held.at[a], load.at[2 * a]),
                pltpu.make_async_copy(halo.at[k], near.at[a], load.at[2 * a + 1]),
            ]
            start_all(pair)
            loads.append(pair)
    stores = []
    for a, pair in enumerate(loads):
        wait_all(pair)
        held[a] = held[a] + slant(base + a, total) * near[a]
        stores.append(pltpu.make_async_copy(held.at[a], out.at[row, a], store.at[a]))
        stores[-1].start()
    wait_all(stores)


def arrive(partial, halos):
    extent = sum(halo.shape[0] for halo in halos)
    block = pltpu.VMEM((extent,) + partial.shape[2:], partial.dtype)
    return pl.pallas_call(
        arrive_kernel,
        out_shape=jax.ShapeDtypeStruct(partial.shape, partial.dtype),
        in_specs=[ANY] * (1 + len(halos)),
        out_specs=ANY,
        scratch_shapes=[
            block,
            block,
            pltpu.SemaphoreType.DMA((2 * extent,)),
            pltpu.SemaphoreType.DMA((extent,)),
        ],
        input_output_aliases={0: 0},
        compiler_params=pltpu.CompilerParams(vmem_limit_bytes=VMEM_LIMIT),
        cost_estimate=LIGHT,
        name="arrive",
    )(in_hbm(partial), *halos)


def arrive_last_kernel(partial, rest, *refs):
    halos, (out, held, sems) = refs[:-3], refs[-3:]
    count, rows = partial.shape[:2]
    extent = rest.shape[0]
    row = jnp.where(is_negative(), count - 1, 0)
    base = lax.axis_index("vel") * rows + rows - extent
    total = rows * lax.axis_size("vel")
    copies = []
    for halo in halos:
        for k in range(halo.shape[0]):
            a = len(copies)
            held[a] = rest[a] + slant(base + a, total) * halo[k]
            target = out.at[row, rows - extent + a]
            copies.append(pltpu.make_async_copy(held.at[a], target, sems.at[a]))
            copies[-1].start()
    wait_all(copies)


def arrive_last(partial, rest, halos):
    return pl.pallas_call(
        arrive_last_kernel,
        out_shape=jax.ShapeDtypeStruct(partial.shape, partial.dtype),
        in_specs=[ANY] + [VMEM] * (1 + len(halos)),
        out_specs=ANY,
        scratch_shapes=[
            pltpu.VMEM(rest.shape, rest.dtype),
            pltpu.SemaphoreType.DMA((rest.shape[0],)),
        ],
        input_output_aliases={0: 0},
        compiler_params=pltpu.CompilerParams(vmem_limit_bytes=VMEM_LIMIT),
        cost_estimate=LIGHT,
        name="arrive_last",
    )(in_hbm(partial), in_vmem(rest), *[in_vmem(halo) for halo in halos])


def routes(mesh):
    names = tuple(mesh.axis_names)
    sizes = [mesh.shape[name] for name in names]
    slabs, groups = mesh.shape["pos"], mesh.shape["vel"]

    def place(pos, vel):
        at = {"pos": pos % slabs, "vel": vel}
        index = 0
        for name, size in zip(names, sizes):
            index = index * size + at[name]
        return index

    value_route, density_route, over_route, swap_route = [], [], [], []
    for pos in range(slabs):
        for vel in range(groups):
            onward = 1 if vel < groups // 2 else -1
            value_route.append((place(pos, vel), place(pos + onward, vel)))
            density_route.append((place(pos, vel), place(pos - onward, vel)))
            leads = slabs % 2 == 0 and (pos % 2 == 0) == (onward > 0)
            over_route.append((place(pos, vel), place(pos - 2 * onward if leads else pos, vel)))
            swap_route.append((place(pos, vel), place(pos + onward if leads else pos - onward, vel)))
    return names, value_route, density_route, over_route, swap_route


def body(mesh, value_next, density):
    names, value_route, density_route, over_route, swap_route = routes(mesh)
    groups = mesh.shape["vel"]
    count, rows, second, width = value_next.shape
    tail = max(1, rows // 8)
    near = rows // 2 - tail - 1
    cuts = (
        (0, near),
        (near, rows - 2 * tail),
        (rows - 2 * tail, rows - tail),
        (rows - tail, rows),
    )
    onward = [(v, v + 1) for v in range(groups - 1)]
    back = [(v + 1, v) for v in range(groups - 1)]

    split = rows // 2 + 1
    value_halos = [
        lax.ppermute(value_rows(value_next, begin, end), names, value_route)
        for begin, end in ((0, split), (split, rows))
    ]
    low, high, *parts = edges(value_next, density, cuts)
    fillers = [lax.ppermute(part, names, over_route) for part in parts[1::2]]
    low = lax.ppermute(low, "vel", onward)
    high = lax.ppermute(high, "vel", back)
    mass = lax.psum(jnp.sum(density, axis=(1, 2)), "vel") / (second * second)
    crowding = CROWDING * mass * mass

    held = (parts[::2], value_halos, crowding, low, high, fillers)
    parts, value_halos, crowding, low, high, _ = lax.optimization_barrier(held)
    fillers = [lax.ppermute(part, names, swap_route) for part in fillers]
    parts = [lax.ppermute(part, names, density_route) for part in parts]

    value_now, low_now, high_now = value_step(value_next, low, high, crowding, value_halos)
    low_now = lax.ppermute(low_now, "vel", onward)
    high_now = lax.ppermute(high_now, "vel", back)
    density_next, rest = density_step(
        density, value_now, low, high, low_now, high_now, 2 * tail
    )
    density_next = arrive(density_next, (parts[0], fillers[0]))
    density_next = arrive_last(density_next, rest, (parts[1], fillers[1]))
    return value_now, density_next


def solution(mesh):
    placed = (P("pos", "vel", None, None), P("pos", "vel", None, None))
    return jax.shard_map(
        functools.partial(body, mesh),
        mesh=mesh,
        in_specs=placed,
        out_specs=placed,
        check_vma=False,
    )
```

```python
import functools

import jax
import jax.numpy as jnp
from jax import lax
from jax.experimental import pallas as pl
from jax.experimental.pallas import tpu as pltpu
from jax.sharding import PartitionSpec as P

COURANT = 0.4
CONTROL_COST = 0.25
VISCOSITY = 0.15
CROWDING = 0.3

SUB = 8
LANES = 128
EARLY = 1
SHIFT = 3
VMEM_LIMIT = 18 * 1024 * 1024
ANY = pl.BlockSpec(memory_space=pl.ANY)
VMEM = pl.BlockSpec(memory_space=pltpu.VMEM)
LIGHT = pl.CostEstimate(flops=0, transcendentals=0, bytes_accessed=0)


def is_negative():
    return lax.axis_index("vel") < lax.axis_size("vel") // 2


def slant(first, total):
    return COURANT * (jnp.abs(first.astype(jnp.float32) + 0.5 - total / 2) / (total / 2))


def start_all(copies):
    for copy in copies:
        copy.start()


def wait_all(copies):
    for copy in copies:
        copy.wait()


def in_hbm(array):
    return pltpu.with_memory_space_constraint(array, pltpu.HBM)


def in_vmem(array):
    return pltpu.with_memory_space_constraint(array, pltpu.VMEM)


def relay(pairs, held, load, store):
    inward = [
        pltpu.make_async_copy(source, held.at[k], load.at[k]) for k, (source, _) in enumerate(pairs)
    ]
    outward = [
        pltpu.make_async_copy(held.at[k], target, store.at[k]) for k, (_, target) in enumerate(pairs)
    ]
    start_all(inward)
    for come, go in zip(inward, outward):
        come.wait()
        go.start()
    wait_all(outward)


def relay_scratch(slots, second, width, dtype):
    sems = pltpu.SemaphoreType.DMA((slots,))
    return [pltpu.VMEM((slots, second, width), dtype), sems, sems]


def leaving_rows(field, row, cuts, sent):
    return [
        (field.at[row, a], target.at[a - begin])
        for (begin, end), target in zip(cuts, sent)
        for a in range(begin, end)
    ]


def value_rows_kernel(begin, value, sent, sems):
    row = jnp.where(is_negative(), value.shape[0] - 1, 0)
    half = sent.shape[1]
    copies = [
        pltpu.make_async_copy(
            value.at[row, (begin + k) // 2, pl.ds((begin + k) % 2 * half, half)],
            sent.at[k],
            sems.at[k],
        )
        for k in range(sent.shape[0])
    ]
    start_all(copies)
    wait_all(copies)


def value_rows(value, begin, end):
    _, _, second, width = value.shape
    return pl.pallas_call(
        functools.partial(value_rows_kernel, begin),
        out_shape=[pltpu.VMEM((end - begin, second // 2, width), value.dtype)],
        in_specs=[ANY],
        out_specs=[VMEM],
        scratch_shapes=[pltpu.SemaphoreType.DMA((end - begin,))],
        compiler_params=pltpu.CompilerParams(vmem_limit_bytes=VMEM_LIMIT),
        cost_estimate=LIGHT,
        name="value_rows",
    )(in_hbm(value))[0]


def edges_kernel(cuts, value, density, after, low, high, *rest):
    del after
    count, rows = value.shape[:2]
    row = jnp.where(is_negative(), 0, count - 1)
    pairs = []
    for k, field in enumerate((value, density)):
        for i in range(count):
            pairs.append((field.at[i, rows - 1], low.at[k, i]))
            pairs.append((field.at[i, 0], high.at[k, i]))
    pairs += leaving_rows(density, row, cuts, rest[: len(cuts)])
    relay(pairs, *rest[len(cuts) :])


def edges(value, density, after, cuts):
    count, rows, second, width = value.shape
    edge = pltpu.HBM((2, count, second, width), value.dtype)
    parts = [pltpu.HBM((e - b, second, width), value.dtype) for b, e in cuts]
    return pl.pallas_call(
        functools.partial(edges_kernel, cuts),
        out_shape=[edge, edge, *parts],
        in_specs=[ANY, ANY, ANY],
        out_specs=[ANY] * (2 + len(cuts)),
        scratch_shapes=relay_scratch(4 * count + rows, second, width, value.dtype),
        compiler_params=pltpu.CompilerParams(vmem_limit_bytes=VMEM_LIMIT),
        cost_estimate=LIGHT,
        name="edges",
    )(in_hbm(value), in_hbm(density), after)


def second_tile(ref, index, at, total):
    here = ref[*index, pl.ds(at, SUB), :]
    place = lax.broadcasted_iota(jnp.int32, here.shape, 0)
    if at + SUB < total:
        above = ref[*index, pl.ds(at + 1, SUB), :]
    else:
        above = jnp.where(place == SUB - 1, here, pltpu.roll(here, SUB - 1, 0))
    if at > 0:
        below = ref[*index, pl.ds(at - 1, SUB), :]
    else:
        below = jnp.where(place == 0, here, pltpu.roll(here, 1, 0))
    return here, above, below


def steep_tiles(second, width):
    tiles = []
    for at in range(0, second, SUB):
        index = at + lax.broadcasted_iota(jnp.int32, (SUB, LANES), 0)
        tiles.append(jnp.concatenate([slant(index, second)] * (width // LANES), 1))
    return tiles


def value_kernel(value, low, high, crowding, *rest):
    parts = len(rest) - 9
    halos = rest[:parts]
    value_now, low_now, high_now, pad, halo, fresh, load, edge, store = rest[parts:]
    count, rows, second, width = value.shape
    negative = is_negative()
    first = lax.axis_index("vel") == 0
    last = lax.axis_index("vel") == lax.axis_size("vel") - 1
    base = lax.axis_index("vel") * rows
    total = rows * lax.axis_size("vel")
    order = [jnp.where(negative, t, count - 1 - t) for t in range(count)]
    half = second // 2

    begin = 0
    halo_copies = []
    for k, part in enumerate(halos):
        extent = part.shape[0]
        halo_copies.append(
            pltpu.make_async_copy(part, halo.at[pl.ds(begin, extent)], load.at[count + k])
        )
        begin += extent
    start_all(halo_copies)
    centre_copies = [
        pltpu.make_async_copy(value.at[i], pad.at[i, pl.ds(1, rows)], load.at[t])
        for t, i in enumerate(order)
    ]
    start_all(centre_copies)
    below_own = pltpu.make_async_copy(value.at[:, 0], pad.at[:, 0], edge.at[0])
    below_far = pltpu.make_async_copy(low.at[0], pad.at[:, 0], edge.at[0])
    above_own = pltpu.make_async_copy(value.at[:, rows - 1], pad.at[:, rows + 1], edge.at[1])
    above_far = pltpu.make_async_copy(high.at[0], pad.at[:, rows + 1], edge.at[1])
    pl.when(first)(below_own.start)
    pl.when(jnp.logical_not(first))(below_far.start)
    pl.when(last)(above_own.start)
    pl.when(jnp.logical_not(last))(above_far.start)
    below_far.wait()
    above_far.wait()
    wait_all(halo_copies)

    steep_y = steep_tiles(second, width)
    stores = []
    for t, i in enumerate(order):
        centre_copies[t].wait()

        def step(a, carry, t=t, i=i):
            steep = slant(base + a, total)
            for at in range(0, second, SUB):
                here, up_w, dn_w = second_tile(pad, (i, a + 1), at, second)
                if t == 0:
                    x_near = halo[2 * a + at // half, pl.ds(at % half, SUB), :]
                else:
                    x_near = pad[order[t - 1], a + 1, pl.ds(at, SUB), :]
                y_near = pltpu.roll(here, 1 if at < second // 2 else width - 1, 1)
                up_v = pad[i, a + 2, pl.ds(at, SUB), :] - here
                dn_v = here - pad[i, a, pl.ds(at, SUB), :]
                up_w = up_w - here
                dn_w = here - dn_w
                hamilton = (
                    jnp.square(jnp.maximum(dn_v, 0.0))
                    + jnp.square(jnp.minimum(up_v, 0.0))
                    + jnp.square(jnp.maximum(dn_w, 0.0))
                    + jnp.square(jnp.minimum(up_w, 0.0))
                )
                laplace = up_v - dn_v + up_w - dn_w
                fresh[i, a, pl.ds(at, SUB), :] = (
                    here
                    + steep * (x_near - here)
                    + steep_y[at // SUB] * (y_near - here)
                    - (0.5 * CONTROL_COST) * hamilton
                    + VISCOSITY * laplace
                    + crowding[pl.ds(i, 1), :]
                )
            return carry

        lax.fori_loop(0, rows, step, 0)
        stores.append(pltpu.make_async_copy(fresh.at[i], value_now.at[i], store.at[t]))
        stores[-1].start()
    stores.append(pltpu.make_async_copy(fresh.at[:, rows - 1], low_now, store.at[count]))
    stores.append(pltpu.make_async_copy(fresh.at[:, 0], high_now, store.at[count + 1]))
    start_all(stores[count:])
    wait_all(stores)


def value_step(value, low, high, crowding, halos):
    count, rows, second, width = value.shape
    cells = count * rows * second * width
    edge = jax.ShapeDtypeStruct((count, second, width), value.dtype)
    return pl.pallas_call(
        value_kernel,
        out_shape=[jax.ShapeDtypeStruct(value.shape, value.dtype), edge, edge],
        in_specs=[ANY, ANY, ANY, VMEM] + [ANY] * len(halos),
        out_specs=[ANY] * 3,
        scratch_shapes=[
            pltpu.VMEM((count, rows + 2, second, width), value.dtype),
            pltpu.VMEM((2 * rows, second // 2, width), value.dtype),
            pltpu.VMEM(value.shape, value.dtype),
            pltpu.SemaphoreType.DMA((count + len(halos),)),
            pltpu.SemaphoreType.DMA((2,)),
            pltpu.SemaphoreType.DMA((count + 2,)),
        ],
        compiler_params=pltpu.CompilerParams(vmem_limit_bytes=VMEM_LIMIT),
        cost_estimate=LIGHT,
        name="value_step",
    )(in_hbm(value), low, high, crowding, *halos)


def density_kernel(
    density, control, low, high, low_now, high_now, out, rest, pad, ctl, fresh, load, edge, store
):
    count, rows, second, width = density.shape
    negative = is_negative()
    first = lax.axis_index("vel") == 0
    last = lax.axis_index("vel") == lax.axis_size("vel") - 1
    base = lax.axis_index("vel") * rows
    total = rows * lax.axis_size("vel")
    order = [jnp.where(negative, count - 1 - t, t) for t in range(count)]

    centre_copies = []
    for t, i in enumerate(order):
        pair = [
            pltpu.make_async_copy(density.at[i], pad.at[i, pl.ds(1, rows)], load.at[2 * t]),
            pltpu.make_async_copy(control.at[i], ctl.at[i, pl.ds(1, rows)], load.at[2 * t + 1]),
        ]
        start_all(pair)
        centre_copies.append(pair)
    waits = []
    fields = ((density, low.at[1], high.at[1], pad), (control, low_now, high_now, ctl))
    for k, (field, below, above, padded) in enumerate(fields):
        for outer, own, far, place, sem in (
            (first, field.at[:, 0], below, 0, edge.at[2 * k]),
            (last, field.at[:, rows - 1], above, rows + 1, edge.at[2 * k + 1]),
        ):
            own_copy = pltpu.make_async_copy(own, padded.at[:, place], sem)
            far_copy = pltpu.make_async_copy(far, padded.at[:, place], sem)
            pl.when(outer)(own_copy.start)
            pl.when(jnp.logical_not(outer))(far_copy.start)
            waits.append(far_copy)
    wait_all(waits)

    steep_y = steep_tiles(second, width)
    stores = []
    for t, i in enumerate(order):
        wait_all(centre_copies[t])

        def step(a, carry, t=t, i=i):
            steep = slant(base + a, total)
            for at in range(0, second, SUB):
                here, up_w, dn_w = second_tile(pad, (i, a + 1), at, second)
                ctl_here, ctl_up_w, ctl_dn_w = second_tile(ctl, (i, a + 1), at, second)
                up_v = pad[i, a + 2, pl.ds(at, SUB), :]
                dn_v = pad[i, a, pl.ds(at, SUB), :]
                y_near = pltpu.roll(here, width - 1 if at < second // 2 else 1, 1)
                if t == 0:
                    along_x = -steep * here
                else:
                    along_x = steep * (pad[order[t - 1], a + 1, pl.ds(at, SUB), :] - here)
                up = ctl[i, a + 2, pl.ds(at, SUB), :] - ctl_here
                dn = ctl_here - ctl[i, a, pl.ds(at, SUB), :]
                right = ctl_up_w - ctl_here
                left = ctl_here - ctl_dn_w
                flux_up = jnp.minimum(up, 0.0) * here + jnp.maximum(up, 0.0) * up_v
                flux_dn = jnp.minimum(dn, 0.0) * dn_v + jnp.maximum(dn, 0.0) * here
                flux_right = jnp.minimum(right, 0.0) * here + jnp.maximum(right, 0.0) * up_w
                flux_left = jnp.minimum(left, 0.0) * dn_w + jnp.maximum(left, 0.0) * here
                flux = flux_up - flux_dn + flux_right - flux_left
                spread = up_v + dn_v + up_w + dn_w - 4.0 * here
                fresh[i, a, pl.ds(at, SUB), :] = (
                    here
                    + along_x
                    + steep_y[at // SUB] * (y_near - here)
                    + CONTROL_COST * flux
                    + VISCOSITY * spread
                )
            return carry

        lax.fori_loop(0, rows, step, 0)
        stores.append(pltpu.make_async_copy(fresh.at[i], out.at[i], store.at[t]))
        stores[-1].start()
        if t == 0:
            extent = rest.shape[0]
            rest[...] = fresh[i, pl.ds(rows - extent, extent)]
    wait_all(stores)


def density_step(density, control, low, high, low_now, high_now, extent):
    count, rows, second, width = density.shape
    cells = count * rows * second * width
    padded = pltpu.VMEM((count, rows + 2, second, width), density.dtype)
    return pl.pallas_call(
        density_kernel,
        out_shape=[
            jax.ShapeDtypeStruct(density.shape, density.dtype),
            pltpu.VMEM((extent, second, width), density.dtype),
        ],
        in_specs=[ANY] * 6,
        out_specs=[ANY, VMEM],
        scratch_shapes=[
            padded,
            padded,
            pltpu.VMEM(density.shape, density.dtype),
            pltpu.SemaphoreType.DMA((2 * count,)),
            pltpu.SemaphoreType.DMA((4,)),
            pltpu.SemaphoreType.DMA((count,)),
        ],
        compiler_params=pltpu.CompilerParams(vmem_limit_bytes=VMEM_LIMIT),
        cost_estimate=LIGHT,
        name="density_step",
    )(in_hbm(density), in_hbm(control), low, high, low_now, high_now)


def arrive_kernel(partial, *refs):
    halos, (out, held, near, load, store) = refs[:-5], refs[-5:]
    count, rows = partial.shape[:2]
    row = jnp.where(is_negative(), count - 1, 0)
    base = lax.axis_index("vel") * rows
    total = rows * lax.axis_size("vel")
    loads = []
    for halo in halos:
        for k in range(halo.shape[0]):
            a = len(loads)
            pair = [
                pltpu.make_async_copy(partial.at[row, a], held.at[a], load.at[2 * a]),
                pltpu.make_async_copy(halo.at[k], near.at[a], load.at[2 * a + 1]),
            ]
            start_all(pair)
            loads.append(pair)
    stores = []
    for a, pair in enumerate(loads):
        wait_all(pair)
        held[a] = held[a] + slant(base + a, total) * near[a]
        stores.append(pltpu.make_async_copy(held.at[a], out.at[row, a], store.at[a]))
        stores[-1].start()
    wait_all(stores)


def arrive(partial, halos):
    extent = sum(halo.shape[0] for halo in halos)
    block = pltpu.VMEM((extent,) + partial.shape[2:], partial.dtype)
    return pl.pallas_call(
        arrive_kernel,
        out_shape=jax.ShapeDtypeStruct(partial.shape, partial.dtype),
        in_specs=[ANY] * (1 + len(halos)),
        out_specs=ANY,
        scratch_shapes=[
            block,
            block,
            pltpu.SemaphoreType.DMA((2 * extent,)),
            pltpu.SemaphoreType.DMA((extent,)),
        ],
        input_output_aliases={0: 0},
        compiler_params=pltpu.CompilerParams(vmem_limit_bytes=VMEM_LIMIT),
        cost_estimate=LIGHT,
        name="arrive",
    )(in_hbm(partial), *halos)


def arrive_last_kernel(partial, rest, *refs):
    halos, (out, held, sems) = refs[:-3], refs[-3:]
    count, rows = partial.shape[:2]
    extent = rest.shape[0]
    row = jnp.where(is_negative(), count - 1, 0)
    base = lax.axis_index("vel") * rows + rows - extent
    total = rows * lax.axis_size("vel")
    copies = []
    for halo in halos:
        for k in range(halo.shape[0]):
            a = len(copies)
            held[a] = rest[a] + slant(base + a, total) * halo[k]
            target = out.at[row, rows - extent + a]
            copies.append(pltpu.make_async_copy(held.at[a], target, sems.at[a]))
            copies[-1].start()
    wait_all(copies)


def arrive_last(partial, rest, halos):
    return pl.pallas_call(
        arrive_last_kernel,
        out_shape=jax.ShapeDtypeStruct(partial.shape, partial.dtype),
        in_specs=[ANY] + [VMEM] * (1 + len(halos)),
        out_specs=ANY,
        scratch_shapes=[
            pltpu.VMEM(rest.shape, rest.dtype),
            pltpu.SemaphoreType.DMA((rest.shape[0],)),
        ],
        input_output_aliases={0: 0},
        compiler_params=pltpu.CompilerParams(vmem_limit_bytes=VMEM_LIMIT),
        cost_estimate=LIGHT,
        name="arrive_last",
    )(in_hbm(partial), in_vmem(rest), *[in_vmem(halo) for halo in halos])


def routes(mesh):
    names = tuple(mesh.axis_names)
    sizes = [mesh.shape[name] for name in names]
    slabs, groups = mesh.shape["pos"], mesh.shape["vel"]

    def place(pos, vel):
        at = {"pos": pos % slabs, "vel": vel}
        index = 0
        for name, size in zip(names, sizes):
            index = index * size + at[name]
        return index

    value_route, density_route, over_route, swap_route = [], [], [], []
    for pos in range(slabs):
        for vel in range(groups):
            onward = 1 if vel < groups // 2 else -1
            value_route.append((place(pos, vel), place(pos + onward, vel)))
            density_route.append((place(pos, vel), place(pos - onward, vel)))
            leads = slabs % 2 == 0 and (pos % 2 == 0) == (onward > 0)
            over_route.append((place(pos, vel), place(pos - 2 * onward if leads else pos, vel)))
            swap_route.append((place(pos, vel), place(pos + onward if leads else pos - onward, vel)))
    return names, value_route, density_route, over_route, swap_route


def body(mesh, value_next, density):
    names, value_route, density_route, over_route, swap_route = routes(mesh)
    groups = mesh.shape["vel"]
    count, rows, second, width = value_next.shape
    tail = max(1, rows // 8)
    near = rows // 2 - tail - 1
    cuts = (
        (0, near),
        (near, rows - 2 * tail),
        (rows - 2 * tail, rows - tail),
        (rows - tail, rows),
    )
    onward = [(v, v + 1) for v in range(groups - 1)]
    back = [(v + 1, v) for v in range(groups - 1)]

    bounds = (0, 2 * EARLY, rows + 2 * EARLY + SHIFT, 2 * rows)
    value_halos = [
        lax.ppermute(value_rows(value_next, begin, end), names, value_route)
        for begin, end in zip(bounds, bounds[1:])
    ]
    low, high, *parts = edges(value_next, density, value_halos[0], cuts)
    fillers = [lax.ppermute(part, names, over_route) for part in parts[1::2]]
    mass = lax.psum(jnp.sum(density, axis=(1, 2)), "vel") / (second * second)
    crowding = CROWDING * mass * mass
    low, high, crowding = lax.optimization_barrier((low, high, crowding))
    low = lax.ppermute(low, "vel", onward)
    high = lax.ppermute(high, "vel", back)

    held = (parts[::2], value_halos, crowding, low, high, fillers)
    parts, value_halos, crowding, low, high, _ = lax.optimization_barrier(held)
    fillers = [lax.ppermute(part, names, swap_route) for part in fillers]
    parts = [lax.ppermute(part, names, density_route) for part in parts]

    value_now, low_now, high_now = value_step(value_next, low, high, crowding, value_halos)
    low_now = lax.ppermute(low_now, "vel", onward)
    high_now = lax.ppermute(high_now, "vel", back)
    density_next, rest = density_step(
        density, value_now, low, high, low_now, high_now, 2 * tail
    )
    density_next = arrive(density_next, (parts[0], fillers[0]))
    density_next = arrive_last(density_next, rest, (parts[1], fillers[1]))
    return value_now, density_next


def solution(mesh):
    placed = (P("pos", "vel", None, None), P("pos", "vel", None, None))
    return jax.shard_map(
        functools.partial(body, mesh),
        mesh=mesh,
        in_specs=placed,
        out_specs=placed,
        check_vma=False,
    )
```

```python
import functools

import jax
import jax.numpy as jnp
from jax import lax
from jax.experimental import pallas as pl
from jax.experimental.pallas import tpu as pltpu
from jax.sharding import PartitionSpec as P

COURANT = 0.4
CONTROL_COST = 0.25
VISCOSITY = 0.15
CROWDING = 0.3

SUB = 8
LANES = 128
EARLY = 1
SHIFT = 1
VMEM_LIMIT = 18 * 1024 * 1024
ANY = pl.BlockSpec(memory_space=pl.ANY)
VMEM = pl.BlockSpec(memory_space=pltpu.VMEM)
LIGHT = pl.CostEstimate(flops=0, transcendentals=0, bytes_accessed=0)


def is_negative():
    return lax.axis_index("vel") < lax.axis_size("vel") // 2


def slant(first, total):
    return COURANT * (jnp.abs(first.astype(jnp.float32) + 0.5 - total / 2) / (total / 2))


def start_all(copies):
    for copy in copies:
        copy.start()


def wait_all(copies):
    for copy in copies:
        copy.wait()


def in_hbm(array):
    return pltpu.with_memory_space_constraint(array, pltpu.HBM)


def in_vmem(array):
    return pltpu.with_memory_space_constraint(array, pltpu.VMEM)


def relay(pairs, held, load, store):
    inward = [
        pltpu.make_async_copy(source, held.at[k], load.at[k]) for k, (source, _) in enumerate(pairs)
    ]
    outward = [
        pltpu.make_async_copy(held.at[k], target, store.at[k]) for k, (_, target) in enumerate(pairs)
    ]
    start_all(inward)
    for come, go in zip(inward, outward):
        come.wait()
        go.start()
    wait_all(outward)


def relay_scratch(slots, second, width, dtype):
    sems = pltpu.SemaphoreType.DMA((slots,))
    return [pltpu.VMEM((slots, second, width), dtype), sems, sems]


def leaving_rows(field, row, cuts, sent):
    return [
        (field.at[row, a], target.at[a - begin])
        for (begin, end), target in zip(cuts, sent)
        for a in range(begin, end)
    ]


def value_rows_kernel(begin, value, sent, sems):
    row = jnp.where(is_negative(), value.shape[0] - 1, 0)
    half = sent.shape[1]
    copies = [
        pltpu.make_async_copy(
            value.at[row, (begin + k) // 2, pl.ds((begin + k) % 2 * half, half)],
            sent.at[k],
            sems.at[k],
        )
        for k in range(sent.shape[0])
    ]
    start_all(copies)
    wait_all(copies)


def value_rows(value, begin, end):
    _, _, second, width = value.shape
    return pl.pallas_call(
        functools.partial(value_rows_kernel, begin),
        out_shape=[pltpu.VMEM((end - begin, second // 2, width), value.dtype)],
        in_specs=[ANY],
        out_specs=[VMEM],
        scratch_shapes=[pltpu.SemaphoreType.DMA((end - begin,))],
        compiler_params=pltpu.CompilerParams(vmem_limit_bytes=VMEM_LIMIT),
        cost_estimate=LIGHT,
        name="value_rows",
    )(in_hbm(value))[0]


def edges_kernel(cuts, value, density, after, low, high, *rest):
    del after
    count, rows = value.shape[:2]
    row = jnp.where(is_negative(), 0, count - 1)
    pairs = []
    for k, field in enumerate((value, density)):
        for i in range(count):
            pairs.append((field.at[i, rows - 1], low.at[k, i]))
            pairs.append((field.at[i, 0], high.at[k, i]))
    pairs += leaving_rows(density, row, cuts, rest[: len(cuts)])
    relay(pairs, *rest[len(cuts) :])


def edges(value, density, after, cuts):
    count, rows, second, width = value.shape
    edge = pltpu.HBM((2, count, second, width), value.dtype)
    parts = [pltpu.HBM((e - b, second, width), value.dtype) for b, e in cuts]
    return pl.pallas_call(
        functools.partial(edges_kernel, cuts),
        out_shape=[edge, edge, *parts],
        in_specs=[ANY, ANY, ANY],
        out_specs=[ANY] * (2 + len(cuts)),
        scratch_shapes=relay_scratch(4 * count + rows, second, width, value.dtype),
        compiler_params=pltpu.CompilerParams(vmem_limit_bytes=VMEM_LIMIT),
        cost_estimate=LIGHT,
        name="edges",
    )(in_hbm(value), in_hbm(density), after)


def second_tile(ref, index, at, total):
    here = ref[*index, pl.ds(at, SUB), :]
    place = lax.broadcasted_iota(jnp.int32, here.shape, 0)
    if at + SUB < total:
        above = ref[*index, pl.ds(at + 1, SUB), :]
    else:
        above = jnp.where(place == SUB - 1, here, pltpu.roll(here, SUB - 1, 0))
    if at > 0:
        below = ref[*index, pl.ds(at - 1, SUB), :]
    else:
        below = jnp.where(place == 0, here, pltpu.roll(here, 1, 0))
    return here, above, below


def steep_tiles(second, width):
    tiles = []
    for at in range(0, second, SUB):
        index = at + lax.broadcasted_iota(jnp.int32, (SUB, LANES), 0)
        tiles.append(jnp.concatenate([slant(index, second)] * (width // LANES), 1))
    return tiles


def value_kernel(value, low, high, crowding, *rest):
    parts = len(rest) - 9
    halos = rest[:parts]
    value_now, low_now, high_now, pad, halo, fresh, load, edge, store = rest[parts:]
    count, rows, second, width = value.shape
    negative = is_negative()
    first = lax.axis_index("vel") == 0
    last = lax.axis_index("vel") == lax.axis_size("vel") - 1
    base = lax.axis_index("vel") * rows
    total = rows * lax.axis_size("vel")
    order = [jnp.where(negative, t, count - 1 - t) for t in range(count)]
    half = second // 2

    begin = 0
    halo_copies = []
    for k, part in enumerate(halos):
        extent = part.shape[0]
        halo_copies.append(
            pltpu.make_async_copy(part, halo.at[pl.ds(begin, extent)], load.at[count + k])
        )
        begin += extent
    start_all(halo_copies)
    centre_copies = [
        pltpu.make_async_copy(value.at[i], pad.at[i, pl.ds(1, rows)], load.at[t])
        for t, i in enumerate(order)
    ]
    start_all(centre_copies)
    below_own = pltpu.make_async_copy(value.at[:, 0], pad.at[:, 0], edge.at[0])
    below_far = pltpu.make_async_copy(low.at[0], pad.at[:, 0], edge.at[0])
    above_own = pltpu.make_async_copy(value.at[:, rows - 1], pad.at[:, rows + 1], edge.at[1])
    above_far = pltpu.make_async_copy(high.at[0], pad.at[:, rows + 1], edge.at[1])
    pl.when(first)(below_own.start)
    pl.when(jnp.logical_not(first))(below_far.start)
    pl.when(last)(above_own.start)
    pl.when(jnp.logical_not(last))(above_far.start)
    below_far.wait()
    above_far.wait()
    wait_all(halo_copies)

    steep_y = steep_tiles(second, width)
    stores = []
    for t, i in enumerate(order):
        centre_copies[t].wait()

        def step(a, carry, t=t, i=i):
            steep = slant(base + a, total)
            for at in range(0, second, SUB):
                here, up_w, dn_w = second_tile(pad, (i, a + 1), at, second)
                if t == 0:
                    x_near = halo[2 * a + at // half, pl.ds(at % half, SUB), :]
                else:
                    x_near = pad[order[t - 1], a + 1, pl.ds(at, SUB), :]
                y_near = pltpu.roll(here, 1 if at < second // 2 else width - 1, 1)
                up_v = pad[i, a + 2, pl.ds(at, SUB), :] - here
                dn_v = here - pad[i, a, pl.ds(at, SUB), :]
                up_w = up_w - here
                dn_w = here - dn_w
                hamilton = (
                    jnp.square(jnp.maximum(dn_v, 0.0))
                    + jnp.square(jnp.minimum(up_v, 0.0))
                    + jnp.square(jnp.maximum(dn_w, 0.0))
                    + jnp.square(jnp.minimum(up_w, 0.0))
                )
                laplace = up_v - dn_v + up_w - dn_w
                fresh[i, a, pl.ds(at, SUB), :] = (
                    here
                    + steep * (x_near - here)
                    + steep_y[at // SUB] * (y_near - here)
                    - (0.5 * CONTROL_COST) * hamilton
                    + VISCOSITY * laplace
                    + crowding[pl.ds(i, 1), :]
                )
            return carry

        lax.fori_loop(0, rows, step, 0)
        stores.append(pltpu.make_async_copy(fresh.at[i], value_now.at[i], store.at[t]))
        stores[-1].start()
    stores.append(pltpu.make_async_copy(fresh.at[:, rows - 1], low_now, store.at[count]))
    stores.append(pltpu.make_async_copy(fresh.at[:, 0], high_now, store.at[count + 1]))
    start_all(stores[count:])
    wait_all(stores)


def value_step(value, low, high, crowding, halos):
    count, rows, second, width = value.shape
    cells = count * rows * second * width
    edge = jax.ShapeDtypeStruct((count, second, width), value.dtype)
    return pl.pallas_call(
        value_kernel,
        out_shape=[jax.ShapeDtypeStruct(value.shape, value.dtype), edge, edge],
        in_specs=[ANY, ANY, ANY, VMEM] + [ANY] * len(halos),
        out_specs=[ANY] * 3,
        scratch_shapes=[
            pltpu.VMEM((count, rows + 2, second, width), value.dtype),
            pltpu.VMEM((2 * rows, second // 2, width), value.dtype),
            pltpu.VMEM(value.shape, value.dtype),
            pltpu.SemaphoreType.DMA((count + len(halos),)),
            pltpu.SemaphoreType.DMA((2,)),
            pltpu.SemaphoreType.DMA((count + 2,)),
        ],
        compiler_params=pltpu.CompilerParams(vmem_limit_bytes=VMEM_LIMIT),
        cost_estimate=LIGHT,
        name="value_step",
    )(in_hbm(value), low, high, crowding, *halos)


def density_kernel(
    density, control, low, high, low_now, high_now, out, rest, pad, ctl, fresh, load, edge, store
):
    count, rows, second, width = density.shape
    negative = is_negative()
    first = lax.axis_index("vel") == 0
    last = lax.axis_index("vel") == lax.axis_size("vel") - 1
    base = lax.axis_index("vel") * rows
    total = rows * lax.axis_size("vel")
    order = [jnp.where(negative, count - 1 - t, t) for t in range(count)]

    centre_copies = []
    for t, i in enumerate(order):
        pair = [
            pltpu.make_async_copy(density.at[i], pad.at[i, pl.ds(1, rows)], load.at[2 * t]),
            pltpu.make_async_copy(control.at[i], ctl.at[i, pl.ds(1, rows)], load.at[2 * t + 1]),
        ]
        start_all(pair)
        centre_copies.append(pair)
    waits = []
    fields = ((density, low.at[1], high.at[1], pad), (control, low_now, high_now, ctl))
    for k, (field, below, above, padded) in enumerate(fields):
        for outer, own, far, place, sem in (
            (first, field.at[:, 0], below, 0, edge.at[2 * k]),
            (last, field.at[:, rows - 1], above, rows + 1, edge.at[2 * k + 1]),
        ):
            own_copy = pltpu.make_async_copy(own, padded.at[:, place], sem)
            far_copy = pltpu.make_async_copy(far, padded.at[:, place], sem)
            pl.when(outer)(own_copy.start)
            pl.when(jnp.logical_not(outer))(far_copy.start)
            waits.append(far_copy)
    wait_all(waits)

    steep_y = steep_tiles(second, width)
    stores = []
    for t, i in enumerate(order):
        wait_all(centre_copies[t])

        def step(a, carry, t=t, i=i):
            steep = slant(base + a, total)
            for at in range(0, second, SUB):
                here, up_w, dn_w = second_tile(pad, (i, a + 1), at, second)
                ctl_here, ctl_up_w, ctl_dn_w = second_tile(ctl, (i, a + 1), at, second)
                up_v = pad[i, a + 2, pl.ds(at, SUB), :]
                dn_v = pad[i, a, pl.ds(at, SUB), :]
                y_near = pltpu.roll(here, width - 1 if at < second // 2 else 1, 1)
                if t == 0:
                    along_x = -steep * here
                else:
                    along_x = steep * (pad[order[t - 1], a + 1, pl.ds(at, SUB), :] - here)
                up = ctl[i, a + 2, pl.ds(at, SUB), :] - ctl_here
                dn = ctl_here - ctl[i, a, pl.ds(at, SUB), :]
                right = ctl_up_w - ctl_here
                left = ctl_here - ctl_dn_w
                flux_up = jnp.minimum(up, 0.0) * here + jnp.maximum(up, 0.0) * up_v
                flux_dn = jnp.minimum(dn, 0.0) * dn_v + jnp.maximum(dn, 0.0) * here
                flux_right = jnp.minimum(right, 0.0) * here + jnp.maximum(right, 0.0) * up_w
                flux_left = jnp.minimum(left, 0.0) * dn_w + jnp.maximum(left, 0.0) * here
                flux = flux_up - flux_dn + flux_right - flux_left
                spread = up_v + dn_v + up_w + dn_w - 4.0 * here
                fresh[i, a, pl.ds(at, SUB), :] = (
                    here
                    + along_x
                    + steep_y[at // SUB] * (y_near - here)
                    + CONTROL_COST * flux
                    + VISCOSITY * spread
                )
            return carry

        lax.fori_loop(0, rows, step, 0)
        stores.append(pltpu.make_async_copy(fresh.at[i], out.at[i], store.at[t]))
        stores[-1].start()
        if t == 0:
            extent = rest.shape[0]
            rest[...] = fresh[i, pl.ds(rows - extent, extent)]
    wait_all(stores)


def density_step(density, control, low, high, low_now, high_now, extent):
    count, rows, second, width = density.shape
    cells = count * rows * second * width
    padded = pltpu.VMEM((count, rows + 2, second, width), density.dtype)
    return pl.pallas_call(
        density_kernel,
        out_shape=[
            jax.ShapeDtypeStruct(density.shape, density.dtype),
            pltpu.VMEM((extent, second, width), density.dtype),
        ],
        in_specs=[ANY] * 6,
        out_specs=[ANY, VMEM],
        scratch_shapes=[
            padded,
            padded,
            pltpu.VMEM(density.shape, density.dtype),
            pltpu.SemaphoreType.DMA((2 * count,)),
            pltpu.SemaphoreType.DMA((4,)),
            pltpu.SemaphoreType.DMA((count,)),
        ],
        compiler_params=pltpu.CompilerParams(vmem_limit_bytes=VMEM_LIMIT),
        cost_estimate=LIGHT,
        name="density_step",
    )(in_hbm(density), in_hbm(control), low, high, low_now, high_now)


def arrive_kernel(partial, *refs):
    halos, (out, held, near, load, store) = refs[:-5], refs[-5:]
    count, rows = partial.shape[:2]
    row = jnp.where(is_negative(), count - 1, 0)
    base = lax.axis_index("vel") * rows
    total = rows * lax.axis_size("vel")
    loads = []
    for halo in halos:
        for k in range(halo.shape[0]):
            a = len(loads)
            pair = [
                pltpu.make_async_copy(partial.at[row, a], held.at[a], load.at[2 * a]),
                pltpu.make_async_copy(halo.at[k], near.at[a], load.at[2 * a + 1]),
            ]
            start_all(pair)
            loads.append(pair)
    stores = []
    for a, pair in enumerate(loads):
        wait_all(pair)
        held[a] = held[a] + slant(base + a, total) * near[a]
        stores.append(pltpu.make_async_copy(held.at[a], out.at[row, a], store.at[a]))
        stores[-1].start()
    wait_all(stores)


def arrive(partial, halos):
    extent = sum(halo.shape[0] for halo in halos)
    block = pltpu.VMEM((extent,) + partial.shape[2:], partial.dtype)
    return pl.pallas_call(
        arrive_kernel,
        out_shape=jax.ShapeDtypeStruct(partial.shape, partial.dtype),
        in_specs=[ANY] * (1 + len(halos)),
        out_specs=ANY,
        scratch_shapes=[
            block,
            block,
            pltpu.SemaphoreType.DMA((2 * extent,)),
            pltpu.SemaphoreType.DMA((extent,)),
        ],
        input_output_aliases={0: 0},
        compiler_params=pltpu.CompilerParams(vmem_limit_bytes=VMEM_LIMIT),
        cost_estimate=LIGHT,
        name="arrive",
    )(in_hbm(partial), *halos)


def arrive_rest_kernel(begin, partial, rest, halo, out, held, sems):
    count, rows = partial.shape[:2]
    extent = halo.shape[0]
    skipped = begin - (rows - rest.shape[0])
    row = jnp.where(is_negative(), count - 1, 0)
    base = lax.axis_index("vel") * rows + begin
    total = rows * lax.axis_size("vel")
    copies = []
    for a in range(extent):
        held[a] = rest[skipped + a] + slant(base + a, total) * halo[a]
        copies.append(pltpu.make_async_copy(held.at[a], out.at[row, begin + a], sems.at[a]))
        copies[-1].start()
    wait_all(copies)


def arrive_rest(partial, rest, halo, begin):
    return pl.pallas_call(
        functools.partial(arrive_rest_kernel, begin),
        out_shape=jax.ShapeDtypeStruct(partial.shape, partial.dtype),
        in_specs=[ANY, VMEM, VMEM],
        out_specs=ANY,
        scratch_shapes=[
            pltpu.VMEM(halo.shape, halo.dtype),
            pltpu.SemaphoreType.DMA((halo.shape[0],)),
        ],
        input_output_aliases={0: 0},
        compiler_params=pltpu.CompilerParams(vmem_limit_bytes=VMEM_LIMIT),
        cost_estimate=LIGHT,
        name="arrive_rest",
    )(in_hbm(partial), in_vmem(rest), in_vmem(halo))


def routes(mesh):
    names = tuple(mesh.axis_names)
    sizes = [mesh.shape[name] for name in names]
    slabs, groups = mesh.shape["pos"], mesh.shape["vel"]

    def place(pos, vel):
        at = {"pos": pos % slabs, "vel": vel}
        index = 0
        for name, size in zip(names, sizes):
            index = index * size + at[name]
        return index

    value_route, density_route, over_route, swap_route = [], [], [], []
    for pos in range(slabs):
        for vel in range(groups):
            onward = 1 if vel < groups // 2 else -1
            value_route.append((place(pos, vel), place(pos + onward, vel)))
            density_route.append((place(pos, vel), place(pos - onward, vel)))
            leads = slabs % 2 == 0 and (pos % 2 == 0) == (onward > 0)
            over_route.append((place(pos, vel), place(pos - 2 * onward if leads else pos, vel)))
            swap_route.append((place(pos, vel), place(pos + onward if leads else pos - onward, vel)))
    return names, value_route, density_route, over_route, swap_route


def body(mesh, value_next, density):
    names, value_route, density_route, over_route, swap_route = routes(mesh)
    groups = mesh.shape["vel"]
    count, rows, second, width = value_next.shape
    last, filler = max(1, rows // 16), max(1, rows // 8)
    near = rows // 2 - 2 * last
    cuts = (
        (0, near),
        (near, rows - last - filler),
        (rows - last - filler, rows - filler),
        (rows - filler, rows),
    )
    onward = [(v, v + 1) for v in range(groups - 1)]
    back = [(v + 1, v) for v in range(groups - 1)]

    bounds = (0, 2 * EARLY, rows + 2 * EARLY + SHIFT, 2 * rows)
    value_halos = [
        lax.ppermute(value_rows(value_next, begin, end), names, value_route)
        for begin, end in zip(bounds, bounds[1:])
    ]
    low, high, *parts = edges(value_next, density, value_halos[0], cuts)
    fillers = [lax.ppermute(part, names, over_route) for part in parts[1::2]]
    mass = lax.psum(jnp.sum(density, axis=(1, 2)), "vel") / (second * second)
    crowding = CROWDING * mass * mass
    low, high, crowding = lax.optimization_barrier((low, high, crowding))
    low = lax.ppermute(low, "vel", onward)
    high = lax.ppermute(high, "vel", back)

    held = (parts[::2], value_halos, crowding, low, high, fillers)
    parts, value_halos, crowding, low, high, _ = lax.optimization_barrier(held)
    fillers = [lax.ppermute(part, names, swap_route) for part in fillers]
    parts = [lax.ppermute(part, names, density_route) for part in parts]

    value_now, low_now, high_now = value_step(value_next, low, high, crowding, value_halos)
    low_now = lax.ppermute(low_now, "vel", onward)
    high_now = lax.ppermute(high_now, "vel", back)
    density_next, rest = density_step(
        density, value_now, low, high, low_now, high_now, last + filler
    )
    density_next = arrive(density_next, (parts[0], fillers[0]))
    density_next = arrive_rest(density_next, rest, fillers[1], cuts[3][0])
    density_next = arrive_rest(density_next, rest, parts[1], cuts[2][0])
    return value_now, density_next


def solution(mesh):
    placed = (P("pos", "vel", None, None), P("pos", "vel", None, None))
    return jax.shard_map(
        functools.partial(body, mesh),
        mesh=mesh,
        in_specs=placed,
        out_specs=placed,
        check_vma=False,
    )
```

```python
import functools

import jax
import jax.numpy as jnp
from jax import lax
from jax.experimental import pallas as pl
from jax.experimental.pallas import tpu as pltpu
from jax.sharding import PartitionSpec as P

COURANT = 0.4
CONTROL_COST = 0.25
VISCOSITY = 0.15
CROWDING = 0.3

SUB = 8
LANES = 128
EARLY = 3
SHIFT = 1
VMEM_LIMIT = 18 * 1024 * 1024
ANY = pl.BlockSpec(memory_space=pl.ANY)
VMEM = pl.BlockSpec(memory_space=pltpu.VMEM)
LIGHT = pl.CostEstimate(flops=0, transcendentals=0, bytes_accessed=0)


def is_negative():
    return lax.axis_index("vel") < lax.axis_size("vel") // 2


def slant(first, total):
    return COURANT * (jnp.abs(first.astype(jnp.float32) + 0.5 - total / 2) / (total / 2))


def start_all(copies):
    for copy in copies:
        copy.start()


def wait_all(copies):
    for copy in copies:
        copy.wait()


def in_hbm(array):
    return pltpu.with_memory_space_constraint(array, pltpu.HBM)


def in_vmem(array):
    return pltpu.with_memory_space_constraint(array, pltpu.VMEM)


def relay(pairs, held, load, store):
    inward = [
        pltpu.make_async_copy(source, held.at[k], load.at[k]) for k, (source, _) in enumerate(pairs)
    ]
    outward = [
        pltpu.make_async_copy(held.at[k], target, store.at[k]) for k, (_, target) in enumerate(pairs)
    ]
    start_all(inward)
    for come, go in zip(inward, outward):
        come.wait()
        go.start()
    wait_all(outward)


def relay_scratch(slots, second, width, dtype):
    sems = pltpu.SemaphoreType.DMA((slots,))
    return [pltpu.VMEM((slots, second, width), dtype), sems, sems]


def leaving_rows(field, row, cuts, sent):
    return [
        (field.at[row, a], target.at[a - begin])
        for (begin, end), target in zip(cuts, sent)
        for a in range(begin, end)
    ]


def value_rows_kernel(begin, value, sent, sems):
    row = jnp.where(is_negative(), value.shape[0] - 1, 0)
    half = sent.shape[1]
    copies = [
        pltpu.make_async_copy(
            value.at[row, (begin + k) // 2, pl.ds((begin + k) % 2 * half, half)],
            sent.at[k],
            sems.at[k],
        )
        for k in range(sent.shape[0])
    ]
    start_all(copies)
    wait_all(copies)


def value_rows(value, begin, end):
    _, _, second, width = value.shape
    return pl.pallas_call(
        functools.partial(value_rows_kernel, begin),
        out_shape=[pltpu.VMEM((end - begin, second // 2, width), value.dtype)],
        in_specs=[ANY],
        out_specs=[VMEM],
        scratch_shapes=[pltpu.SemaphoreType.DMA((end - begin,))],
        compiler_params=pltpu.CompilerParams(vmem_limit_bytes=VMEM_LIMIT),
        cost_estimate=LIGHT,
        name="value_rows",
    )(in_hbm(value))[0]


def edges_kernel(cuts, value, density, after, low, high, *rest):
    del after
    count, rows = value.shape[:2]
    row = jnp.where(is_negative(), 0, count - 1)
    pairs = []
    for k, field in enumerate((value, density)):
        for i in range(count):
            pairs.append((field.at[i, rows - 1], low.at[k, i]))
            pairs.append((field.at[i, 0], high.at[k, i]))
    pairs += leaving_rows(density, row, cuts, rest[: len(cuts)])
    relay(pairs, *rest[len(cuts) :])


def edges(value, density, after, cuts):
    count, rows, second, width = value.shape
    edge = pltpu.HBM((2, count, second, width), value.dtype)
    parts = [pltpu.HBM((e - b, second, width), value.dtype) for b, e in cuts]
    return pl.pallas_call(
        functools.partial(edges_kernel, cuts),
        out_shape=[edge, edge, *parts],
        in_specs=[ANY, ANY, ANY],
        out_specs=[ANY] * (2 + len(cuts)),
        scratch_shapes=relay_scratch(4 * count + rows, second, width, value.dtype),
        compiler_params=pltpu.CompilerParams(vmem_limit_bytes=VMEM_LIMIT),
        cost_estimate=LIGHT,
        name="edges",
    )(in_hbm(value), in_hbm(density), after)


def second_tile(ref, index, at, total):
    here = ref[*index, pl.ds(at, SUB), :]
    place = lax.broadcasted_iota(jnp.int32, here.shape, 0)
    if at + SUB < total:
        above = ref[*index, pl.ds(at + 1, SUB), :]
    else:
        above = jnp.where(place == SUB - 1, here, pltpu.roll(here, SUB - 1, 0))
    if at > 0:
        below = ref[*index, pl.ds(at - 1, SUB), :]
    else:
        below = jnp.where(place == 0, here, pltpu.roll(here, 1, 0))
    return here, above, below


def steep_tiles(second, width):
    tiles = []
    for at in range(0, second, SUB):
        index = at + lax.broadcasted_iota(jnp.int32, (SUB, LANES), 0)
        tiles.append(jnp.concatenate([slant(index, second)] * (width // LANES), 1))
    return tiles


def value_kernel(value, low, high, crowding, *rest):
    parts = len(rest) - 9
    halos = rest[:parts]
    value_now, low_now, high_now, pad, halo, fresh, load, edge, store = rest[parts:]
    count, rows, second, width = value.shape
    negative = is_negative()
    first = lax.axis_index("vel") == 0
    last = lax.axis_index("vel") == lax.axis_size("vel") - 1
    base = lax.axis_index("vel") * rows
    total = rows * lax.axis_size("vel")
    order = [jnp.where(negative, t, count - 1 - t) for t in range(count)]
    half = second // 2

    begin = 0
    halo_copies = []
    for k, part in enumerate(halos):
        extent = part.shape[0]
        halo_copies.append(
            pltpu.make_async_copy(part, halo.at[pl.ds(begin, extent)], load.at[count + k])
        )
        begin += extent
    start_all(halo_copies)
    centre_copies = [
        pltpu.make_async_copy(value.at[i], pad.at[i, pl.ds(1, rows)], load.at[t])
        for t, i in enumerate(order)
    ]
    start_all(centre_copies)
    below_own = pltpu.make_async_copy(value.at[:, 0], pad.at[:, 0], edge.at[0])
    below_far = pltpu.make_async_copy(low.at[0], pad.at[:, 0], edge.at[0])
    above_own = pltpu.make_async_copy(value.at[:, rows - 1], pad.at[:, rows + 1], edge.at[1])
    above_far = pltpu.make_async_copy(high.at[0], pad.at[:, rows + 1], edge.at[1])
    pl.when(first)(below_own.start)
    pl.when(jnp.logical_not(first))(below_far.start)
    pl.when(last)(above_own.start)
    pl.when(jnp.logical_not(last))(above_far.start)
    below_far.wait()
    above_far.wait()
    wait_all(halo_copies)

    steep_y = steep_tiles(second, width)
    stores = []
    for t, i in enumerate(order):
        centre_copies[t].wait()

        def step(a, carry, t=t, i=i):
            steep = slant(base + a, total)
            for at in range(0, second, SUB):
                here, up_w, dn_w = second_tile(pad, (i, a + 1), at, second)
                if t == 0:
                    x_near = halo[2 * a + at // half, pl.ds(at % half, SUB), :]
                else:
                    x_near = pad[order[t - 1], a + 1, pl.ds(at, SUB), :]
                y_near = pltpu.roll(here, 1 if at < second // 2 else width - 1, 1)
                up_v = pad[i, a + 2, pl.ds(at, SUB), :] - here
                dn_v = here - pad[i, a, pl.ds(at, SUB), :]
                up_w = up_w - here
                dn_w = here - dn_w
                hamilton = (
                    jnp.square(jnp.maximum(dn_v, 0.0))
                    + jnp.square(jnp.minimum(up_v, 0.0))
                    + jnp.square(jnp.maximum(dn_w, 0.0))
                    + jnp.square(jnp.minimum(up_w, 0.0))
                )
                laplace = up_v - dn_v + up_w - dn_w
                fresh[i, a, pl.ds(at, SUB), :] = (
                    here
                    + steep * (x_near - here)
                    + steep_y[at // SUB] * (y_near - here)
                    - (0.5 * CONTROL_COST) * hamilton
                    + VISCOSITY * laplace
                    + crowding[pl.ds(i, 1), :]
                )
            return carry

        lax.fori_loop(0, rows, step, 0)
        stores.append(pltpu.make_async_copy(fresh.at[i], value_now.at[i], store.at[t]))
        stores[-1].start()
    stores.append(pltpu.make_async_copy(fresh.at[:, rows - 1], low_now, store.at[count]))
    stores.append(pltpu.make_async_copy(fresh.at[:, 0], high_now, store.at[count + 1]))
    start_all(stores[count:])
    wait_all(stores)


def value_step(value, low, high, crowding, halos):
    count, rows, second, width = value.shape
    cells = count * rows * second * width
    edge = jax.ShapeDtypeStruct((count, second, width), value.dtype)
    return pl.pallas_call(
        value_kernel,
        out_shape=[jax.ShapeDtypeStruct(value.shape, value.dtype), edge, edge],
        in_specs=[ANY, ANY, ANY, VMEM] + [ANY] * len(halos),
        out_specs=[ANY] * 3,
        scratch_shapes=[
            pltpu.VMEM((count, rows + 2, second, width), value.dtype),
            pltpu.VMEM((2 * rows, second // 2, width), value.dtype),
            pltpu.VMEM(value.shape, value.dtype),
            pltpu.SemaphoreType.DMA((count + len(halos),)),
            pltpu.SemaphoreType.DMA((2,)),
            pltpu.SemaphoreType.DMA((count + 2,)),
        ],
        compiler_params=pltpu.CompilerParams(vmem_limit_bytes=VMEM_LIMIT),
        cost_estimate=LIGHT,
        name="value_step",
    )(in_hbm(value), low, high, crowding, *halos)


def density_kernel(
    density, control, low, high, low_now, high_now, out, rest, pad, ctl, fresh, load, edge, store
):
    count, rows, second, width = density.shape
    negative = is_negative()
    first = lax.axis_index("vel") == 0
    last = lax.axis_index("vel") == lax.axis_size("vel") - 1
    base = lax.axis_index("vel") * rows
    total = rows * lax.axis_size("vel")
    order = [jnp.where(negative, count - 1 - t, t) for t in range(count)]

    centre_copies = []
    for t, i in enumerate(order):
        pair = [
            pltpu.make_async_copy(density.at[i], pad.at[i, pl.ds(1, rows)], load.at[2 * t]),
            pltpu.make_async_copy(control.at[i], ctl.at[i, pl.ds(1, rows)], load.at[2 * t + 1]),
        ]
        start_all(pair)
        centre_copies.append(pair)
    waits = []
    fields = ((density, low.at[1], high.at[1], pad), (control, low_now, high_now, ctl))
    for k, (field, below, above, padded) in enumerate(fields):
        for outer, own, far, place, sem in (
            (first, field.at[:, 0], below, 0, edge.at[2 * k]),
            (last, field.at[:, rows - 1], above, rows + 1, edge.at[2 * k + 1]),
        ):
            own_copy = pltpu.make_async_copy(own, padded.at[:, place], sem)
            far_copy = pltpu.make_async_copy(far, padded.at[:, place], sem)
            pl.when(outer)(own_copy.start)
            pl.when(jnp.logical_not(outer))(far_copy.start)
            waits.append(far_copy)
    wait_all(waits)

    steep_y = steep_tiles(second, width)
    stores = []
    for t, i in enumerate(order):
        wait_all(centre_copies[t])

        def step(a, carry, t=t, i=i):
            steep = slant(base + a, total)
            for at in range(0, second, SUB):
                here, up_w, dn_w = second_tile(pad, (i, a + 1), at, second)
                ctl_here, ctl_up_w, ctl_dn_w = second_tile(ctl, (i, a + 1), at, second)
                up_v = pad[i, a + 2, pl.ds(at, SUB), :]
                dn_v = pad[i, a, pl.ds(at, SUB), :]
                y_near = pltpu.roll(here, width - 1 if at < second // 2 else 1, 1)
                if t == 0:
                    along_x = -steep * here
                else:
                    along_x = steep * (pad[order[t - 1], a + 1, pl.ds(at, SUB), :] - here)
                up = ctl[i, a + 2, pl.ds(at, SUB), :] - ctl_here
                dn = ctl_here - ctl[i, a, pl.ds(at, SUB), :]
                right = ctl_up_w - ctl_here
                left = ctl_here - ctl_dn_w
                flux_up = jnp.minimum(up, 0.0) * here + jnp.maximum(up, 0.0) * up_v
                flux_dn = jnp.minimum(dn, 0.0) * dn_v + jnp.maximum(dn, 0.0) * here
                flux_right = jnp.minimum(right, 0.0) * here + jnp.maximum(right, 0.0) * up_w
                flux_left = jnp.minimum(left, 0.0) * dn_w + jnp.maximum(left, 0.0) * here
                flux = flux_up - flux_dn + flux_right - flux_left
                spread = up_v + dn_v + up_w + dn_w - 4.0 * here
                fresh[i, a, pl.ds(at, SUB), :] = (
                    here
                    + along_x
                    + steep_y[at // SUB] * (y_near - here)
                    + CONTROL_COST * flux
                    + VISCOSITY * spread
                )
            return carry

        lax.fori_loop(0, rows, step, 0)
        stores.append(pltpu.make_async_copy(fresh.at[i], out.at[i], store.at[t]))
        stores[-1].start()
        if t == 0:
            extent = rest.shape[0]
            rest[...] = fresh[i, pl.ds(rows - extent, extent)]
    wait_all(stores)


def density_step(density, control, low, high, low_now, high_now, extent):
    count, rows, second, width = density.shape
    cells = count * rows * second * width
    padded = pltpu.VMEM((count, rows + 2, second, width), density.dtype)
    return pl.pallas_call(
        density_kernel,
        out_shape=[
            jax.ShapeDtypeStruct(density.shape, density.dtype),
            pltpu.VMEM((extent, second, width), density.dtype),
        ],
        in_specs=[ANY] * 6,
        out_specs=[ANY, VMEM],
        scratch_shapes=[
            padded,
            padded,
            pltpu.VMEM(density.shape, density.dtype),
            pltpu.SemaphoreType.DMA((2 * count,)),
            pltpu.SemaphoreType.DMA((4,)),
            pltpu.SemaphoreType.DMA((count,)),
        ],
        compiler_params=pltpu.CompilerParams(vmem_limit_bytes=VMEM_LIMIT),
        cost_estimate=LIGHT,
        name="density_step",
    )(in_hbm(density), in_hbm(control), low, high, low_now, high_now)


def arrive_kernel(partial, *refs):
    halos, (out, held, near, load, store) = refs[:-5], refs[-5:]
    count, rows = partial.shape[:2]
    row = jnp.where(is_negative(), count - 1, 0)
    base = lax.axis_index("vel") * rows
    total = rows * lax.axis_size("vel")
    loads = []
    for halo in halos:
        for k in range(halo.shape[0]):
            a = len(loads)
            pair = [
                pltpu.make_async_copy(partial.at[row, a], held.at[a], load.at[2 * a]),
                pltpu.make_async_copy(halo.at[k], near.at[a], load.at[2 * a + 1]),
            ]
            start_all(pair)
            loads.append(pair)
    stores = []
    for a, pair in enumerate(loads):
        wait_all(pair)
        held[a] = held[a] + slant(base + a, total) * near[a]
        stores.append(pltpu.make_async_copy(held.at[a], out.at[row, a], store.at[a]))
        stores[-1].start()
    wait_all(stores)


def arrive(partial, halos):
    extent = sum(halo.shape[0] for halo in halos)
    block = pltpu.VMEM((extent,) + partial.shape[2:], partial.dtype)
    return pl.pallas_call(
        arrive_kernel,
        out_shape=jax.ShapeDtypeStruct(partial.shape, partial.dtype),
        in_specs=[ANY] * (1 + len(halos)),
        out_specs=ANY,
        scratch_shapes=[
            block,
            block,
            pltpu.SemaphoreType.DMA((2 * extent,)),
            pltpu.SemaphoreType.DMA((extent,)),
        ],
        input_output_aliases={0: 0},
        compiler_params=pltpu.CompilerParams(vmem_limit_bytes=VMEM_LIMIT),
        cost_estimate=LIGHT,
        name="arrive",
    )(in_hbm(partial), *halos)


def arrive_rest_kernel(begin, partial, rest, halo, out, held, sems):
    count, rows = partial.shape[:2]
    extent = halo.shape[0]
    skipped = begin - (rows - rest.shape[0])
    row = jnp.where(is_negative(), count - 1, 0)
    base = lax.axis_index("vel") * rows + begin
    total = rows * lax.axis_size("vel")
    copies = []
    for a in range(extent):
        held[a] = rest[skipped + a] + slant(base + a, total) * halo[a]
        copies.append(pltpu.make_async_copy(held.at[a], out.at[row, begin + a], sems.at[a]))
        copies[-1].start()
    wait_all(copies)


def arrive_rest(partial, rest, halo, begin):
    return pl.pallas_call(
        functools.partial(arrive_rest_kernel, begin),
        out_shape=jax.ShapeDtypeStruct(partial.shape, partial.dtype),
        in_specs=[ANY, VMEM, VMEM],
        out_specs=ANY,
        scratch_shapes=[
            pltpu.VMEM(halo.shape, halo.dtype),
            pltpu.SemaphoreType.DMA((halo.shape[0],)),
        ],
        input_output_aliases={0: 0},
        compiler_params=pltpu.CompilerParams(vmem_limit_bytes=VMEM_LIMIT),
        cost_estimate=LIGHT,
        name="arrive_rest",
    )(in_hbm(partial), in_vmem(rest), in_vmem(halo))


def routes(mesh):
    names = tuple(mesh.axis_names)
    sizes = [mesh.shape[name] for name in names]
    slabs, groups = mesh.shape["pos"], mesh.shape["vel"]

    def place(pos, vel):
        at = {"pos": pos % slabs, "vel": vel}
        index = 0
        for name, size in zip(names, sizes):
            index = index * size + at[name]
        return index

    value_route, density_route, over_route, swap_route = [], [], [], []
    for pos in range(slabs):
        for vel in range(groups):
            onward = 1 if vel < groups // 2 else -1
            value_route.append((place(pos, vel), place(pos + onward, vel)))
            density_route.append((place(pos, vel), place(pos - onward, vel)))
            leads = slabs % 2 == 0 and (pos % 2 == 0) == (onward > 0)
            over_route.append((place(pos, vel), place(pos - 2 * onward if leads else pos, vel)))
            swap_route.append((place(pos, vel), place(pos + onward if leads else pos - onward, vel)))
    return names, value_route, density_route, over_route, swap_route


def body(mesh, value_next, density):
    names, value_route, density_route, over_route, swap_route = routes(mesh)
    groups = mesh.shape["vel"]
    count, rows, second, width = value_next.shape
    last, filler = max(1, rows // 16), max(1, rows // 8)
    near = rows // 2 - 2 * last
    cuts = (
        (0, near),
        (near, rows - last - filler),
        (rows - last - filler, rows - filler),
        (rows - filler, rows),
    )
    onward = [(v, v + 1) for v in range(groups - 1)]
    back = [(v + 1, v) for v in range(groups - 1)]

    bounds = (0, EARLY, rows + EARLY + SHIFT, 2 * rows)
    value_halos = [
        lax.ppermute(value_rows(value_next, begin, end), names, value_route)
        for begin, end in zip(bounds, bounds[1:])
    ]
    low, high, *parts = edges(value_next, density, value_halos[0], cuts)
    fillers = [lax.ppermute(part, names, over_route) for part in parts[1::2]]
    mass = lax.psum(jnp.sum(density, axis=(1, 2)), "vel") / (second * second)
    crowding = CROWDING * mass * mass
    low, high, crowding = lax.optimization_barrier((low, high, crowding))
    low = lax.ppermute(low, "vel", onward)
    high = lax.ppermute(high, "vel", back)

    held = (parts[::2], value_halos, crowding, low, high, fillers)
    parts, value_halos, crowding, low, high, _ = lax.optimization_barrier(held)
    fillers = [lax.ppermute(part, names, swap_route) for part in fillers]
    parts = [lax.ppermute(part, names, density_route) for part in parts]

    value_now, low_now, high_now = value_step(value_next, low, high, crowding, value_halos)
    low_now = lax.ppermute(low_now, "vel", onward)
    high_now = lax.ppermute(high_now, "vel", back)
    density_next, rest = density_step(
        density, value_now, low, high, low_now, high_now, last + filler
    )
    density_next = arrive(density_next, (parts[0], fillers[0]))
    density_next = arrive_rest(density_next, rest, fillers[1], cuts[3][0])
    density_next = arrive_rest(density_next, rest, parts[1], cuts[2][0])
    return value_now, density_next


def solution(mesh):
    placed = (P("pos", "vel", None, None), P("pos", "vel", None, None))
    return jax.shard_map(
        functools.partial(body, mesh),
        mesh=mesh,
        in_specs=placed,
        out_specs=placed,
        check_vma=False,
    )
```

```python
import functools

import jax
import jax.numpy as jnp
from jax import lax
from jax.experimental import pallas as pl
from jax.experimental.pallas import tpu as pltpu
from jax.sharding import PartitionSpec as P

COURANT = 0.4
CONTROL_COST = 0.25
VISCOSITY = 0.15
CROWDING = 0.3

SUB = 8
LANES = 128
EARLY = 1
SHIFT = 1
VMEM_LIMIT = 15 * 1024 * 1024
ANY = pl.BlockSpec(memory_space=pl.ANY)
VMEM = pl.BlockSpec(memory_space=pltpu.VMEM)
LIGHT = pl.CostEstimate(flops=0, transcendentals=0, bytes_accessed=0)


def is_negative():
    return lax.axis_index("vel") < lax.axis_size("vel") // 2


def slant(first, total):
    return COURANT * (jnp.abs(first.astype(jnp.float32) + 0.5 - total / 2) / (total / 2))


def start_all(copies):
    for copy in copies:
        copy.start()


def wait_all(copies):
    for copy in copies:
        copy.wait()


def in_hbm(array):
    return pltpu.with_memory_space_constraint(array, pltpu.HBM)


def in_vmem(array):
    return pltpu.with_memory_space_constraint(array, pltpu.VMEM)


def relay(pairs, held, load, store):
    inward = [
        pltpu.make_async_copy(source, held.at[k], load.at[k]) for k, (source, _) in enumerate(pairs)
    ]
    outward = [
        pltpu.make_async_copy(held.at[k], target, store.at[k]) for k, (_, target) in enumerate(pairs)
    ]
    start_all(inward)
    for come, go in zip(inward, outward):
        come.wait()
        go.start()
    wait_all(outward)


def relay_scratch(slots, second, width, dtype):
    sems = pltpu.SemaphoreType.DMA((slots,))
    return [pltpu.VMEM((slots, second, width), dtype), sems, sems]


def leaving_rows(field, row, cuts, sent):
    return [
        (field.at[row, a], target.at[a - begin])
        for (begin, end), target in zip(cuts, sent)
        for a in range(begin, end)
    ]


def value_rows_kernel(begin, value, sent, sems):
    row = jnp.where(is_negative(), value.shape[0] - 1, 0)
    half = sent.shape[1]
    copies = [
        pltpu.make_async_copy(
            value.at[row, (begin + k) // 2, pl.ds((begin + k) % 2 * half, half)],
            sent.at[k],
            sems.at[k],
        )
        for k in range(sent.shape[0])
    ]
    start_all(copies)
    wait_all(copies)


def value_rows(value, begin, end):
    _, _, second, width = value.shape
    return pl.pallas_call(
        functools.partial(value_rows_kernel, begin),
        out_shape=[pltpu.VMEM((end - begin, second // 2, width), value.dtype)],
        in_specs=[ANY],
        out_specs=[VMEM],
        scratch_shapes=[pltpu.SemaphoreType.DMA((end - begin,))],
        compiler_params=pltpu.CompilerParams(vmem_limit_bytes=VMEM_LIMIT),
        cost_estimate=LIGHT,
        name="value_rows",
    )(in_hbm(value))[0]


def edges_kernel(cuts, value, density, after, low, high, *rest):
    del after
    count, rows = value.shape[:2]
    row = jnp.where(is_negative(), 0, count - 1)
    pairs = []
    for k, field in enumerate((value, density)):
        for i in range(count):
            pairs.append((field.at[i, rows - 1], low.at[k, i]))
            pairs.append((field.at[i, 0], high.at[k, i]))
    pairs += leaving_rows(density, row, cuts, rest[: len(cuts)])
    relay(pairs, *rest[len(cuts) :])


def edges(value, density, after, cuts):
    count, rows, second, width = value.shape
    edge = pltpu.HBM((2, count, second, width), value.dtype)
    parts = [pltpu.HBM((e - b, second, width), value.dtype) for b, e in cuts]
    return pl.pallas_call(
        functools.partial(edges_kernel, cuts),
        out_shape=[edge, edge, *parts],
        in_specs=[ANY, ANY, ANY],
        out_specs=[ANY] * (2 + len(cuts)),
        scratch_shapes=relay_scratch(4 * count + rows, second, width, value.dtype),
        compiler_params=pltpu.CompilerParams(vmem_limit_bytes=VMEM_LIMIT),
        cost_estimate=LIGHT,
        name="edges",
    )(in_hbm(value), in_hbm(density), after)


def second_tile(ref, index, at, total):
    here = ref[*index, pl.ds(at, SUB), :]
    place = lax.broadcasted_iota(jnp.int32, here.shape, 0)
    if at + SUB < total:
        above = ref[*index, pl.ds(at + 1, SUB), :]
    else:
        above = jnp.where(place == SUB - 1, here, pltpu.roll(here, SUB - 1, 0))
    if at > 0:
        below = ref[*index, pl.ds(at - 1, SUB), :]
    else:
        below = jnp.where(place == 0, here, pltpu.roll(here, 1, 0))
    return here, above, below


def steep_tiles(second, width):
    tiles = []
    for at in range(0, second, SUB):
        index = at + lax.broadcasted_iota(jnp.int32, (SUB, LANES), 0)
        tiles.append(jnp.concatenate([slant(index, second)] * (width // LANES), 1))
    return tiles


def value_kernel(value, low, high, crowding, *rest):
    parts = len(rest) - 9
    halos = rest[:parts]
    value_now, low_now, high_now, pad, halo, fresh, load, edge, store = rest[parts:]
    count, rows, second, width = value.shape
    negative = is_negative()
    first = lax.axis_index("vel") == 0
    last = lax.axis_index("vel") == lax.axis_size("vel") - 1
    base = lax.axis_index("vel") * rows
    total = rows * lax.axis_size("vel")
    order = [jnp.where(negative, t, count - 1 - t) for t in range(count)]
    half = second // 2

    begin = 0
    halo_copies = []
    for k, part in enumerate(halos):
        extent = part.shape[0]
        halo_copies.append(
            pltpu.make_async_copy(part, halo.at[pl.ds(begin, extent)], load.at[count + k])
        )
        begin += extent
    start_all(halo_copies)
    centre_copies = [
        pltpu.make_async_copy(value.at[i], pad.at[i, pl.ds(1, rows)], load.at[t])
        for t, i in enumerate(order)
    ]
    start_all(centre_copies)
    below_own = pltpu.make_async_copy(value.at[:, 0], pad.at[:, 0], edge.at[0])
    below_far = pltpu.make_async_copy(low.at[0], pad.at[:, 0], edge.at[0])
    above_own = pltpu.make_async_copy(value.at[:, rows - 1], pad.at[:, rows + 1], edge.at[1])
    above_far = pltpu.make_async_copy(high.at[0], pad.at[:, rows + 1], edge.at[1])
    pl.when(first)(below_own.start)
    pl.when(jnp.logical_not(first))(below_far.start)
    pl.when(last)(above_own.start)
    pl.when(jnp.logical_not(last))(above_far.start)
    below_far.wait()
    above_far.wait()
    wait_all(halo_copies)

    steep_y = steep_tiles(second, width)
    stores = []
    for t, i in enumerate(order):
        centre_copies[t].wait()

        def step(a, carry, t=t, i=i):
            steep = slant(base + a, total)
            for at in range(0, second, SUB):
                here, up_w, dn_w = second_tile(pad, (i, a + 1), at, second)
                if t == 0:
                    x_near = halo[2 * a + at // half, pl.ds(at % half, SUB), :]
                else:
                    x_near = pad[order[t - 1], a + 1, pl.ds(at, SUB), :]
                y_near = pltpu.roll(here, 1 if at < second // 2 else width - 1, 1)
                up_v = pad[i, a + 2, pl.ds(at, SUB), :] - here
                dn_v = here - pad[i, a, pl.ds(at, SUB), :]
                up_w = up_w - here
                dn_w = here - dn_w
                hamilton = (
                    jnp.square(jnp.maximum(dn_v, 0.0))
                    + jnp.square(jnp.minimum(up_v, 0.0))
                    + jnp.square(jnp.maximum(dn_w, 0.0))
                    + jnp.square(jnp.minimum(up_w, 0.0))
                )
                laplace = up_v - dn_v + up_w - dn_w
                fresh[i, a, pl.ds(at, SUB), :] = (
                    here
                    + steep * (x_near - here)
                    + steep_y[at // SUB] * (y_near - here)
                    - (0.5 * CONTROL_COST) * hamilton
                    + VISCOSITY * laplace
                    + crowding[pl.ds(i, 1), :]
                )
            return carry

        lax.fori_loop(0, rows, step, 0)
        stores.append(pltpu.make_async_copy(fresh.at[i], value_now.at[i], store.at[t]))
        stores[-1].start()
    stores.append(pltpu.make_async_copy(fresh.at[:, rows - 1], low_now, store.at[count]))
    stores.append(pltpu.make_async_copy(fresh.at[:, 0], high_now, store.at[count + 1]))
    start_all(stores[count:])
    wait_all(stores)


def value_step(value, low, high, crowding, halos):
    count, rows, second, width = value.shape
    cells = count * rows * second * width
    edge = jax.ShapeDtypeStruct((count, second, width), value.dtype)
    return pl.pallas_call(
        value_kernel,
        out_shape=[jax.ShapeDtypeStruct(value.shape, value.dtype), edge, edge],
        in_specs=[ANY, ANY, ANY, VMEM] + [ANY] * len(halos),
        out_specs=[ANY] * 3,
        scratch_shapes=[
            pltpu.VMEM((count, rows + 2, second, width), value.dtype),
            pltpu.VMEM((2 * rows, second // 2, width), value.dtype),
            pltpu.VMEM(value.shape, value.dtype),
            pltpu.SemaphoreType.DMA((count + len(halos),)),
            pltpu.SemaphoreType.DMA((2,)),
            pltpu.SemaphoreType.DMA((count + 2,)),
        ],
        compiler_params=pltpu.CompilerParams(vmem_limit_bytes=VMEM_LIMIT),
        cost_estimate=LIGHT,
        name="value_step",
    )(in_hbm(value), low, high, crowding, *halos)


def density_kernel(
    density, control, low, high, low_now, high_now, out, rest, pad, ctl, fresh, load, edge, store
):
    count, rows, second, width = density.shape
    negative = is_negative()
    first = lax.axis_index("vel") == 0
    last = lax.axis_index("vel") == lax.axis_size("vel") - 1
    base = lax.axis_index("vel") * rows
    total = rows * lax.axis_size("vel")
    order = [jnp.where(negative, count - 1 - t, t) for t in range(count)]

    centre_copies = []
    for t, i in enumerate(order):
        pair = [
            pltpu.make_async_copy(density.at[i], pad.at[i, pl.ds(1, rows)], load.at[2 * t]),
            pltpu.make_async_copy(control.at[i], ctl.at[i, pl.ds(1, rows)], load.at[2 * t + 1]),
        ]
        start_all(pair)
        centre_copies.append(pair)
    waits = []
    fields = ((density, low.at[1], high.at[1], pad), (control, low_now, high_now, ctl))
    for k, (field, below, above, padded) in enumerate(fields):
        for outer, own, far, place, sem in (
            (first, field.at[:, 0], below, 0, edge.at[2 * k]),
            (last, field.at[:, rows - 1], above, rows + 1, edge.at[2 * k + 1]),
        ):
            own_copy = pltpu.make_async_copy(own, padded.at[:, place], sem)
            far_copy = pltpu.make_async_copy(far, padded.at[:, place], sem)
            pl.when(outer)(own_copy.start)
            pl.when(jnp.logical_not(outer))(far_copy.start)
            waits.append(far_copy)
    wait_all(waits)

    steep_y = steep_tiles(second, width)
    stores = []
    for t, i in enumerate(order):
        wait_all(centre_copies[t])

        def step(a, carry, t=t, i=i):
            steep = slant(base + a, total)
            for at in range(0, second, SUB):
                here, up_w, dn_w = second_tile(pad, (i, a + 1), at, second)
                ctl_here, ctl_up_w, ctl_dn_w = second_tile(ctl, (i, a + 1), at, second)
                up_v = pad[i, a + 2, pl.ds(at, SUB), :]
                dn_v = pad[i, a, pl.ds(at, SUB), :]
                y_near = pltpu.roll(here, width - 1 if at < second // 2 else 1, 1)
                if t == 0:
                    along_x = -steep * here
                else:
                    along_x = steep * (pad[order[t - 1], a + 1, pl.ds(at, SUB), :] - here)
                up = ctl[i, a + 2, pl.ds(at, SUB), :] - ctl_here
                dn = ctl_here - ctl[i, a, pl.ds(at, SUB), :]
                right = ctl_up_w - ctl_here
                left = ctl_here - ctl_dn_w
                flux_up = jnp.minimum(up, 0.0) * here + jnp.maximum(up, 0.0) * up_v
                flux_dn = jnp.minimum(dn, 0.0) * dn_v + jnp.maximum(dn, 0.0) * here
                flux_right = jnp.minimum(right, 0.0) * here + jnp.maximum(right, 0.0) * up_w
                flux_left = jnp.minimum(left, 0.0) * dn_w + jnp.maximum(left, 0.0) * here
                flux = flux_up - flux_dn + flux_right - flux_left
                spread = up_v + dn_v + up_w + dn_w - 4.0 * here
                fresh[i, a, pl.ds(at, SUB), :] = (
                    here
                    + along_x
                    + steep_y[at // SUB] * (y_near - here)
                    + CONTROL_COST * flux
                    + VISCOSITY * spread
                )
            return carry

        lax.fori_loop(0, rows, step, 0)
        stores.append(pltpu.make_async_copy(fresh.at[i], out.at[i], store.at[t]))
        stores[-1].start()
        if t == 0:
            extent = rest.shape[0]
            rest[...] = fresh[i, pl.ds(rows - extent, extent)]
    wait_all(stores)


def density_step(density, control, low, high, low_now, high_now, extent):
    count, rows, second, width = density.shape
    cells = count * rows * second * width
    padded = pltpu.VMEM((count, rows + 2, second, width), density.dtype)
    return pl.pallas_call(
        density_kernel,
        out_shape=[
            jax.ShapeDtypeStruct(density.shape, density.dtype),
            pltpu.VMEM((extent, second, width), density.dtype),
        ],
        in_specs=[ANY] * 6,
        out_specs=[ANY, VMEM],
        scratch_shapes=[
            padded,
            padded,
            pltpu.VMEM(density.shape, density.dtype),
            pltpu.SemaphoreType.DMA((2 * count,)),
            pltpu.SemaphoreType.DMA((4,)),
            pltpu.SemaphoreType.DMA((count,)),
        ],
        compiler_params=pltpu.CompilerParams(vmem_limit_bytes=VMEM_LIMIT),
        cost_estimate=LIGHT,
        name="density_step",
    )(in_hbm(density), in_hbm(control), low, high, low_now, high_now)


def arrive_kernel(partial, *refs):
    halos, (out, held, near, load, store) = refs[:-5], refs[-5:]
    count, rows = partial.shape[:2]
    row = jnp.where(is_negative(), count - 1, 0)
    base = lax.axis_index("vel") * rows
    total = rows * lax.axis_size("vel")
    loads = []
    for halo in halos:
        for k in range(halo.shape[0]):
            a = len(loads)
            pair = [
                pltpu.make_async_copy(partial.at[row, a], held.at[a], load.at[2 * a]),
                pltpu.make_async_copy(halo.at[k], near.at[a], load.at[2 * a + 1]),
            ]
            start_all(pair)
            loads.append(pair)
    stores = []
    for a, pair in enumerate(loads):
        wait_all(pair)
        held[a] = held[a] + slant(base + a, total) * near[a]
        stores.append(pltpu.make_async_copy(held.at[a], out.at[row, a], store.at[a]))
        stores[-1].start()
    wait_all(stores)


def arrive(partial, halos):
    extent = sum(halo.shape[0] for halo in halos)
    block = pltpu.VMEM((extent,) + partial.shape[2:], partial.dtype)
    return pl.pallas_call(
        arrive_kernel,
        out_shape=jax.ShapeDtypeStruct(partial.shape, partial.dtype),
        in_specs=[ANY] * (1 + len(halos)),
        out_specs=ANY,
        scratch_shapes=[
            block,
            block,
            pltpu.SemaphoreType.DMA((2 * extent,)),
            pltpu.SemaphoreType.DMA((extent,)),
        ],
        input_output_aliases={0: 0},
        compiler_params=pltpu.CompilerParams(vmem_limit_bytes=VMEM_LIMIT),
        cost_estimate=LIGHT,
        name="arrive",
    )(in_hbm(partial), *halos)


def arrive_rest_kernel(begin, partial, rest, halo, out, held, sems):
    count, rows = partial.shape[:2]
    extent = halo.shape[0]
    skipped = begin - (rows - rest.shape[0])
    row = jnp.where(is_negative(), count - 1, 0)
    base = lax.axis_index("vel") * rows + begin
    total = rows * lax.axis_size("vel")
    copies = []
    for a in range(extent):
        held[a] = rest[skipped + a] + slant(base + a, total) * halo[a]
        copies.append(pltpu.make_async_copy(held.at[a], out.at[row, begin + a], sems.at[a]))
        copies[-1].start()
    wait_all(copies)


def arrive_rest(partial, rest, halo, begin):
    return pl.pallas_call(
        functools.partial(arrive_rest_kernel, begin),
        out_shape=jax.ShapeDtypeStruct(partial.shape, partial.dtype),
        in_specs=[ANY, VMEM, VMEM],
        out_specs=ANY,
        scratch_shapes=[
            pltpu.VMEM(halo.shape, halo.dtype),
            pltpu.SemaphoreType.DMA((halo.shape[0],)),
        ],
        input_output_aliases={0: 0},
        compiler_params=pltpu.CompilerParams(vmem_limit_bytes=VMEM_LIMIT),
        cost_estimate=LIGHT,
        name="arrive_rest",
    )(in_hbm(partial), in_vmem(rest), in_vmem(halo))


def routes(mesh):
    names = tuple(mesh.axis_names)
    sizes = [mesh.shape[name] for name in names]
    slabs, groups = mesh.shape["pos"], mesh.shape["vel"]

    def place(pos, vel):
        at = {"pos": pos % slabs, "vel": vel}
        index = 0
        for name, size in zip(names, sizes):
            index = index * size + at[name]
        return index

    value_route, density_route, over_route, swap_route = [], [], [], []
    for pos in range(slabs):
        for vel in range(groups):
            onward = 1 if vel < groups // 2 else -1
            value_route.append((place(pos, vel), place(pos + onward, vel)))
            density_route.append((place(pos, vel), place(pos - onward, vel)))
            leads = slabs % 2 == 0 and (pos % 2 == 0) == (onward > 0)
            over_route.append((place(pos, vel), place(pos - 2 * onward if leads else pos, vel)))
            swap_route.append((place(pos, vel), place(pos + onward if leads else pos - onward, vel)))
    return names, value_route, density_route, over_route, swap_route


def body(mesh, value_next, density):
    names, value_route, density_route, over_route, swap_route = routes(mesh)
    groups = mesh.shape["vel"]
    count, rows, second, width = value_next.shape
    last, filler = max(1, rows // 16), max(1, rows // 8)
    near = rows // 2 - 2 * last
    cuts = (
        (0, near),
        (near, rows - last - filler),
        (rows - last - filler, rows - filler),
        (rows - filler, rows),
    )
    onward = [(v, v + 1) for v in range(groups - 1)]
    back = [(v + 1, v) for v in range(groups - 1)]

    bounds = (0, 2 * EARLY, rows + 2 * EARLY + SHIFT, 2 * rows)
    value_halos = [
        lax.ppermute(value_rows(value_next, begin, end), names, value_route)
        for begin, end in zip(bounds, bounds[1:])
    ]
    low, high, *parts = edges(value_next, density, value_halos[0], cuts)
    fillers = [lax.ppermute(part, names, over_route) for part in parts[1::2]]
    mass = lax.psum(jnp.sum(density, axis=(1, 2)), "vel") / (second * second)
    crowding = CROWDING * mass * mass
    low, high, crowding = lax.optimization_barrier((low, high, crowding))
    low = lax.ppermute(low, "vel", onward)
    high = lax.ppermute(high, "vel", back)

    held = (parts[::2], value_halos, crowding, low, high, fillers)
    parts, value_halos, crowding, low, high, _ = lax.optimization_barrier(held)
    fillers = [lax.ppermute(part, names, swap_route) for part in fillers]
    parts = [lax.ppermute(part, names, density_route) for part in parts]

    value_now, low_now, high_now = value_step(value_next, low, high, crowding, value_halos)
    low_now = lax.ppermute(low_now, "vel", onward)
    high_now = lax.ppermute(high_now, "vel", back)
    density_next, rest = density_step(
        density, value_now, low, high, low_now, high_now, last + filler
    )
    density_next = arrive(density_next, (parts[0], fillers[0]))
    density_next = arrive_rest(density_next, rest, fillers[1], cuts[3][0])
    density_next = arrive_rest(density_next, rest, parts[1], cuts[2][0])
    return value_now, density_next


def solution(mesh):
    placed = (P("pos", "vel", None, None), P("pos", "vel", None, None))
    return jax.shard_map(
        functools.partial(body, mesh),
        mesh=mesh,
        in_specs=placed,
        out_specs=placed,
        check_vma=False,
    )
```

```python
import functools

import jax
import jax.numpy as jnp
from jax import lax
from jax.experimental import pallas as pl
from jax.experimental.pallas import tpu as pltpu
from jax.sharding import PartitionSpec as P

COURANT = 0.4
CONTROL_COST = 0.25
VISCOSITY = 0.15
CROWDING = 0.3

SUB = 8
LANES = 128
EARLY = 1
SHIFT = 1
VMEM_LIMIT = 18 * 1024 * 1024
ANY = pl.BlockSpec(memory_space=pl.ANY)
VMEM = pl.BlockSpec(memory_space=pltpu.VMEM)
LIGHT = pl.CostEstimate(flops=0, transcendentals=0, bytes_accessed=0)


def is_negative():
    return lax.axis_index("vel") < lax.axis_size("vel") // 2


def slant(first, total):
    return COURANT * (jnp.abs(first.astype(jnp.float32) + 0.5 - total / 2) / (total / 2))


def start_all(copies):
    for copy in copies:
        copy.start()


def wait_all(copies):
    for copy in copies:
        copy.wait()


def in_hbm(array):
    return pltpu.with_memory_space_constraint(array, pltpu.HBM)


def in_vmem(array):
    return pltpu.with_memory_space_constraint(array, pltpu.VMEM)


def relay(pairs, held, load, store):
    inward = [
        pltpu.make_async_copy(source, held.at[k], load.at[k]) for k, (source, _) in enumerate(pairs)
    ]
    outward = [
        pltpu.make_async_copy(held.at[k], target, store.at[k]) for k, (_, target) in enumerate(pairs)
    ]
    start_all(inward)
    for come, go in zip(inward, outward):
        come.wait()
        go.start()
    wait_all(outward)


def relay_scratch(slots, second, width, dtype):
    sems = pltpu.SemaphoreType.DMA((slots,))
    return [pltpu.VMEM((slots, second, width), dtype), sems, sems]


def leaving_rows(field, row, cuts, sent):
    return [
        (field.at[row, a], target.at[a - begin])
        for (begin, end), target in zip(cuts, sent)
        for a in range(begin, end)
    ]


def value_rows_kernel(begin, value, sent, sems):
    row = jnp.where(is_negative(), value.shape[0] - 1, 0)
    half = sent.shape[1]
    copies = [
        pltpu.make_async_copy(
            value.at[row, (begin + k) // 2, pl.ds((begin + k) % 2 * half, half)],
            sent.at[k],
            sems.at[k],
        )
        for k in range(sent.shape[0])
    ]
    start_all(copies)
    wait_all(copies)


def value_rows(value, begin, end):
    _, _, second, width = value.shape
    return pl.pallas_call(
        functools.partial(value_rows_kernel, begin),
        out_shape=[pltpu.VMEM((end - begin, second // 2, width), value.dtype)],
        in_specs=[ANY],
        out_specs=[VMEM],
        scratch_shapes=[pltpu.SemaphoreType.DMA((end - begin,))],
        compiler_params=pltpu.CompilerParams(vmem_limit_bytes=VMEM_LIMIT),
        cost_estimate=LIGHT,
        name="value_rows",
    )(in_hbm(value))[0]


def edges_kernel(cuts, value, density, after, low, high, *rest):
    del after
    count, rows = value.shape[:2]
    row = jnp.where(is_negative(), 0, count - 1)
    pairs = []
    for k, field in enumerate((value, density)):
        for i in range(count):
            pairs.append((field.at[i, rows - 1], low.at[k, i]))
            pairs.append((field.at[i, 0], high.at[k, i]))
    pairs += leaving_rows(density, row, cuts, rest[: len(cuts)])
    relay(pairs, *rest[len(cuts) :])


def edges(value, density, after, cuts):
    count, rows, second, width = value.shape
    edge = pltpu.HBM((2, count, second, width), value.dtype)
    parts = [pltpu.HBM((e - b, second, width), value.dtype) for b, e in cuts]
    return pl.pallas_call(
        functools.partial(edges_kernel, cuts),
        out_shape=[edge, edge, *parts],
        in_specs=[ANY, ANY, ANY],
        out_specs=[ANY] * (2 + len(cuts)),
        scratch_shapes=relay_scratch(4 * count + rows, second, width, value.dtype),
        compiler_params=pltpu.CompilerParams(vmem_limit_bytes=VMEM_LIMIT),
        cost_estimate=LIGHT,
        name="edges",
    )(in_hbm(value), in_hbm(density), after)


def second_tile(ref, index, at, total):
    here = ref[*index, pl.ds(at, SUB), :]
    place = lax.broadcasted_iota(jnp.int32, here.shape, 0)
    if at + SUB < total:
        above = ref[*index, pl.ds(at + 1, SUB), :]
    else:
        above = jnp.where(place == SUB - 1, here, pltpu.roll(here, SUB - 1, 0))
    if at > 0:
        below = ref[*index, pl.ds(at - 1, SUB), :]
    else:
        below = jnp.where(place == 0, here, pltpu.roll(here, 1, 0))
    return here, above, below


def steep_tiles(second, width):
    tiles = []
    for at in range(0, second, SUB):
        index = at + lax.broadcasted_iota(jnp.int32, (SUB, LANES), 0)
        tiles.append(jnp.concatenate([slant(index, second)] * (width // LANES), 1))
    return tiles


def value_kernel(value, low, high, crowding, *rest):
    parts = len(rest) - 9
    halos = rest[:parts]
    value_now, low_now, high_now, pad, halo, fresh, load, edge, store = rest[parts:]
    count, rows, second, width = value.shape
    negative = is_negative()
    first = lax.axis_index("vel") == 0
    last = lax.axis_index("vel") == lax.axis_size("vel") - 1
    base = lax.axis_index("vel") * rows
    total = rows * lax.axis_size("vel")
    order = [jnp.where(negative, t, count - 1 - t) for t in range(count)]
    half = second // 2

    begin = 0
    halo_copies = []
    for k, part in enumerate(halos):
        extent = part.shape[0]
        halo_copies.append(
            pltpu.make_async_copy(part, halo.at[pl.ds(begin, extent)], load.at[count + k])
        )
        begin += extent
    start_all(halo_copies)
    centre_copies = [
        pltpu.make_async_copy(value.at[i], pad.at[i, pl.ds(1, rows)], load.at[t])
        for t, i in enumerate(order)
    ]
    start_all(centre_copies)
    below_own = pltpu.make_async_copy(value.at[:, 0], pad.at[:, 0], edge.at[0])
    below_far = pltpu.make_async_copy(low.at[0], pad.at[:, 0], edge.at[0])
    above_own = pltpu.make_async_copy(value.at[:, rows - 1], pad.at[:, rows + 1], edge.at[1])
    above_far = pltpu.make_async_copy(high.at[0], pad.at[:, rows + 1], edge.at[1])
    pl.when(first)(below_own.start)
    pl.when(jnp.logical_not(first))(below_far.start)
    pl.when(last)(above_own.start)
    pl.when(jnp.logical_not(last))(above_far.start)
    below_far.wait()
    above_far.wait()
    wait_all(halo_copies)

    steep_y = steep_tiles(second, width)
    stores = []
    for t, i in enumerate(order):
        centre_copies[t].wait()

        def step(a, carry, t=t, i=i):
            steep = slant(base + a, total)
            for at in range(0, second, SUB):
                here, up_w, dn_w = second_tile(pad, (i, a + 1), at, second)
                if t == 0:
                    x_near = halo[2 * a + at // half, pl.ds(at % half, SUB), :]
                else:
                    x_near = pad[order[t - 1], a + 1, pl.ds(at, SUB), :]
                y_near = pltpu.roll(here, 1 if at < second // 2 else width - 1, 1)
                up_v = pad[i, a + 2, pl.ds(at, SUB), :] - here
                dn_v = here - pad[i, a, pl.ds(at, SUB), :]
                up_w = up_w - here
                dn_w = here - dn_w
                hamilton = (
                    jnp.square(jnp.maximum(dn_v, 0.0))
                    + jnp.square(jnp.minimum(up_v, 0.0))
                    + jnp.square(jnp.maximum(dn_w, 0.0))
                    + jnp.square(jnp.minimum(up_w, 0.0))
                )
                laplace = up_v - dn_v + up_w - dn_w
                fresh[i, a, pl.ds(at, SUB), :] = (
                    here
                    + steep * (x_near - here)
                    + steep_y[at // SUB] * (y_near - here)
                    - (0.5 * CONTROL_COST) * hamilton
                    + VISCOSITY * laplace
                    + crowding[pl.ds(i, 1), :]
                )
            return carry

        lax.fori_loop(0, rows, step, 0)
        stores.append(pltpu.make_async_copy(fresh.at[i], value_now.at[i], store.at[t]))
        stores[-1].start()
    stores.append(pltpu.make_async_copy(fresh.at[:, rows - 1], low_now, store.at[count]))
    stores.append(pltpu.make_async_copy(fresh.at[:, 0], high_now, store.at[count + 1]))
    start_all(stores[count:])
    wait_all(stores)


def value_step(value, low, high, crowding, halos):
    count, rows, second, width = value.shape
    cells = count * rows * second * width
    edge = jax.ShapeDtypeStruct((count, second, width), value.dtype)
    return pl.pallas_call(
        value_kernel,
        out_shape=[jax.ShapeDtypeStruct(value.shape, value.dtype), edge, edge],
        in_specs=[ANY, ANY, ANY, VMEM] + [ANY] * len(halos),
        out_specs=[ANY] * 3,
        scratch_shapes=[
            pltpu.VMEM((count, rows + 2, second, width), value.dtype),
            pltpu.VMEM((2 * rows, second // 2, width), value.dtype),
            pltpu.VMEM(value.shape, value.dtype),
            pltpu.SemaphoreType.DMA((count + len(halos),)),
            pltpu.SemaphoreType.DMA((2,)),
            pltpu.SemaphoreType.DMA((count + 2,)),
        ],
        compiler_params=pltpu.CompilerParams(vmem_limit_bytes=VMEM_LIMIT),
        cost_estimate=LIGHT,
        name="value_step",
    )(in_hbm(value), low, high, crowding, *halos)


def density_kernel(
    density, control, low, high, low_now, high_now, out, rest, pad, ctl, fresh, load, edge, store
):
    count, rows, second, width = density.shape
    negative = is_negative()
    first = lax.axis_index("vel") == 0
    last = lax.axis_index("vel") == lax.axis_size("vel") - 1
    base = lax.axis_index("vel") * rows
    total = rows * lax.axis_size("vel")
    order = [jnp.where(negative, count - 1 - t, t) for t in range(count)]

    centre_copies = []
    for t, i in enumerate(order):
        pair = [
            pltpu.make_async_copy(density.at[i], pad.at[i, pl.ds(1, rows)], load.at[2 * t]),
            pltpu.make_async_copy(control.at[i], ctl.at[i, pl.ds(1, rows)], load.at[2 * t + 1]),
        ]
        start_all(pair)
        centre_copies.append(pair)
    waits = []
    fields = ((density, low.at[1], high.at[1], pad), (control, low_now, high_now, ctl))
    for k, (field, below, above, padded) in enumerate(fields):
        for outer, own, far, place, sem in (
            (first, field.at[:, 0], below, 0, edge.at[2 * k]),
            (last, field.at[:, rows - 1], above, rows + 1, edge.at[2 * k + 1]),
        ):
            own_copy = pltpu.make_async_copy(own, padded.at[:, place], sem)
            far_copy = pltpu.make_async_copy(far, padded.at[:, place], sem)
            pl.when(outer)(own_copy.start)
            pl.when(jnp.logical_not(outer))(far_copy.start)
            waits.append(far_copy)
    wait_all(waits)

    steep_y = steep_tiles(second, width)
    stores = []
    for t, i in enumerate(order):
        wait_all(centre_copies[t])

        def step(a, carry, t=t, i=i):
            steep = slant(base + a, total)
            for at in range(0, second, SUB):
                here, up_w, dn_w = second_tile(pad, (i, a + 1), at, second)
                ctl_here, ctl_up_w, ctl_dn_w = second_tile(ctl, (i, a + 1), at, second)
                up_v = pad[i, a + 2, pl.ds(at, SUB), :]
                dn_v = pad[i, a, pl.ds(at, SUB), :]
                y_near = pltpu.roll(here, width - 1 if at < second // 2 else 1, 1)
                if t == 0:
                    along_x = -steep * here
                else:
                    along_x = steep * (pad[order[t - 1], a + 1, pl.ds(at, SUB), :] - here)
                up = ctl[i, a + 2, pl.ds(at, SUB), :] - ctl_here
                dn = ctl_here - ctl[i, a, pl.ds(at, SUB), :]
                right = ctl_up_w - ctl_here
                left = ctl_here - ctl_dn_w
                flux_up = jnp.minimum(up, 0.0) * here + jnp.maximum(up, 0.0) * up_v
                flux_dn = jnp.minimum(dn, 0.0) * dn_v + jnp.maximum(dn, 0.0) * here
                flux_right = jnp.minimum(right, 0.0) * here + jnp.maximum(right, 0.0) * up_w
                flux_left = jnp.minimum(left, 0.0) * dn_w + jnp.maximum(left, 0.0) * here
                flux = flux_up - flux_dn + flux_right - flux_left
                spread = up_v + dn_v + up_w + dn_w - 4.0 * here
                fresh[i, a, pl.ds(at, SUB), :] = (
                    here
                    + along_x
                    + steep_y[at // SUB] * (y_near - here)
                    + CONTROL_COST * flux
                    + VISCOSITY * spread
                )
            return carry

        lax.fori_loop(0, rows, step, 0)
        stores.append(pltpu.make_async_copy(fresh.at[i], out.at[i], store.at[t]))
        stores[-1].start()
        if t == 0:
            extent = rest.shape[0]
            rest[...] = fresh[i, pl.ds(rows - extent, extent)]
    wait_all(stores)


def density_step(density, control, low, high, low_now, high_now, extent):
    count, rows, second, width = density.shape
    cells = count * rows * second * width
    padded = pltpu.VMEM((count, rows + 2, second, width), density.dtype)
    return pl.pallas_call(
        density_kernel,
        out_shape=[
            jax.ShapeDtypeStruct(density.shape, density.dtype),
            pltpu.VMEM((extent, second, width), density.dtype),
        ],
        in_specs=[ANY] * 6,
        out_specs=[ANY, VMEM],
        scratch_shapes=[
            padded,
            padded,
            pltpu.VMEM(density.shape, density.dtype),
            pltpu.SemaphoreType.DMA((2 * count,)),
            pltpu.SemaphoreType.DMA((4,)),
            pltpu.SemaphoreType.DMA((count,)),
        ],
        compiler_params=pltpu.CompilerParams(vmem_limit_bytes=VMEM_LIMIT),
        cost_estimate=LIGHT,
        name="density_step",
    )(in_hbm(density), in_hbm(control), low, high, low_now, high_now)


def arrive_kernel(begin, partial, *refs):
    halos, (out, held, near, load, store) = refs[:-5], refs[-5:]
    count, rows = partial.shape[:2]
    row = jnp.where(is_negative(), count - 1, 0)
    base = lax.axis_index("vel") * rows + begin
    total = rows * lax.axis_size("vel")
    loads = []
    for halo in halos:
        for k in range(halo.shape[0]):
            a = len(loads)
            pair = [
                pltpu.make_async_copy(partial.at[row, begin + a], held.at[a], load.at[2 * a]),
                pltpu.make_async_copy(halo.at[k], near.at[a], load.at[2 * a + 1]),
            ]
            start_all(pair)
            loads.append(pair)
    stores = []
    for a, pair in enumerate(loads):
        wait_all(pair)
        held[a] = held[a] + slant(base + a, total) * near[a]
        stores.append(pltpu.make_async_copy(held.at[a], out.at[row, begin + a], store.at[a]))
        stores[-1].start()
    wait_all(stores)


def arrive(partial, halos, begin):
    extent = sum(halo.shape[0] for halo in halos)
    block = pltpu.VMEM((extent,) + partial.shape[2:], partial.dtype)
    return pl.pallas_call(
        functools.partial(arrive_kernel, begin),
        out_shape=jax.ShapeDtypeStruct(partial.shape, partial.dtype),
        in_specs=[ANY] * (1 + len(halos)),
        out_specs=ANY,
        scratch_shapes=[
            block,
            block,
            pltpu.SemaphoreType.DMA((2 * extent,)),
            pltpu.SemaphoreType.DMA((extent,)),
        ],
        input_output_aliases={0: 0},
        compiler_params=pltpu.CompilerParams(vmem_limit_bytes=VMEM_LIMIT),
        cost_estimate=LIGHT,
        name="arrive",
    )(in_hbm(partial), *halos)


def arrive_rest_kernel(begin, partial, rest, halo, out, held, sems):
    count, rows = partial.shape[:2]
    extent = halo.shape[0]
    skipped = begin - (rows - rest.shape[0])
    row = jnp.where(is_negative(), count - 1, 0)
    base = lax.axis_index("vel") * rows + begin
    total = rows * lax.axis_size("vel")
    copies = []
    for a in range(extent):
        held[a] = rest[skipped + a] + slant(base + a, total) * halo[a]
        copies.append(pltpu.make_async_copy(held.at[a], out.at[row, begin + a], sems.at[a]))
        copies[-1].start()
    wait_all(copies)


def arrive_rest(partial, rest, halo, begin):
    return pl.pallas_call(
        functools.partial(arrive_rest_kernel, begin),
        out_shape=jax.ShapeDtypeStruct(partial.shape, partial.dtype),
        in_specs=[ANY, VMEM, VMEM],
        out_specs=ANY,
        scratch_shapes=[
            pltpu.VMEM(halo.shape, halo.dtype),
            pltpu.SemaphoreType.DMA((halo.shape[0],)),
        ],
        input_output_aliases={0: 0},
        compiler_params=pltpu.CompilerParams(vmem_limit_bytes=VMEM_LIMIT),
        cost_estimate=LIGHT,
        name="arrive_rest",
    )(in_hbm(partial), in_vmem(rest), in_vmem(halo))


def routes(mesh):
    names = tuple(mesh.axis_names)
    sizes = [mesh.shape[name] for name in names]
    slabs, groups = mesh.shape["pos"], mesh.shape["vel"]

    def place(pos, vel):
        at = {"pos": pos % slabs, "vel": vel}
        index = 0
        for name, size in zip(names, sizes):
            index = index * size + at[name]
        return index

    value_route, density_route, over_route, swap_route = [], [], [], []
    for pos in range(slabs):
        for vel in range(groups):
            onward = 1 if vel < groups // 2 else -1
            value_route.append((place(pos, vel), place(pos + onward, vel)))
            density_route.append((place(pos, vel), place(pos - onward, vel)))
            leads = slabs % 2 == 0 and (pos % 2 == 0) == (onward > 0)
            over_route.append((place(pos, vel), place(pos - 2 * onward if leads else pos, vel)))
            swap_route.append((place(pos, vel), place(pos + onward if leads else pos - onward, vel)))
    return names, value_route, density_route, over_route, swap_route


def body(mesh, value_next, density):
    names, value_route, density_route, over_route, swap_route = routes(mesh)
    groups = mesh.shape["vel"]
    count, rows, second, width = value_next.shape
    last, filler = max(1, rows // 16), max(1, rows // 8)
    near = rows // 2 - 2 * last
    cuts = (
        (0, near),
        (near, rows - last - filler),
        (rows - last - filler, rows - filler),
        (rows - filler, rows),
    )
    onward = [(v, v + 1) for v in range(groups - 1)]
    back = [(v + 1, v) for v in range(groups - 1)]

    bounds = (0, 2 * EARLY, rows + 2 * EARLY + SHIFT, 2 * rows)
    value_halos = [
        lax.ppermute(value_rows(value_next, begin, end), names, value_route)
        for begin, end in zip(bounds, bounds[1:])
    ]
    low, high, *parts = edges(value_next, density, value_halos[0], cuts)
    fillers = [lax.ppermute(part, names, over_route) for part in parts[1::2]]
    mass = lax.psum(jnp.sum(density, axis=(1, 2)), "vel") / (second * second)
    crowding = CROWDING * mass * mass
    low, high, crowding = lax.optimization_barrier((low, high, crowding))
    low = lax.ppermute(low, "vel", onward)
    high = lax.ppermute(high, "vel", back)

    held = (parts[::2], value_halos, crowding, low, high, fillers)
    parts, value_halos, crowding, low, high, _ = lax.optimization_barrier(held)
    fillers = [lax.ppermute(part, names, swap_route) for part in fillers]
    parts = [lax.ppermute(part, names, density_route) for part in parts]

    value_now, low_now, high_now = value_step(value_next, low, high, crowding, value_halos)
    low_now = lax.ppermute(low_now, "vel", onward)
    high_now = lax.ppermute(high_now, "vel", back)
    density_next, rest = density_step(
        density, value_now, low, high, low_now, high_now, last + filler
    )
    density_next = arrive(density_next, (parts[0],), cuts[0][0])
    density_next = arrive(density_next, (fillers[0],), cuts[1][0])
    density_next = arrive_rest(density_next, rest, fillers[1], cuts[3][0])
    density_next = arrive_rest(density_next, rest, parts[1], cuts[2][0])
    return value_now, density_next


def solution(mesh):
    placed = (P("pos", "vel", None, None), P("pos", "vel", None, None))
    return jax.shard_map(
        functools.partial(body, mesh),
        mesh=mesh,
        in_specs=placed,
        out_specs=placed,
        check_vma=False,
    )
```

```python
import functools

import jax
import jax.numpy as jnp
from jax import lax
from jax.experimental import pallas as pl
from jax.experimental.pallas import tpu as pltpu
from jax.sharding import PartitionSpec as P

COURANT = 0.4
CONTROL_COST = 0.25
VISCOSITY = 0.15
CROWDING = 0.3

SUB = 8
LANES = 128
EARLY = 1
SHIFT = 1
VMEM_LIMIT = 18 * 1024 * 1024
ANY = pl.BlockSpec(memory_space=pl.ANY)
VMEM = pl.BlockSpec(memory_space=pltpu.VMEM)
LIGHT = pl.CostEstimate(flops=0, transcendentals=0, bytes_accessed=0)


def is_negative():
    return lax.axis_index("vel") < lax.axis_size("vel") // 2


def slant(first, total):
    return COURANT * (jnp.abs(first.astype(jnp.float32) + 0.5 - total / 2) / (total / 2))


def start_all(copies):
    for copy in copies:
        copy.start()


def wait_all(copies):
    for copy in copies:
        copy.wait()


def in_hbm(array):
    return pltpu.with_memory_space_constraint(array, pltpu.HBM)


def in_vmem(array):
    return pltpu.with_memory_space_constraint(array, pltpu.VMEM)


def relay(pairs, held, load, store):
    inward = [
        pltpu.make_async_copy(source, held.at[k], load.at[k]) for k, (source, _) in enumerate(pairs)
    ]
    outward = [
        pltpu.make_async_copy(held.at[k], target, store.at[k]) for k, (_, target) in enumerate(pairs)
    ]
    start_all(inward)
    for come, go in zip(inward, outward):
        come.wait()
        go.start()
    wait_all(outward)


def relay_scratch(slots, second, width, dtype):
    sems = pltpu.SemaphoreType.DMA((slots,))
    return [pltpu.VMEM((slots, second, width), dtype), sems, sems]


def leaving_rows(field, row, cuts, sent):
    return [
        (field.at[row, a], target.at[a - begin])
        for (begin, end), target in zip(cuts, sent)
        for a in range(begin, end)
    ]


def value_rows_kernel(begin, value, sent, sems):
    row = jnp.where(is_negative(), value.shape[0] - 1, 0)
    half = sent.shape[1]
    copies = [
        pltpu.make_async_copy(
            value.at[row, (begin + k) // 2, pl.ds((begin + k) % 2 * half, half)],
            sent.at[k],
            sems.at[k],
        )
        for k in range(sent.shape[0])
    ]
    start_all(copies)
    wait_all(copies)


def value_rows(value, begin, end):
    _, _, second, width = value.shape
    return pl.pallas_call(
        functools.partial(value_rows_kernel, begin),
        out_shape=[pltpu.VMEM((end - begin, second // 2, width), value.dtype)],
        in_specs=[ANY],
        out_specs=[VMEM],
        scratch_shapes=[pltpu.SemaphoreType.DMA((end - begin,))],
        compiler_params=pltpu.CompilerParams(vmem_limit_bytes=VMEM_LIMIT),
        cost_estimate=LIGHT,
        name="value_rows",
    )(in_hbm(value))[0]


def edges_kernel(cuts, value, density, after, low, high, *rest):
    del after
    count, rows = value.shape[:2]
    row = jnp.where(is_negative(), 0, count - 1)
    pairs = []
    for k, field in enumerate((value, density)):
        for i in range(count):
            pairs.append((field.at[i, rows - 1], low.at[k, i]))
            pairs.append((field.at[i, 0], high.at[k, i]))
    pairs += leaving_rows(density, row, cuts, rest[: len(cuts)])
    relay(pairs, *rest[len(cuts) :])


def edges(value, density, after, cuts):
    count, rows, second, width = value.shape
    edge = pltpu.HBM((2, count, second, width), value.dtype)
    parts = [pltpu.HBM((e - b, second, width), value.dtype) for b, e in cuts]
    return pl.pallas_call(
        functools.partial(edges_kernel, cuts),
        out_shape=[edge, edge, *parts],
        in_specs=[ANY, ANY, ANY],
        out_specs=[ANY] * (2 + len(cuts)),
        scratch_shapes=relay_scratch(4 * count + rows, second, width, value.dtype),
        compiler_params=pltpu.CompilerParams(vmem_limit_bytes=VMEM_LIMIT),
        cost_estimate=LIGHT,
        name="edges",
    )(in_hbm(value), in_hbm(density), after)


def second_tile(ref, index, at, total):
    here = ref[*index, pl.ds(at, SUB), :]
    place = lax.broadcasted_iota(jnp.int32, here.shape, 0)
    if at + SUB < total:
        above = ref[*index, pl.ds(at + 1, SUB), :]
    else:
        above = jnp.where(place == SUB - 1, here, pltpu.roll(here, SUB - 1, 0))
    if at > 0:
        below = ref[*index, pl.ds(at - 1, SUB), :]
    else:
        below = jnp.where(place == 0, here, pltpu.roll(here, 1, 0))
    return here, above, below


def steep_tiles(second, width):
    tiles = []
    for at in range(0, second, SUB):
        index = at + lax.broadcasted_iota(jnp.int32, (SUB, LANES), 0)
        tiles.append(jnp.concatenate([slant(index, second)] * (width // LANES), 1))
    return tiles


def value_kernel(value, low, high, crowding, *rest):
    parts = len(rest) - 9
    halos = rest[:parts]
    value_now, low_now, high_now, pad, halo, fresh, load, edge, store = rest[parts:]
    count, rows, second, width = value.shape
    negative = is_negative()
    first = lax.axis_index("vel") == 0
    last = lax.axis_index("vel") == lax.axis_size("vel") - 1
    base = lax.axis_index("vel") * rows
    total = rows * lax.axis_size("vel")
    order = [jnp.where(negative, t, count - 1 - t) for t in range(count)]
    half = second // 2

    begin = 0
    halo_copies = []
    for k, part in enumerate(halos):
        extent = part.shape[0]
        halo_copies.append(
            pltpu.make_async_copy(part, halo.at[pl.ds(begin, extent)], load.at[count + k])
        )
        begin += extent
    start_all(halo_copies)
    centre_copies = [
        pltpu.make_async_copy(value.at[i], pad.at[i, pl.ds(1, rows)], load.at[t])
        for t, i in enumerate(order)
    ]
    start_all(centre_copies)
    below_own = pltpu.make_async_copy(value.at[:, 0], pad.at[:, 0], edge.at[0])
    below_far = pltpu.make_async_copy(low.at[0], pad.at[:, 0], edge.at[0])
    above_own = pltpu.make_async_copy(value.at[:, rows - 1], pad.at[:, rows + 1], edge.at[1])
    above_far = pltpu.make_async_copy(high.at[0], pad.at[:, rows + 1], edge.at[1])
    pl.when(first)(below_own.start)
    pl.when(jnp.logical_not(first))(below_far.start)
    pl.when(last)(above_own.start)
    pl.when(jnp.logical_not(last))(above_far.start)
    below_far.wait()
    above_far.wait()
    wait_all(halo_copies)

    steep_y = steep_tiles(second, width)
    stores = []
    for t, i in enumerate(order):
        centre_copies[t].wait()

        def step(a, carry, t=t, i=i):
            steep = slant(base + a, total)
            for at in range(0, second, SUB):
                here, up_w, dn_w = second_tile(pad, (i, a + 1), at, second)
                if t == 0:
                    x_near = halo[2 * a + at // half, pl.ds(at % half, SUB), :]
                else:
                    x_near = pad[order[t - 1], a + 1, pl.ds(at, SUB), :]
                y_near = pltpu.roll(here, 1 if at < second // 2 else width - 1, 1)
                up_v = pad[i, a + 2, pl.ds(at, SUB), :] - here
                dn_v = here - pad[i, a, pl.ds(at, SUB), :]
                up_w = up_w - here
                dn_w = here - dn_w
                hamilton = (
                    jnp.square(jnp.maximum(dn_v, 0.0))
                    + jnp.square(jnp.minimum(up_v, 0.0))
                    + jnp.square(jnp.maximum(dn_w, 0.0))
                    + jnp.square(jnp.minimum(up_w, 0.0))
                )
                laplace = up_v - dn_v + up_w - dn_w
                fresh[i, a, pl.ds(at, SUB), :] = (
                    here
                    + steep * (x_near - here)
                    + steep_y[at // SUB] * (y_near - here)
                    - (0.5 * CONTROL_COST) * hamilton
                    + VISCOSITY * laplace
                    + crowding[pl.ds(i, 1), :]
                )
            return carry

        lax.fori_loop(0, rows, step, 0)
        stores.append(pltpu.make_async_copy(fresh.at[i], value_now.at[i], store.at[t]))
        stores[-1].start()
    stores.append(pltpu.make_async_copy(fresh.at[:, rows - 1], low_now, store.at[count]))
    stores.append(pltpu.make_async_copy(fresh.at[:, 0], high_now, store.at[count + 1]))
    start_all(stores[count:])
    wait_all(stores)


def value_step(value, low, high, crowding, halos):
    count, rows, second, width = value.shape
    cells = count * rows * second * width
    edge = jax.ShapeDtypeStruct((count, second, width), value.dtype)
    return pl.pallas_call(
        value_kernel,
        out_shape=[jax.ShapeDtypeStruct(value.shape, value.dtype), edge, edge],
        in_specs=[ANY, ANY, ANY, VMEM] + [ANY] * len(halos),
        out_specs=[ANY] * 3,
        scratch_shapes=[
            pltpu.VMEM((count, rows + 2, second, width), value.dtype),
            pltpu.VMEM((2 * rows, second // 2, width), value.dtype),
            pltpu.VMEM(value.shape, value.dtype),
            pltpu.SemaphoreType.DMA((count + len(halos),)),
            pltpu.SemaphoreType.DMA((2,)),
            pltpu.SemaphoreType.DMA((count + 2,)),
        ],
        compiler_params=pltpu.CompilerParams(vmem_limit_bytes=VMEM_LIMIT),
        cost_estimate=LIGHT,
        name="value_step",
    )(in_hbm(value), low, high, crowding, *halos)


def density_kernel(
    density, control, low, high, low_now, high_now, out, rest, pad, ctl, fresh, load, edge, store
):
    count, rows, second, width = density.shape
    negative = is_negative()
    first = lax.axis_index("vel") == 0
    last = lax.axis_index("vel") == lax.axis_size("vel") - 1
    base = lax.axis_index("vel") * rows
    total = rows * lax.axis_size("vel")
    order = [jnp.where(negative, count - 1 - t, t) for t in range(count)]

    centre_copies = []
    for t, i in enumerate(order):
        pair = [
            pltpu.make_async_copy(density.at[i], pad.at[i, pl.ds(1, rows)], load.at[2 * t]),
            pltpu.make_async_copy(control.at[i], ctl.at[i, pl.ds(1, rows)], load.at[2 * t + 1]),
        ]
        start_all(pair)
        centre_copies.append(pair)
    waits = []
    fields = ((density, low.at[1], high.at[1], pad), (control, low_now, high_now, ctl))
    for k, (field, below, above, padded) in enumerate(fields):
        for outer, own, far, place, sem in (
            (first, field.at[:, 0], below, 0, edge.at[2 * k]),
            (last, field.at[:, rows - 1], above, rows + 1, edge.at[2 * k + 1]),
        ):
            own_copy = pltpu.make_async_copy(own, padded.at[:, place], sem)
            far_copy = pltpu.make_async_copy(far, padded.at[:, place], sem)
            pl.when(outer)(own_copy.start)
            pl.when(jnp.logical_not(outer))(far_copy.start)
            waits.append(far_copy)
    wait_all(waits)

    steep_y = steep_tiles(second, width)
    stores = []
    for t, i in enumerate(order):
        wait_all(centre_copies[t])

        def step(a, carry, t=t, i=i):
            steep = slant(base + a, total)
            for at in range(0, second, SUB):
                here, up_w, dn_w = second_tile(pad, (i, a + 1), at, second)
                ctl_here, ctl_up_w, ctl_dn_w = second_tile(ctl, (i, a + 1), at, second)
                up_v = pad[i, a + 2, pl.ds(at, SUB), :]
                dn_v = pad[i, a, pl.ds(at, SUB), :]
                y_near = pltpu.roll(here, width - 1 if at < second // 2 else 1, 1)
                if t == 0:
                    along_x = -steep * here
                else:
                    along_x = steep * (pad[order[t - 1], a + 1, pl.ds(at, SUB), :] - here)
                up = ctl[i, a + 2, pl.ds(at, SUB), :] - ctl_here
                dn = ctl_here - ctl[i, a, pl.ds(at, SUB), :]
                right = ctl_up_w - ctl_here
                left = ctl_here - ctl_dn_w
                flux_up = jnp.minimum(up, 0.0) * here + jnp.maximum(up, 0.0) * up_v
                flux_dn = jnp.minimum(dn, 0.0) * dn_v + jnp.maximum(dn, 0.0) * here
                flux_right = jnp.minimum(right, 0.0) * here + jnp.maximum(right, 0.0) * up_w
                flux_left = jnp.minimum(left, 0.0) * dn_w + jnp.maximum(left, 0.0) * here
                flux = flux_up - flux_dn + flux_right - flux_left
                spread = up_v + dn_v + up_w + dn_w - 4.0 * here
                fresh[i, a, pl.ds(at, SUB), :] = (
                    here
                    + along_x
                    + steep_y[at // SUB] * (y_near - here)
                    + CONTROL_COST * flux
                    + VISCOSITY * spread
                )
            return carry

        lax.fori_loop(0, rows, step, 0)
        stores.append(pltpu.make_async_copy(fresh.at[i], out.at[i], store.at[t]))
        stores[-1].start()
        if t == 0:
            extent = rest.shape[0]
            rest[...] = fresh[i, pl.ds(rows - extent, extent)]
    wait_all(stores)


def density_step(density, control, low, high, low_now, high_now, extent):
    count, rows, second, width = density.shape
    cells = count * rows * second * width
    padded = pltpu.VMEM((count, rows + 2, second, width), density.dtype)
    return pl.pallas_call(
        density_kernel,
        out_shape=[
            jax.ShapeDtypeStruct(density.shape, density.dtype),
            pltpu.VMEM((extent, second, width), density.dtype),
        ],
        in_specs=[ANY] * 6,
        out_specs=[ANY, VMEM],
        scratch_shapes=[
            padded,
            padded,
            pltpu.VMEM(density.shape, density.dtype),
            pltpu.SemaphoreType.DMA((2 * count,)),
            pltpu.SemaphoreType.DMA((4,)),
            pltpu.SemaphoreType.DMA((count,)),
        ],
        compiler_params=pltpu.CompilerParams(vmem_limit_bytes=VMEM_LIMIT),
        cost_estimate=LIGHT,
        name="density_step",
    )(in_hbm(density), in_hbm(control), low, high, low_now, high_now)


def arrive_kernel(partial, *refs):
    halos, (out, held, near, load, store) = refs[:-5], refs[-5:]
    count, rows = partial.shape[:2]
    row = jnp.where(is_negative(), count - 1, 0)
    base = lax.axis_index("vel") * rows
    total = rows * lax.axis_size("vel")
    loads = []
    for halo in halos:
        for k in range(halo.shape[0]):
            a = len(loads)
            pair = [
                pltpu.make_async_copy(partial.at[row, a], held.at[a], load.at[2 * a]),
                pltpu.make_async_copy(halo.at[k], near.at[a], load.at[2 * a + 1]),
            ]
            start_all(pair)
            loads.append(pair)
    stores = []
    for a, pair in enumerate(loads):
        wait_all(pair)
        held[a] = held[a] + slant(base + a, total) * near[a]
        stores.append(pltpu.make_async_copy(held.at[a], out.at[row, a], store.at[a]))
        stores[-1].start()
    wait_all(stores)


def arrive(partial, halos):
    extent = sum(halo.shape[0] for halo in halos)
    block = pltpu.VMEM((extent,) + partial.shape[2:], partial.dtype)
    return pl.pallas_call(
        arrive_kernel,
        out_shape=jax.ShapeDtypeStruct(partial.shape, partial.dtype),
        in_specs=[ANY] * (1 + len(halos)),
        out_specs=ANY,
        scratch_shapes=[
            block,
            block,
            pltpu.SemaphoreType.DMA((2 * extent,)),
            pltpu.SemaphoreType.DMA((extent,)),
        ],
        input_output_aliases={0: 0},
        compiler_params=pltpu.CompilerParams(vmem_limit_bytes=VMEM_LIMIT),
        cost_estimate=LIGHT,
        name="arrive",
    )(in_hbm(partial), *halos)


def arrive_rest_kernel(begin, partial, rest, halo, out, held, sems):
    count, rows = partial.shape[:2]
    extent = halo.shape[0]
    skipped = begin - (rows - rest.shape[0])
    step = halo.shape[1] // 2
    row = jnp.where(is_negative(), count - 1, 0)
    base = lax.axis_index("vel") * rows + begin
    total = rows * lax.axis_size("vel")
    copies = []
    for a in range(extent):
        for u in range(2):
            part = pl.ds(u * step, step)
            held[a, part] = rest[skipped + a, part] + slant(base + a, total) * halo[a, part]
            target = out.at[row, begin + a, part]
            copies.append(pltpu.make_async_copy(held.at[a, part], target, sems.at[2 * a + u]))
            copies[-1].start()
    wait_all(copies)


def arrive_rest(partial, rest, halo, begin):
    return pl.pallas_call(
        functools.partial(arrive_rest_kernel, begin),
        out_shape=jax.ShapeDtypeStruct(partial.shape, partial.dtype),
        in_specs=[ANY, VMEM, VMEM],
        out_specs=ANY,
        scratch_shapes=[
            pltpu.VMEM(halo.shape, halo.dtype),
            pltpu.SemaphoreType.DMA((2 * halo.shape[0],)),
        ],
        input_output_aliases={0: 0},
        compiler_params=pltpu.CompilerParams(vmem_limit_bytes=VMEM_LIMIT),
        cost_estimate=LIGHT,
        name="arrive_rest",
    )(in_hbm(partial), in_vmem(rest), in_vmem(halo))


def routes(mesh):
    names = tuple(mesh.axis_names)
    sizes = [mesh.shape[name] for name in names]
    slabs, groups = mesh.shape["pos"], mesh.shape["vel"]

    def place(pos, vel):
        at = {"pos": pos % slabs, "vel": vel}
        index = 0
        for name, size in zip(names, sizes):
            index = index * size + at[name]
        return index

    value_route, density_route, over_route, swap_route = [], [], [], []
    for pos in range(slabs):
        for vel in range(groups):
            onward = 1 if vel < groups // 2 else -1
            value_route.append((place(pos, vel), place(pos + onward, vel)))
            density_route.append((place(pos, vel), place(pos - onward, vel)))
            leads = slabs % 2 == 0 and (pos % 2 == 0) == (onward > 0)
            over_route.append((place(pos, vel), place(pos - 2 * onward if leads else pos, vel)))
            swap_route.append((place(pos, vel), place(pos + onward if leads else pos - onward, vel)))
    return names, value_route, density_route, over_route, swap_route


def body(mesh, value_next, density):
    names, value_route, density_route, over_route, swap_route = routes(mesh)
    groups = mesh.shape["vel"]
    count, rows, second, width = value_next.shape
    last, filler = max(1, rows // 16), max(1, rows // 8)
    near = rows // 2 - 2 * last
    cuts = (
        (0, near),
        (near, rows - last - filler),
        (rows - last - filler, rows - filler),
        (rows - filler, rows),
    )
    onward = [(v, v + 1) for v in range(groups - 1)]
    back = [(v + 1, v) for v in range(groups - 1)]

    bounds = (0, 2 * EARLY, rows + 2 * EARLY + SHIFT, 2 * rows)
    value_halos = [
        lax.ppermute(value_rows(value_next, begin, end), names, value_route)
        for begin, end in zip(bounds, bounds[1:])
    ]
    low, high, *parts = edges(value_next, density, value_halos[0], cuts)
    fillers = [lax.ppermute(part, names, over_route) for part in parts[1::2]]
    mass = lax.psum(jnp.sum(density, axis=(1, 2)), "vel") / (second * second)
    crowding = CROWDING * mass * mass
    low, high, crowding = lax.optimization_barrier((low, high, crowding))
    low = lax.ppermute(low, "vel", onward)
    high = lax.ppermute(high, "vel", back)

    held = (parts[::2], value_halos, crowding, low, high, fillers)
    parts, value_halos, crowding, low, high, _ = lax.optimization_barrier(held)
    fillers = [lax.ppermute(part, names, swap_route) for part in fillers]
    parts = [lax.ppermute(part, names, density_route) for part in parts]

    value_now, low_now, high_now = value_step(value_next, low, high, crowding, value_halos)
    low_now = lax.ppermute(low_now, "vel", onward)
    high_now = lax.ppermute(high_now, "vel", back)
    density_next, rest = density_step(
        density, value_now, low, high, low_now, high_now, last + filler
    )
    density_next = arrive(density_next, (parts[0], fillers[0]))
    density_next = arrive_rest(density_next, rest, fillers[1], cuts[3][0])
    density_next = arrive_rest(density_next, rest, parts[1], cuts[2][0])
    return value_now, density_next


def solution(mesh):
    placed = (P("pos", "vel", None, None), P("pos", "vel", None, None))
    return jax.shard_map(
        functools.partial(body, mesh),
        mesh=mesh,
        in_specs=placed,
        out_specs=placed,
        check_vma=False,
    )
```

```python
import functools

import jax
import jax.numpy as jnp
from jax import lax
from jax.experimental import pallas as pl
from jax.experimental.pallas import tpu as pltpu
from jax.sharding import PartitionSpec as P

COURANT = 0.4
CONTROL_COST = 0.25
VISCOSITY = 0.15
CROWDING = 0.3

SUB = 8
LANES = 128
EARLY = 1
SHIFT = 2
VMEM_LIMIT = 18 * 1024 * 1024
ANY = pl.BlockSpec(memory_space=pl.ANY)
VMEM = pl.BlockSpec(memory_space=pltpu.VMEM)
LIGHT = pl.CostEstimate(flops=0, transcendentals=0, bytes_accessed=0)


def is_negative():
    return lax.axis_index("vel") < lax.axis_size("vel") // 2


def slant(first, total):
    return COURANT * (jnp.abs(first.astype(jnp.float32) + 0.5 - total / 2) / (total / 2))


def start_all(copies):
    for copy in copies:
        copy.start()


def wait_all(copies):
    for copy in copies:
        copy.wait()


def in_hbm(array):
    return pltpu.with_memory_space_constraint(array, pltpu.HBM)


def in_vmem(array):
    return pltpu.with_memory_space_constraint(array, pltpu.VMEM)


def relay(pairs, held, load, store):
    inward = [
        pltpu.make_async_copy(source, held.at[k], load.at[k]) for k, (source, _) in enumerate(pairs)
    ]
    outward = [
        pltpu.make_async_copy(held.at[k], target, store.at[k]) for k, (_, target) in enumerate(pairs)
    ]
    start_all(inward)
    for come, go in zip(inward, outward):
        come.wait()
        go.start()
    wait_all(outward)


def relay_scratch(slots, second, width, dtype):
    sems = pltpu.SemaphoreType.DMA((slots,))
    return [pltpu.VMEM((slots, second, width), dtype), sems, sems]


def leaving_rows(field, row, cuts, sent):
    return [
        (field.at[row, a], target.at[a - begin])
        for (begin, end), target in zip(cuts, sent)
        for a in range(begin, end)
    ]


def value_rows_kernel(begin, value, sent, sems):
    row = jnp.where(is_negative(), value.shape[0] - 1, 0)
    half = sent.shape[1]
    copies = [
        pltpu.make_async_copy(
            value.at[row, (begin + k) // 2, pl.ds((begin + k) % 2 * half, half)],
            sent.at[k],
            sems.at[k],
        )
        for k in range(sent.shape[0])
    ]
    start_all(copies)
    wait_all(copies)


def value_rows(value, begin, end):
    _, _, second, width = value.shape
    return pl.pallas_call(
        functools.partial(value_rows_kernel, begin),
        out_shape=[pltpu.VMEM((end - begin, second // 2, width), value.dtype)],
        in_specs=[ANY],
        out_specs=[VMEM],
        scratch_shapes=[pltpu.SemaphoreType.DMA((end - begin,))],
        compiler_params=pltpu.CompilerParams(vmem_limit_bytes=VMEM_LIMIT),
        cost_estimate=LIGHT,
        name="value_rows",
    )(in_hbm(value))[0]


def edges_kernel(cuts, value, density, after, low, high, *rest):
    del after
    count, rows = value.shape[:2]
    row = jnp.where(is_negative(), 0, count - 1)
    pairs = []
    for k, field in enumerate((value, density)):
        for i in range(count):
            pairs.append((field.at[i, rows - 1], low.at[k, i]))
            pairs.append((field.at[i, 0], high.at[k, i]))
    pairs += leaving_rows(density, row, cuts, rest[: len(cuts)])
    relay(pairs, *rest[len(cuts) :])


def edges(value, density, after, cuts):
    count, rows, second, width = value.shape
    edge = pltpu.HBM((2, count, second, width), value.dtype)
    parts = [pltpu.HBM((e - b, second, width), value.dtype) for b, e in cuts]
    return pl.pallas_call(
        functools.partial(edges_kernel, cuts),
        out_shape=[edge, edge, *parts],
        in_specs=[ANY, ANY, ANY],
        out_specs=[ANY] * (2 + len(cuts)),
        scratch_shapes=relay_scratch(4 * count + rows, second, width, value.dtype),
        compiler_params=pltpu.CompilerParams(vmem_limit_bytes=VMEM_LIMIT),
        cost_estimate=LIGHT,
        name="edges",
    )(in_hbm(value), in_hbm(density), after)


def second_tile(ref, index, at, total):
    here = ref[*index, pl.ds(at, SUB), :]
    place = lax.broadcasted_iota(jnp.int32, here.shape, 0)
    if at + SUB < total:
        above = ref[*index, pl.ds(at + 1, SUB), :]
    else:
        above = jnp.where(place == SUB - 1, here, pltpu.roll(here, SUB - 1, 0))
    if at > 0:
        below = ref[*index, pl.ds(at - 1, SUB), :]
    else:
        below = jnp.where(place == 0, here, pltpu.roll(here, 1, 0))
    return here, above, below


def steep_tiles(second, width):
    tiles = []
    for at in range(0, second, SUB):
        index = at + lax.broadcasted_iota(jnp.int32, (SUB, LANES), 0)
        tiles.append(jnp.concatenate([slant(index, second)] * (width // LANES), 1))
    return tiles


def value_kernel(value, low, high, crowding, *rest):
    parts = len(rest) - 9
    halos = rest[:parts]
    value_now, low_now, high_now, pad, halo, fresh, load, edge, store = rest[parts:]
    count, rows, second, width = value.shape
    negative = is_negative()
    first = lax.axis_index("vel") == 0
    last = lax.axis_index("vel") == lax.axis_size("vel") - 1
    base = lax.axis_index("vel") * rows
    total = rows * lax.axis_size("vel")
    order = [jnp.where(negative, t, count - 1 - t) for t in range(count)]
    half = second // 2

    begin = 0
    halo_copies = []
    for k, part in enumerate(halos):
        extent = part.shape[0]
        halo_copies.append(
            pltpu.make_async_copy(part, halo.at[pl.ds(begin, extent)], load.at[count + k])
        )
        begin += extent
    start_all(halo_copies)
    centre_copies = [
        pltpu.make_async_copy(value.at[i], pad.at[i, pl.ds(1, rows)], load.at[t])
        for t, i in enumerate(order)
    ]
    start_all(centre_copies)
    below_own = pltpu.make_async_copy(value.at[:, 0], pad.at[:, 0], edge.at[0])
    below_far = pltpu.make_async_copy(low.at[0], pad.at[:, 0], edge.at[0])
    above_own = pltpu.make_async_copy(value.at[:, rows - 1], pad.at[:, rows + 1], edge.at[1])
    above_far = pltpu.make_async_copy(high.at[0], pad.at[:, rows + 1], edge.at[1])
    pl.when(first)(below_own.start)
    pl.when(jnp.logical_not(first))(below_far.start)
    pl.when(last)(above_own.start)
    pl.when(jnp.logical_not(last))(above_far.start)
    below_far.wait()
    above_far.wait()
    wait_all(halo_copies)

    steep_y = steep_tiles(second, width)
    stores = []
    for t, i in enumerate(order):
        centre_copies[t].wait()

        def step(a, carry, t=t, i=i):
            steep = slant(base + a, total)
            for at in range(0, second, SUB):
                here, up_w, dn_w = second_tile(pad, (i, a + 1), at, second)
                if t == 0:
                    x_near = halo[2 * a + at // half, pl.ds(at % half, SUB), :]
                else:
                    x_near = pad[order[t - 1], a + 1, pl.ds(at, SUB), :]
                y_near = pltpu.roll(here, 1 if at < second // 2 else width - 1, 1)
                up_v = pad[i, a + 2, pl.ds(at, SUB), :] - here
                dn_v = here - pad[i, a, pl.ds(at, SUB), :]
                up_w = up_w - here
                dn_w = here - dn_w
                hamilton = (
                    jnp.square(jnp.maximum(dn_v, 0.0))
                    + jnp.square(jnp.minimum(up_v, 0.0))
                    + jnp.square(jnp.maximum(dn_w, 0.0))
                    + jnp.square(jnp.minimum(up_w, 0.0))
                )
                laplace = up_v - dn_v + up_w - dn_w
                fresh[i, a, pl.ds(at, SUB), :] = (
                    here
                    + steep * (x_near - here)
                    + steep_y[at // SUB] * (y_near - here)
                    - (0.5 * CONTROL_COST) * hamilton
                    + VISCOSITY * laplace
                    + crowding[pl.ds(i, 1), :]
                )
            return carry

        lax.fori_loop(0, rows, step, 0)
        stores.append(pltpu.make_async_copy(fresh.at[i], value_now.at[i], store.at[t]))
        stores[-1].start()
    stores.append(pltpu.make_async_copy(fresh.at[:, rows - 1], low_now, store.at[count]))
    stores.append(pltpu.make_async_copy(fresh.at[:, 0], high_now, store.at[count + 1]))
    start_all(stores[count:])
    wait_all(stores)


def value_step(value, low, high, crowding, halos):
    count, rows, second, width = value.shape
    cells = count * rows * second * width
    edge = jax.ShapeDtypeStruct((count, second, width), value.dtype)
    return pl.pallas_call(
        value_kernel,
        out_shape=[jax.ShapeDtypeStruct(value.shape, value.dtype), edge, edge],
        in_specs=[ANY, ANY, ANY, VMEM] + [ANY] * len(halos),
        out_specs=[ANY] * 3,
        scratch_shapes=[
            pltpu.VMEM((count, rows + 2, second, width), value.dtype),
            pltpu.VMEM((2 * rows, second // 2, width), value.dtype),
            pltpu.VMEM(value.shape, value.dtype),
            pltpu.SemaphoreType.DMA((count + len(halos),)),
            pltpu.SemaphoreType.DMA((2,)),
            pltpu.SemaphoreType.DMA((count + 2,)),
        ],
        compiler_params=pltpu.CompilerParams(vmem_limit_bytes=VMEM_LIMIT),
        cost_estimate=LIGHT,
        name="value_step",
    )(in_hbm(value), low, high, crowding, *halos)


def density_kernel(
    density, control, low, high, low_now, high_now, out, rest, pad, ctl, fresh, load, edge, store
):
    count, rows, second, width = density.shape
    negative = is_negative()
    first = lax.axis_index("vel") == 0
    last = lax.axis_index("vel") == lax.axis_size("vel") - 1
    base = lax.axis_index("vel") * rows
    total = rows * lax.axis_size("vel")
    order = [jnp.where(negative, count - 1 - t, t) for t in range(count)]

    centre_copies = []
    for t, i in enumerate(order):
        pair = [
            pltpu.make_async_copy(density.at[i], pad.at[i, pl.ds(1, rows)], load.at[2 * t]),
            pltpu.make_async_copy(control.at[i], ctl.at[i, pl.ds(1, rows)], load.at[2 * t + 1]),
        ]
        start_all(pair)
        centre_copies.append(pair)
    waits = []
    fields = ((density, low.at[1], high.at[1], pad), (control, low_now, high_now, ctl))
    for k, (field, below, above, padded) in enumerate(fields):
        for outer, own, far, place, sem in (
            (first, field.at[:, 0], below, 0, edge.at[2 * k]),
            (last, field.at[:, rows - 1], above, rows + 1, edge.at[2 * k + 1]),
        ):
            own_copy = pltpu.make_async_copy(own, padded.at[:, place], sem)
            far_copy = pltpu.make_async_copy(far, padded.at[:, place], sem)
            pl.when(outer)(own_copy.start)
            pl.when(jnp.logical_not(outer))(far_copy.start)
            waits.append(far_copy)
    wait_all(waits)

    steep_y = steep_tiles(second, width)
    stores = []
    for t, i in enumerate(order):
        wait_all(centre_copies[t])

        def step(a, carry, t=t, i=i):
            steep = slant(base + a, total)
            for at in range(0, second, SUB):
                here, up_w, dn_w = second_tile(pad, (i, a + 1), at, second)
                ctl_here, ctl_up_w, ctl_dn_w = second_tile(ctl, (i, a + 1), at, second)
                up_v = pad[i, a + 2, pl.ds(at, SUB), :]
                dn_v = pad[i, a, pl.ds(at, SUB), :]
                y_near = pltpu.roll(here, width - 1 if at < second // 2 else 1, 1)
                if t == 0:
                    along_x = -steep * here
                else:
                    along_x = steep * (pad[order[t - 1], a + 1, pl.ds(at, SUB), :] - here)
                up = ctl[i, a + 2, pl.ds(at, SUB), :] - ctl_here
                dn = ctl_here - ctl[i, a, pl.ds(at, SUB), :]
                right = ctl_up_w - ctl_here
                left = ctl_here - ctl_dn_w
                flux_up = jnp.minimum(up, 0.0) * here + jnp.maximum(up, 0.0) * up_v
                flux_dn = jnp.minimum(dn, 0.0) * dn_v + jnp.maximum(dn, 0.0) * here
                flux_right = jnp.minimum(right, 0.0) * here + jnp.maximum(right, 0.0) * up_w
                flux_left = jnp.minimum(left, 0.0) * dn_w + jnp.maximum(left, 0.0) * here
                flux = flux_up - flux_dn + flux_right - flux_left
                spread = up_v + dn_v + up_w + dn_w - 4.0 * here
                fresh[i, a, pl.ds(at, SUB), :] = (
                    here
                    + along_x
                    + steep_y[at // SUB] * (y_near - here)
                    + CONTROL_COST * flux
                    + VISCOSITY * spread
                )
            return carry

        lax.fori_loop(0, rows, step, 0)
        stores.append(pltpu.make_async_copy(fresh.at[i], out.at[i], store.at[t]))
        stores[-1].start()
        if t == 0:
            extent = rest.shape[0]
            rest[...] = fresh[i, pl.ds(rows - extent, extent)]
    wait_all(stores)


def density_step(density, control, low, high, low_now, high_now, extent):
    count, rows, second, width = density.shape
    cells = count * rows * second * width
    padded = pltpu.VMEM((count, rows + 2, second, width), density.dtype)
    return pl.pallas_call(
        density_kernel,
        out_shape=[
            jax.ShapeDtypeStruct(density.shape, density.dtype),
            pltpu.VMEM((extent, second, width), density.dtype),
        ],
        in_specs=[ANY] * 6,
        out_specs=[ANY, VMEM],
        scratch_shapes=[
            padded,
            padded,
            pltpu.VMEM(density.shape, density.dtype),
            pltpu.SemaphoreType.DMA((2 * count,)),
            pltpu.SemaphoreType.DMA((4,)),
            pltpu.SemaphoreType.DMA((count,)),
        ],
        compiler_params=pltpu.CompilerParams(vmem_limit_bytes=VMEM_LIMIT),
        cost_estimate=LIGHT,
        name="density_step",
    )(in_hbm(density), in_hbm(control), low, high, low_now, high_now)


def arrive_kernel(partial, *refs):
    halos, (out, held, near, load, store) = refs[:-5], refs[-5:]
    count, rows = partial.shape[:2]
    row = jnp.where(is_negative(), count - 1, 0)
    base = lax.axis_index("vel") * rows
    total = rows * lax.axis_size("vel")
    loads = []
    for halo in halos:
        for k in range(halo.shape[0]):
            a = len(loads)
            pair = [
                pltpu.make_async_copy(partial.at[row, a], held.at[a], load.at[2 * a]),
                pltpu.make_async_copy(halo.at[k], near.at[a], load.at[2 * a + 1]),
            ]
            start_all(pair)
            loads.append(pair)
    stores = []
    for a, pair in enumerate(loads):
        wait_all(pair)
        held[a] = held[a] + slant(base + a, total) * near[a]
        stores.append(pltpu.make_async_copy(held.at[a], out.at[row, a], store.at[a]))
        stores[-1].start()
    wait_all(stores)


def arrive(partial, halos):
    extent = sum(halo.shape[0] for halo in halos)
    block = pltpu.VMEM((extent,) + partial.shape[2:], partial.dtype)
    return pl.pallas_call(
        arrive_kernel,
        out_shape=jax.ShapeDtypeStruct(partial.shape, partial.dtype),
        in_specs=[ANY] * (1 + len(halos)),
        out_specs=ANY,
        scratch_shapes=[
            block,
            block,
            pltpu.SemaphoreType.DMA((2 * extent,)),
            pltpu.SemaphoreType.DMA((extent,)),
        ],
        input_output_aliases={0: 0},
        compiler_params=pltpu.CompilerParams(vmem_limit_bytes=VMEM_LIMIT),
        cost_estimate=LIGHT,
        name="arrive",
    )(in_hbm(partial), *halos)


def arrive_rest_kernel(begin, partial, rest, halo, out, held, sems):
    count, rows = partial.shape[:2]
    extent = halo.shape[0]
    skipped = begin - (rows - rest.shape[0])
    row = jnp.where(is_negative(), count - 1, 0)
    base = lax.axis_index("vel") * rows + begin
    total = rows * lax.axis_size("vel")
    copies = []
    for a in range(extent):
        held[a] = rest[skipped + a] + slant(base + a, total) * halo[a]
        copies.append(pltpu.make_async_copy(held.at[a], out.at[row, begin + a], sems.at[a]))
        copies[-1].start()
    wait_all(copies)


def arrive_rest(partial, rest, halo, begin):
    return pl.pallas_call(
        functools.partial(arrive_rest_kernel, begin),
        out_shape=jax.ShapeDtypeStruct(partial.shape, partial.dtype),
        in_specs=[ANY, VMEM, VMEM],
        out_specs=ANY,
        scratch_shapes=[
            pltpu.VMEM(halo.shape, halo.dtype),
            pltpu.SemaphoreType.DMA((halo.shape[0],)),
        ],
        input_output_aliases={0: 0},
        compiler_params=pltpu.CompilerParams(vmem_limit_bytes=VMEM_LIMIT),
        cost_estimate=LIGHT,
        name="arrive_rest",
    )(in_hbm(partial), in_vmem(rest), in_vmem(halo))


def routes(mesh):
    names = tuple(mesh.axis_names)
    sizes = [mesh.shape[name] for name in names]
    slabs, groups = mesh.shape["pos"], mesh.shape["vel"]

    def place(pos, vel):
        at = {"pos": pos % slabs, "vel": vel}
        index = 0
        for name, size in zip(names, sizes):
            index = index * size + at[name]
        return index

    value_route, density_route, over_route, swap_route = [], [], [], []
    for pos in range(slabs):
        for vel in range(groups):
            onward = 1 if vel < groups // 2 else -1
            value_route.append((place(pos, vel), place(pos + onward, vel)))
            density_route.append((place(pos, vel), place(pos - onward, vel)))
            leads = slabs % 2 == 0 and (pos % 2 == 0) == (onward > 0)
            over_route.append((place(pos, vel), place(pos - 2 * onward if leads else pos, vel)))
            swap_route.append((place(pos, vel), place(pos + onward if leads else pos - onward, vel)))
    return names, value_route, density_route, over_route, swap_route


def body(mesh, value_next, density):
    names, value_route, density_route, over_route, swap_route = routes(mesh)
    groups = mesh.shape["vel"]
    count, rows, second, width = value_next.shape
    last, filler = max(1, rows // 16), max(1, rows // 8)
    near = rows // 2 - 2 * last
    cuts = (
        (0, near),
        (near, rows - last - filler),
        (rows - last - filler, rows - filler),
        (rows - filler, rows),
    )
    onward = [(v, v + 1) for v in range(groups - 1)]
    back = [(v + 1, v) for v in range(groups - 1)]

    bounds = (0, 2 * EARLY, rows + 2 * EARLY + SHIFT, 2 * rows)
    value_halos = [
        lax.ppermute(value_rows(value_next, begin, end), names, value_route)
        for begin, end in zip(bounds, bounds[1:])
    ]
    low, high, *parts = edges(value_next, density, value_halos[0], cuts)
    fillers = [lax.ppermute(part, names, over_route) for part in parts[1::2]]
    mass = lax.psum(jnp.sum(density, axis=(1, 2)), "vel") / (second * second)
    crowding = CROWDING * mass * mass
    low, high, crowding = lax.optimization_barrier((low, high, crowding))
    low = lax.ppermute(low, "vel", onward)
    high = lax.ppermute(high, "vel", back)

    held = (parts[::2], value_halos, crowding, low, high, fillers)
    parts, value_halos, crowding, low, high, _ = lax.optimization_barrier(held)
    fillers = [lax.ppermute(part, names, swap_route) for part in fillers]
    parts = [lax.ppermute(part, names, density_route) for part in parts]

    value_now, low_now, high_now = value_step(value_next, low, high, crowding, value_halos)
    low_now = lax.ppermute(low_now, "vel", onward)
    high_now = lax.ppermute(high_now, "vel", back)
    density_next, rest = density_step(
        density, value_now, low, high, low_now, high_now, last + filler
    )
    density_next = arrive(density_next, (parts[0], fillers[0]))
    density_next = arrive_rest(density_next, rest, fillers[1], cuts[3][0])
    density_next = arrive_rest(density_next, rest, parts[1], cuts[2][0])
    return value_now, density_next


def solution(mesh):
    placed = (P("pos", "vel", None, None), P("pos", "vel", None, None))
    return jax.shard_map(
        functools.partial(body, mesh),
        mesh=mesh,
        in_specs=placed,
        out_specs=placed,
        check_vma=False,
    )
```
